32 devices in a mesh: groups: 2 (over y), gx: 4 (over z), ta: 4 (over x, core).
Axes of the slice: x: 2, y: 2, z: 4, core: 2. Of those that a mesh axis runs over, the one named last changes fastest.
Arguments:
- queries: bfloat16 [512, 6144], P(('groups', 'gx'), 'ta'), parts along dimension 0, may hold values from -320 to 320
- new_kv: bfloat16 [2, 512, 1024], P(None, ('groups', 'gx'), 'ta'), parts along dimension 1, may hold values from -6 to 6
- kv_cache: bfloat16 [2, 512, 192, 1024], P(None, ('groups', 'gx'), None, 'ta'), parts along dimension 1, may hold values from -6 to 6
- lengths: int32 [512], P(('groups', 'gx')), parts along dimension 0, may hold values from 2 to 192, as said below
- out_proj: bfloat16 [6144, 3072], P('ta', 'gx'), may hold values from -0.078125 to 0.078125
- norm_gain: float32 [3072], replicated, may hold values from 0.1 to 1.9
- expert_ids: int32 [512, 4], P('groups'), parts along dimension 0, may hold values from 0 to 3, as said below
- gate_weights: float32 [512, 4], P(('groups', 'gx')), parts along dimension 0, may hold values from 0.05 to 0.6
- w_up: bfloat16 [4, 3072, 5376], P('gx', None, 'ta'), may hold values from -0.109375 to 0.109375
- w_down: bfloat16 [4, 5376, 3072], P('gx', 'ta'), may hold values from -0.109375 to 0.109375
Outputs:
- mixture: bfloat16 [512, 3072], P(('groups', 'gx'), 'ta'), parts along dimension 0
The draws below stay inside these ranges and needn't reach their ends.
There are 2 independent parts, one for each index of `groups`. The reference program is written for one: setup_inputs(seed, part) draws one part's arguments, and reference() takes and returns one part's arrays. A program takes and returns all parts, laid end to end along the dimension named above; an argument that names none is the same for every part. Nothing has to cross between parts.
Inputs may be any that keep to these rules, and one draw needn't show every extreme that they name: `lengths`: in every aligned block of 64 rows at least one row has length 192. `expert_ids`: each row names 4 different experts. In every aligned block of 64 rows one expert, the same for all blocks, is named by exactly 64 rows; every other expert by at most 64 rows, and the counts of the other experts in a block differ by at most one.
All inputs are finite; a program needn't handle non-finite values.
Results may differ from the reference program's by a relative error of at most 0.017.
Values may be sent and summed in bfloat16 or wider, within the bound.
No kernel may reach another device: no remote copies, remote signals or barrier semaphores. Data moves between devices by JAX's collectives and lax.ppermute only.
A program may use at most 128 MiB of HBM per device.

```python
import math
import jax
import jax.numpy as jnp
from jax import lax

D = 3072
HEADS = 48
KVH = 8
HD = 128
FFW = 5376
TOPK = 4
CTX = 192
ROWS_DEV = 64
ROWS = 256
EXPERTS = 4
CAP = 64
N_TA = 4


def draw_kv_cache(key, part):
    key = jax.random.fold_in(key, 11)
    cache = jnp.clip(jax.random.normal(key, (2, ROWS, CTX, KVH * HD), jnp.float32), -6.0, 6.0)
    return cache.astype(jnp.bfloat16)


def draw_queries(key, part):
    key = jax.random.fold_in(key, 12)
    values = jnp.clip(jax.random.normal(key, (ROWS, HEADS * HD), jnp.float32), -6.0, 6.0)
    return values.astype(jnp.bfloat16)


def draw_lengths(key, part):
    key = jax.random.fold_in(key, 13)
    drawn = jax.random.randint(key, (ROWS,), 2, CTX + 1)
    chosen = jax.random.randint(jax.random.fold_in(key, 1), (ROWS // ROWS_DEV, 1), 0, ROWS_DEV)
    longest = (jnp.arange(ROWS_DEV)[None, :] == chosen).reshape(ROWS)
    return jnp.where(longest, CTX, drawn).astype(jnp.int32)


def draw_expert_ids(key, part):
    key = jax.random.fold_in(key, 14)
    blocks = ROWS // ROWS_DEV
    picks = ROWS_DEV * TOPK
    hottest = jax.random.randint(key, (), 0, EXPERTS)
    position = jnp.arange(picks)
    level = jnp.where(position < CAP, 0, 1 + (position - CAP) * (EXPERTS - 1) // (picks - CAP))

    def one_block(index):
        block_key = jax.random.fold_in(key, index + 1)
        order = jax.random.permutation(block_key, EXPERTS - 1)
        others = order[jnp.clip(level - 1, 0, EXPERTS - 2)]
        others = others + (others >= hottest).astype(jnp.int32)
        chosen = jnp.where(level == 0, hottest, others)
        table = chosen.reshape(TOPK, ROWS_DEV).T
        shuffle = jax.random.permutation(jax.random.fold_in(block_key, 5), ROWS_DEV)
        table = table[shuffle]
        turns = jax.random.randint(jax.random.fold_in(block_key, 6), (ROWS_DEV, 1), 0, TOPK)
        columns = (jnp.arange(TOPK)[None, :] + turns) % TOPK
        return jnp.take_along_axis(table, columns, axis=1)
    result = jax.vmap(one_block)(jnp.arange(blocks))
    return result.reshape(ROWS, TOPK).astype(jnp.int32)


def with_spikes(array, key, source, target, parts, factor):
    def block_of(dim):
        return (jnp.arange(array.shape[dim]) // (array.shape[dim] // parts)).reshape((-1,) + (1,) * (array.ndim - 1 - dim))

    first = jax.random.permutation(key, parts)[block_of(target)]
    far = (block_of(target) + parts // 2) % parts
    return jnp.where((block_of(source) == first) | (block_of(source) == far), factor * array, array)


def level_of(rng, shape, split, least, high):
    gain = 1.0
    for dim, shards_of in split:
        draws = jax.random.uniform(jax.random.fold_in(jax.random.fold_in(rng, 6), dim), (shards_of,), jnp.float32, least / len(split), high / len(split))
        gain = gain * jnp.repeat(jnp.exp(draws), shape[dim] // shards_of).reshape((-1,) + (1,) * (len(shape) - 1 - dim))
    return gain


def bell_draw(own_key, dims, width, limit, shards=(), kind=jnp.bfloat16):
    entries = jax.random.normal(own_key, dims, jnp.float32) * width
    if len(shards) > 0:
        entries = level_of(own_key, dims, shards, -0.22, 0.18) * entries
    return jnp.clip(entries, min=-limit, max=limit).astype(kind)


def gaussian_with(key, dims, scale, most, cuts, heavy, held_as=jnp.bfloat16):
    array = scale * jax.random.normal(key, dims, jnp.float32)
    if cuts:
        array = array * level_of(key, dims, cuts, -0.22, 0.18)
    return jnp.clip(with_spikes(array, jax.random.fold_in(key, 3), *heavy), -most, most).astype(held_as)


def setup_inputs(seed: int = 0, part: int = 0) -> dict:
    key_list = jax.random.split(jax.random.key(seed), 11)
    own_keys = jax.random.split(jax.random.fold_in(key_list[10], part), 11)
    queries = draw_queries(jax.random.fold_in(jax.random.fold_in(key_list[10], part), 71), part)
    new_kv = bell_draw(own_keys[1], (2, ROWS, KVH * HD), 1.0, 6.0, ((1, 4), (2, 4)))
    kv_cache = draw_kv_cache(jax.random.fold_in(jax.random.fold_in(key_list[10], part), 71), part)
    lengths = draw_lengths(jax.random.fold_in(jax.random.fold_in(key_list[10], part), 71), part)
    out_proj = bell_draw(key_list[4], (HEADS * HD, D), (HEADS * HD) ** -0.5, 0.078125, ((0, 4), (1, 4)))
    norm_gain = jnp.clip(1.0 + 0.18 * jax.random.normal(key_list[5], (D,), jnp.float32), 0.1, 1.9)
    expert_ids = draw_expert_ids(jax.random.fold_in(jax.random.fold_in(key_list[10], part), 71), part)
    gate_weights = jnp.clip(0.05 + 0.55 * jax.random.uniform(own_keys[7], (ROWS, TOPK), jnp.float32) ** level_of(own_keys[7], (ROWS, TOPK), ((0, 4),), -0.2, 0.2), 0.05, 0.6)
    w_up = bell_draw(key_list[8], (EXPERTS, D, FFW), D ** -0.5, 0.109375, ((0, 4), (2, 4)))
    w_down = gaussian_with(key_list[9], (EXPERTS, FFW, D), FFW ** -0.5, 0.109375, ((0, 4), (1, 4)), (1, 2, 4, 2.0))
    return dict(queries=queries, new_kv=new_kv, kv_cache=kv_cache, lengths=lengths, out_proj=out_proj, norm_gain=norm_gain, expert_ids=expert_ids, gate_weights=gate_weights, w_up=w_up, w_down=w_down)


def route_tables(expert_ids, expert_count, block_rows, capacity):
    blocks = expert_ids.shape[0] // block_rows
    expert_range = jnp.arange(expert_count, dtype=jnp.int32)
    matches = (expert_ids[:, :, None] == expert_range[None, None, :]).astype(jnp.int32)
    routed = lax.optimization_barrier(jnp.sum(matches, axis=1)).reshape(blocks, block_rows, expert_count)
    position = (jnp.cumsum(routed, axis=1) - routed).astype(jnp.int32)
    slot_range = jnp.arange(capacity, dtype=jnp.int32)
    slot_hits = routed[:, :, :, None] * (position[:, :, :, None] == slot_range[None, None, None, :]).astype(jnp.int32)
    row_range = jnp.arange(block_rows, dtype=jnp.int32)
    block_start = (jnp.arange(blocks, dtype=jnp.int32) * block_rows)[:, None, None]
    source_row = lax.optimization_barrier(jnp.sum(slot_hits * row_range[None, :, None, None], axis=1)) + block_start
    filled = lax.optimization_barrier(jnp.sum(slot_hits, axis=1))
    source_row = jnp.transpose(source_row, (1, 0, 2)).reshape(expert_count, blocks * capacity)
    filled = jnp.transpose(filled, (1, 0, 2)).reshape(expert_count, blocks * capacity)
    pick_slot = lax.optimization_barrier(jnp.sum(matches * position.reshape(blocks * block_rows, 1, expert_count), axis=2))
    return (source_row, filled, pick_slot)

def attend(queries, cache_keys, cache_values, fresh_keys, fresh_values, lengths):
    row_count = queries.shape[0]
    context = cache_keys.shape[1]
    kv_heads = fresh_keys.shape[1] // HD
    group_size = queries.shape[1] // (HD * kv_heads)
    scale = 1.0 / math.sqrt(HD)
    query_heads = queries.astype(jnp.float32).reshape(row_count, kv_heads, group_size, HD)
    key_heads = cache_keys.astype(jnp.float32).reshape(row_count, context, kv_heads, HD)
    value_heads = cache_values.astype(jnp.float32).reshape(row_count, context, kv_heads, HD)
    fresh_key = fresh_keys.astype(jnp.float32).reshape(row_count, kv_heads, HD)
    fresh_value = fresh_values.astype(jnp.float32).reshape(row_count, kv_heads, HD)
    cached = jnp.einsum('rkgd,rckd->rkgc', query_heads, key_heads) * scale
    own_score = jnp.einsum('rkgd,rkd->rkg', query_heads, fresh_key)[..., None] * scale
    visible = jnp.arange(context, dtype=jnp.int32)[None, :] < lengths[:, None]
    cached = jnp.where(visible[:, None, None, :], cached, -jnp.inf)
    scores = jnp.concatenate([cached, own_score], axis=3)
    largest = lax.optimization_barrier(jnp.max(scores, axis=3, keepdims=True))
    lifted = jnp.exp(scores - largest)
    probs = (lifted / lax.optimization_barrier(jnp.sum(lifted, axis=3, keepdims=True))).astype(jnp.bfloat16)
    probs = lax.optimization_barrier(probs).astype(jnp.float32)
    mixed = jnp.einsum('rkgc,rckd->rkgd', probs[..., :context], value_heads)
    mixed = mixed + probs[..., context:] * fresh_value[:, :, None, :]
    return mixed.reshape(row_count, -1).astype(jnp.bfloat16)

def layer_norm(hidden, norm_gain):
    values = hidden.astype(jnp.float32)
    center = values - lax.optimization_barrier(jnp.mean(values, axis=1, keepdims=True))
    spread = lax.optimization_barrier(jnp.mean(center * center, axis=1, keepdims=True))
    return (center * lax.rsqrt(spread + 1e-05) * norm_gain).astype(jnp.bfloat16)

def reference(queries, new_kv, kv_cache, lengths, out_proj, norm_gain, expert_ids, gate_weights, w_up, w_down):
    blocks = ROWS // ROWS_DEV
    shaped = (queries.reshape(blocks, ROWS_DEV, HEADS * HD), kv_cache[0].reshape(blocks, ROWS_DEV, CTX, KVH * HD), kv_cache[1].reshape(blocks, ROWS_DEV, CTX, KVH * HD), new_kv[0].reshape(blocks, ROWS_DEV, KVH * HD), new_kv[1].reshape(blocks, ROWS_DEV, KVH * HD), lengths.reshape(blocks, ROWS_DEV))
    attended = lax.map(lambda operands: attend(*operands), shaped).reshape(ROWS, HEADS * HD)
    head_width = HEADS * HD // N_TA
    pieces = jnp.einsum('rjh,jhd->jrd', attended.astype(jnp.float32).reshape(ROWS, N_TA, head_width), out_proj.astype(jnp.float32).reshape(N_TA, head_width, D))
    pieces = lax.optimization_barrier(pieces.astype(jnp.bfloat16)).astype(jnp.float32)
    hidden = lax.optimization_barrier(jnp.sum(pieces, axis=0)).astype(jnp.bfloat16)
    normed = layer_norm(hidden, norm_gain)
    source_row, filled, pick_slot = route_tables(expert_ids, EXPERTS, ROWS_DEV, CAP)

    def run_expert(operands):
        up_matrix, down_matrix, rows_used, used = operands
        inputs = jnp.where(used[:, None] > 0, normed[rows_used], jnp.zeros((), jnp.bfloat16))
        raised = jnp.dot(inputs.astype(jnp.float32), up_matrix.astype(jnp.float32), preferred_element_type=jnp.float32)
        active = jax.nn.silu(raised).astype(jnp.bfloat16)
        lowered = jnp.dot(active.astype(jnp.float32), down_matrix.astype(jnp.float32), preferred_element_type=jnp.float32)
        return lowered.astype(jnp.bfloat16)
    outputs = lax.map(run_expert, (w_up, w_down, source_row, filled))
    block_index = (jnp.arange(ROWS, dtype=jnp.int32) // ROWS_DEV)[:, None]
    picked = outputs[expert_ids, block_index * CAP + pick_slot]
    return lax.optimization_barrier(jnp.sum(picked.astype(jnp.float32) * gate_weights[:, :, None], axis=1)).astype(jnp.bfloat16)
```

```python
import functools
import math

import jax
import jax.numpy as jnp
from jax import lax
from jax.experimental import pallas as pl
from jax.experimental.pallas import tpu as pltpu
from jax.sharding import PartitionSpec as P

HD = 128
MIB = 1 << 20
VMEM = pl.BlockSpec(memory_space=pltpu.VMEM)
SMEM = pl.BlockSpec(memory_space=pltpu.SMEM)
F32 = jnp.float32
BF16 = jnp.bfloat16


def local_call(kernel, out_shape, in_specs, scratch=(), vmem=32, flops=0, moved=0, name=None):
    several = isinstance(out_shape, (tuple, list))
    return pl.pallas_call(
        kernel,
        out_shape=out_shape,
        in_specs=in_specs,
        out_specs=[VMEM] * len(out_shape) if several else VMEM,
        scratch_shapes=list(scratch),
        compiler_params=pltpu.CompilerParams(vmem_limit_bytes=vmem * MIB),
        cost_estimate=pl.CostEstimate(flops=flops, bytes_accessed=moved, transcendentals=0),
        name=name,
    )


def attend_kernel(
    kv_heads, group, slots, batch,
    lengths_ref, q_ref, fresh_ref, cache_ref, out_ref,
    keys, values, q_rows, scores, own_scores, probs, own_probs, mixed, sems,
):
    rows = q_ref.shape[0]
    context = keys.shape[1]
    width = kv_heads * HD
    heads = kv_heads * group
    steps = rows // batch
    scale = 1.0 / math.sqrt(HD)

    def fetch(step, kind):
        part = pl.ds(step * batch, batch)
        buffer = (keys, values)[kind]
        return pltpu.make_async_copy(
            cache_ref.at[kind, part], buffer.at[part], sems.at[kind, step]
        )

    for step in range(steps):
        for kind in range(2):
            fetch(step, kind).start()
    q_rows[...] = jnp.zeros_like(q_rows)
    for head in range(heads):
        q_rows[head // group, pl.ds(head, rows, stride=slots), :] = q_ref[
            :, head * HD : (head + 1) * HD
        ].astype(F32)
    place = lax.broadcasted_iota(jnp.int32, (slots, context), 1)
    for step in range(steps):
        fetch(step, 0).wait()
        for k in range(batch):
            row = step * batch + k
            mine = jnp.concatenate(
                [q_rows[g, row * slots : (row + 1) * slots, :] for g in range(kv_heads)], axis=1
            )
            cached = lax.dot_general(
                mine.astype(BF16), keys[row], (((1,), (1,)), ((), ())),
                preferred_element_type=F32,
            )
            here = slice(k * slots, (k + 1) * slots)
            scores[here, :] = jnp.where(place < lengths_ref[row], cached * scale, -jnp.inf)
            fresh_key = fresh_ref[0, row : row + 1, :].astype(F32)
            own_scores[here, :] = jnp.broadcast_to(
                jnp.sum(mine * fresh_key, axis=1, keepdims=True) * scale, (slots, HD)
            )
        cached = scores[...]
        own = own_scores[:, :1]
        largest = jnp.maximum(jnp.max(cached, axis=1, keepdims=True), own)
        lifted = jnp.exp(cached - largest)
        own_lifted = jnp.exp(own - largest)
        total = jnp.sum(lifted, axis=1, keepdims=True) + own_lifted
        probs[...] = (lifted / total).astype(BF16)
        own_probs[...] = jnp.broadcast_to(
            (own_lifted / total).astype(BF16).astype(F32), own_probs.shape
        )
        fetch(step, 1).wait()
        for k in range(batch):
            row = step * batch + k
            here = slice(k * slots, (k + 1) * slots)
            weighted = jnp.dot(probs[here, :], values[row], preferred_element_type=F32)
            fresh_value = fresh_ref[1, row : row + 1, :].astype(F32)
            total = weighted + own_probs[here, :1] * fresh_value
            for g in range(kv_heads):
                mixed[g, here, :] = total[:, g * HD : (g + 1) * HD]
        for head in range(heads):
            out_ref[step * batch : (step + 1) * batch, head * HD : (head + 1) * HD] = mixed[
                head // group, pl.ds(head, batch, stride=slots), :
            ].astype(BF16)


def attend(queries, new_kv, kv_cache, lengths):
    rows, features = queries.shape
    context, width = kv_cache.shape[2:]
    kv_heads = width // HD
    heads = features // HD
    slots = -(-heads // 8) * 8
    batch = 16
    return pl.pallas_call(
        functools.partial(attend_kernel, kv_heads, heads // kv_heads, slots, batch),
        out_shape=jax.ShapeDtypeStruct(queries.shape, BF16),
        in_specs=[SMEM, VMEM, VMEM, pl.BlockSpec(memory_space=pl.ANY)],
        out_specs=VMEM,
        scratch_shapes=[
            pltpu.VMEM((rows, context, width), BF16),
            pltpu.VMEM((rows, context, width), BF16),
            pltpu.VMEM((kv_heads, rows * slots, HD), F32),
            pltpu.VMEM((batch * slots, context), F32),
            pltpu.VMEM((batch * slots, HD), F32),
            pltpu.VMEM((batch * slots, context), BF16),
            pltpu.VMEM((batch * slots, HD), F32),
            pltpu.VMEM((kv_heads, batch * slots, HD), F32),
            pltpu.SemaphoreType.DMA((2, rows // batch)),
        ],
        compiler_params=pltpu.CompilerParams(vmem_limit_bytes=56 * MIB),
        cost_estimate=pl.CostEstimate(
            flops=4 * rows * slots * context * width,
            bytes_accessed=2 * kv_cache.size,
            transcendentals=rows * slots * context,
        ),
        name="attend",
    )(lengths, queries, new_kv, kv_cache)


def project_kernel(parts, place_ref, *refs):
    shards, weight_ref = refs[:parts], refs[parts]
    outs, held = refs[parts + 1 : parts + 1 + parts], refs[-1]
    rows = shards[0].shape[0]
    turn = place_ref[0] ^ place_ref[1]
    block = jnp.concatenate([shard[...] for shard in shards], axis=0)
    pieces = jnp.dot(block, weight_ref[...], preferred_element_type=F32).astype(BF16)
    for s in range(parts):
        held[turn ^ s] = pieces[s * rows : (s + 1) * rows, :]
    for t in range(parts):
        outs[t][...] = held[t]


def add_kernel(*refs):
    terms, out = refs[:-1], refs[-1]
    total = terms[0][...].astype(F32)
    for term in terms[1:]:
        total = total + term[...].astype(F32)
    out[...] = total.astype(BF16)


def norm_kernel(parts, place_ref, gain_ref, *refs):
    shards, out, held = refs[:parts], refs[parts], refs[parts + 1]
    width = shards[0].shape[1]
    for s in range(parts):
        first = pl.multiple_of((place_ref[0] ^ s) * width, HD)
        held[:, pl.ds(first, width)] = shards[s][...].astype(F32)
    values = held[...]
    center = values - jnp.mean(values, axis=1, keepdims=True)
    spread = jnp.mean(center * center, axis=1, keepdims=True)
    out[...] = (center * lax.rsqrt(spread + 1e-05) * gain_ref[...]).astype(BF16)


def expert_kernel(parts, place_ref, *refs):
    shards, (up_ref, down_ref), outs = refs[:parts], refs[parts : parts + 2], refs[parts + 2 : -2]
    held, active = refs[-2:]
    far_ref, cross_ref, own_ref = outs
    hidden = up_ref.shape[0]
    share = own_ref.shape[1]
    rows = shards[0].shape[0]
    for t in range(parts):
        first = pl.multiple_of((place_ref[1] ^ t) * rows, rows)
        held[pl.ds(first, rows), :] = shards[t][...]
    block = held[...]
    for first in range(0, hidden, 256):
        last = min(first + 256, hidden)
        raised = lax.dot_general(
            block, up_ref[first:last, :], (((1,), (1,)), ((), ())), preferred_element_type=F32
        )
        active[:, first:last] = (raised / (1.0 + jnp.exp(-raised))).astype(BF16)

    def lowered(turn):
        first = pl.multiple_of((place_ref[1] ^ turn) * share, HD)
        return jnp.dot(
            active[...], down_ref[:, pl.ds(first, share)], preferred_element_type=F32
        )

    far_ref[0] = lowered(1).astype(BF16)
    far_ref[1] = lowered(3).astype(BF16)
    cross_ref[...] = lowered(2)
    own_ref[...] = lowered(0)


def cross_kernel(cross_ref, near_ref, out_ref):
    out_ref[...] = (cross_ref[...] + near_ref[1].astype(F32)).astype(BF16)


def split_kernel(parts, place_ref, own_ref, near_ref, cross_ref, *outs):
    rows = outs[0].shape[0]
    for s in range(parts):
        here = pl.ds(pl.multiple_of((place_ref[0] ^ s) * rows, rows), rows)
        total = own_ref[here, :] + near_ref[0, here, :].astype(F32) + cross_ref[here, :].astype(F32)
        outs[s][...] = total.astype(BF16)


def mix_kernel(parts, place_ref, ids_ref, gates_ref, *refs):
    terms, out = refs[:parts], refs[parts]
    rows = out.shape[0]
    ids = ids_ref[pl.ds(pl.multiple_of(place_ref[0] * rows, rows), rows), :]
    total = jnp.zeros(out.shape, F32)
    for s in range(parts):
        gate = jnp.sum(
            jnp.where(ids == (place_ref[0] ^ s), gates_ref[...], 0.0), axis=1, keepdims=True
        )
        total = total + gate * terms[s][...].astype(F32)
    out[...] = total.astype(BF16)


def trade(array, axis, turn):
    count = lax.axis_size(axis)
    return lax.ppermute(array, axis, [(k, k ^ turn) for k in range(count)])


def every_row_body(attended, out_proj, norm_gain, expert_ids, gate_weights, w_up, w_down):
    gx_count = lax.axis_size("gx")
    ta_count = lax.axis_size("ta")
    rows = attended.shape[0]
    width = out_proj.shape[1]
    model = norm_gain.shape[0]
    share = model // ta_count
    all_rows = rows * gx_count
    place = jnp.stack([lax.axis_index("gx"), lax.axis_index("ta")]).astype(jnp.int32)
    shape = jax.ShapeDtypeStruct
    shards = [attended] + [trade(attended, "gx", s) for s in range(1, gx_count)]
    pieces = local_call(
        functools.partial(project_kernel, gx_count),
        [shape((rows, width), BF16)] * ta_count,
        [SMEM] + [VMEM] * (gx_count + 1),
        [pltpu.VMEM((ta_count, rows, width), BF16)],
        flops=2 * all_rows * out_proj.size,
        moved=2 * out_proj.size,
        name="project",
    )(place, *shards, out_proj)
    pieces = [pieces[0]] + [trade(pieces[t], "ta", t) for t in range(1, ta_count)]
    hidden = local_call(
        add_kernel, shape((rows, width), BF16), [VMEM] * ta_count, moved=8 * rows * width, name="add"
    )(*pieces)
    hidden = [hidden] + [trade(hidden, "gx", s) for s in range(1, gx_count)]
    normed = local_call(
        functools.partial(norm_kernel, gx_count),
        shape((rows, model), BF16),
        [SMEM] + [VMEM] * (gx_count + 1),
        [pltpu.VMEM((rows, model), F32)],
        moved=4 * rows * model,
        name="norm",
    )(place, norm_gain.reshape(1, model), *hidden)
    over_x = trade(normed, "ta", 2)
    blocks = [normed, trade(normed, "ta", 1), over_x, trade(over_x, "ta", 1)]
    far, cross, own = local_call(
        functools.partial(expert_kernel, ta_count),
        [
            shape((2, all_rows, share), BF16),
            shape((all_rows, share), F32),
            shape((all_rows, share), F32),
        ],
        [SMEM] + [VMEM] * (ta_count + 2),
        [pltpu.VMEM((all_rows, model), BF16), pltpu.VMEM((all_rows, w_up.shape[2]), BF16)],
        vmem=40,
        flops=4 * all_rows * w_up.size,
        moved=4 * w_up.size,
        name="experts",
    )(place, *blocks, jnp.swapaxes(w_up[0], 0, 1), w_down[0])
    near = trade(far, "ta", 1)
    crossing = local_call(
        cross_kernel, shape((all_rows, share), BF16), [VMEM] * 2, moved=8 * all_rows * share, name="cross"
    )(cross, near)
    crossed = trade(crossing, "ta", 2)
    terms = local_call(
        functools.partial(split_kernel, gx_count),
        [shape((rows, share), BF16)] * gx_count,
        [SMEM] + [VMEM] * 3,
        moved=10 * all_rows * share,
        name="split",
    )(place, own, near, crossed)
    terms = [terms[0]] + [trade(terms[s], "gx", s) for s in range(1, gx_count)]
    return local_call(
        functools.partial(mix_kernel, gx_count),
        shape((rows, share), BF16),
        [SMEM] + [VMEM] * (gx_count + 2),
        moved=10 * rows * share,
        name="mix",
    )(place, expert_ids, gate_weights, *terms)


def route_tables(expert_ids, expert_count, block_rows, capacity):
    blocks = expert_ids.shape[0] // block_rows
    expert_range = jnp.arange(expert_count, dtype=jnp.int32)
    matches = (expert_ids[:, :, None] == expert_range[None, None, :]).astype(jnp.int32)
    routed = jnp.sum(matches, axis=1).reshape(blocks, block_rows, expert_count)
    position = jnp.cumsum(routed, axis=1) - routed
    slot_range = jnp.arange(capacity, dtype=jnp.int32)
    slot_hits = routed[:, :, :, None] * (
        position[:, :, :, None] == slot_range[None, None, None, :]
    ).astype(jnp.int32)
    row_range = jnp.arange(block_rows, dtype=jnp.int32)
    block_start = (jnp.arange(blocks, dtype=jnp.int32) * block_rows)[:, None, None]
    source_row = jnp.sum(slot_hits * row_range[None, :, None, None], axis=1) + block_start
    filled = jnp.sum(slot_hits, axis=1)
    source_row = jnp.transpose(source_row, (1, 0, 2)).reshape(expert_count, blocks * capacity)
    filled = jnp.transpose(filled, (1, 0, 2)).reshape(expert_count, blocks * capacity)
    pick_slot = jnp.sum(matches * position.reshape(blocks * block_rows, 1, expert_count), axis=2)
    return (source_row, filled, pick_slot)


def layer_norm(hidden, norm_gain):
    values = hidden.astype(jnp.float32)
    center = values - jnp.mean(values, axis=1, keepdims=True)
    spread = jnp.mean(center * center, axis=1, keepdims=True)
    return (center * lax.rsqrt(spread + 1e-05) * norm_gain).astype(jnp.bfloat16)


def body(
    queries, new_kv, kv_cache, lengths, out_proj, norm_gain, expert_ids, gate_weights, w_up, w_down
):
    gx_count = lax.axis_size("gx")
    ta_count = lax.axis_size("ta")
    block_rows = queries.shape[0]
    top_count = expert_ids.shape[1]
    capacity = min(block_rows, 2 * block_rows * top_count // gx_count)
    slot_count = gx_count * capacity
    model_width = norm_gain.shape[0]
    width_share = model_width // ta_count
    attended = attend(queries, new_kv, kv_cache, lengths)
    if gx_count == top_count and ta_count == gx_count == 4:
        return every_row_body(
            attended, out_proj, norm_gain, expert_ids, gate_weights, w_up, w_down
        )
    projected = jnp.dot(
        lax.all_gather(attended, "gx", axis=0, tiled=True),
        out_proj,
        preferred_element_type=jnp.float32,
    ).astype(jnp.bfloat16)
    source_row, filled, pick_slot = route_tables(expert_ids, gx_count, block_rows, capacity)
    live_slots = (filled > 0)[:, :, None]
    widened = lax.optimization_barrier(projected).astype(jnp.float32)
    hidden_share = lax.psum_scatter(
        widened.astype(jnp.bfloat16), "ta", scatter_dimension=1, tiled=True
    )
    outgoing = jnp.where(live_slots, hidden_share[source_row], jnp.zeros((), jnp.bfloat16))[
        :, :, None, :
    ]
    arrived = lax.all_to_all(outgoing, "gx", split_axis=0, concat_axis=2, tiled=True)
    gathered = lax.all_gather(arrived, "ta", axis=3, tiled=True)
    hidden = gathered.reshape(slot_count, model_width)
    normed = layer_norm(hidden, norm_gain)
    raised = jnp.dot(normed, w_up[0], preferred_element_type=jnp.float32)
    active = jax.nn.silu(raised).astype(jnp.bfloat16)
    terms = jnp.dot(active, w_down[0], preferred_element_type=jnp.float32)
    mine = lax.psum_scatter(terms, "ta", scatter_dimension=1, tiled=True)
    result = mine.astype(jnp.bfloat16).reshape(gx_count, capacity, width_share)
    returned = lax.all_to_all(result, "gx", split_axis=0, concat_axis=0, tiled=True)
    first_row = lax.axis_index("gx") * block_rows
    local_ids = lax.dynamic_slice_in_dim(expert_ids, first_row, block_rows, 0)
    local_slot = lax.dynamic_slice_in_dim(pick_slot, first_row, block_rows, 0)
    flat_rows = returned.reshape(gx_count * capacity, width_share)
    picked = flat_rows[local_ids * capacity + local_slot]
    return jnp.sum(picked.astype(jnp.float32) * gate_weights[:, :, None], axis=1).astype(
        jnp.bfloat16
    )


def solution(mesh):
    return jax.shard_map(
        body,
        mesh=mesh,
        in_specs=(
            P(("groups", "gx"), "ta"),
            P(None, ("groups", "gx"), "ta"),
            P(None, ("groups", "gx"), None, "ta"),
            P(("groups", "gx")),
            P("ta", "gx"),
            P(),
            P("groups", None),
            P(("groups", "gx"), None),
            P("gx", None, "ta"),
            P("gx", "ta", None),
        ),
        out_specs=P(("groups", "gx"), "ta"),
        check_vma=False,
    )
```

```python
import functools
import math

import jax
import jax.numpy as jnp
from jax import lax
from jax.experimental import pallas as pl
from jax.experimental.pallas import tpu as pltpu
from jax.sharding import PartitionSpec as P

HD = 128
MIB = 1 << 20
VMEM = pl.BlockSpec(memory_space=pltpu.VMEM)
SMEM = pl.BlockSpec(memory_space=pltpu.SMEM)
F32 = jnp.float32
BF16 = jnp.bfloat16


ANYWHERE = pl.BlockSpec(memory_space=pl.ANY)


def local_call(kernel, out_shape, in_specs, scratch=(), vmem=32, name=None, after=None):
    several = isinstance(out_shape, (tuple, list))
    if after is not None:
        count, inner = len(in_specs), kernel
        in_specs = [*in_specs, ANYWHERE]
        kernel = lambda *refs: inner(*refs[:count], *refs[count + 1 :])
    call = pl.pallas_call(
        kernel,
        out_shape=out_shape,
        in_specs=in_specs,
        out_specs=[VMEM] * len(out_shape) if several else VMEM,
        scratch_shapes=list(scratch),
        compiler_params=pltpu.CompilerParams(vmem_limit_bytes=vmem * MIB),
        cost_estimate=pl.CostEstimate(flops=1024, bytes_accessed=1024, transcendentals=0),
        name=name,
    )
    return call if after is None else lambda *args: call(*args, after)


def attend_kernel(
    kv_heads, group, slots, batch, begin,
    lengths_ref, q_ref, fresh_ref, cache_ref, after_ref, out_ref,
    keys, values, q_rows, scores, own_scores, probs, own_probs, mixed, sems,
):
    rows = out_ref.shape[0]
    context = keys.shape[1]
    width = kv_heads * HD
    heads = kv_heads * group
    steps = rows // batch
    scale = 1.0 / math.sqrt(HD)

    def fetch(step, kind):
        buffer = (keys, values)[kind]
        return pltpu.make_async_copy(
            cache_ref.at[kind, pl.ds(begin + step * batch, batch)],
            buffer.at[pl.ds(step * batch, batch)],
            sems.at[kind, step],
        )

    for step in range(steps):
        for kind in range(2):
            fetch(step, kind).start()
    q_rows[...] = jnp.zeros_like(q_rows)
    for head in range(heads):
        q_rows[head // group, pl.ds(head, rows, stride=slots), :] = q_ref[
            begin : begin + rows, head * HD : (head + 1) * HD
        ].astype(F32)
    place = lax.broadcasted_iota(jnp.int32, (slots, context), 1)
    for step in range(steps):
        fetch(step, 0).wait()
        for k in range(batch):
            row = step * batch + k
            mine = jnp.concatenate(
                [q_rows[g, row * slots : (row + 1) * slots, :] for g in range(kv_heads)], axis=1
            )
            cached = lax.dot_general(
                mine.astype(BF16), keys[row], (((1,), (1,)), ((), ())),
                preferred_element_type=F32,
            )
            here = slice(k * slots, (k + 1) * slots)
            scores[here, :] = jnp.where(place < lengths_ref[begin + row], cached * scale, -jnp.inf)
            fresh_key = fresh_ref[0, begin + row : begin + row + 1, :].astype(F32)
            own_scores[here, :] = jnp.broadcast_to(
                jnp.sum(mine * fresh_key, axis=1, keepdims=True) * scale, (slots, HD)
            )
        cached = scores[...]
        own = own_scores[:, :1]
        largest = jnp.maximum(jnp.max(cached, axis=1, keepdims=True), own)
        lifted = jnp.exp(cached - largest)
        own_lifted = jnp.exp(own - largest)
        total = jnp.sum(lifted, axis=1, keepdims=True) + own_lifted
        probs[...] = (lifted / total).astype(BF16)
        own_probs[...] = jnp.broadcast_to(
            (own_lifted / total).astype(BF16).astype(F32), own_probs.shape
        )
        fetch(step, 1).wait()
        for k in range(batch):
            row = step * batch + k
            here = slice(k * slots, (k + 1) * slots)
            weighted = jnp.dot(probs[here, :], values[row], preferred_element_type=F32)
            fresh_value = fresh_ref[1, begin + row : begin + row + 1, :].astype(F32)
            total = weighted + own_probs[here, :1] * fresh_value
            for g in range(kv_heads):
                mixed[g, here, :] = total[:, g * HD : (g + 1) * HD]
        for head in range(heads):
            out_ref[step * batch : (step + 1) * batch, head * HD : (head + 1) * HD] = mixed[
                head // group, pl.ds(head, batch, stride=slots), :
            ].astype(BF16)


def attend(queries, new_kv, kv_cache, lengths, begin, rows, after):
    features = queries.shape[1]
    context, width = kv_cache.shape[2:]
    kv_heads = width // HD
    heads = features // HD
    slots = -(-heads // 8) * 8
    batch = 16
    return pl.pallas_call(
        functools.partial(attend_kernel, kv_heads, heads // kv_heads, slots, batch, begin),
        out_shape=jax.ShapeDtypeStruct((rows, features), BF16),
        in_specs=[SMEM, VMEM, VMEM, ANYWHERE, ANYWHERE],
        out_specs=VMEM,
        scratch_shapes=[
            pltpu.VMEM((rows, context, width), BF16),
            pltpu.VMEM((rows, context, width), BF16),
            pltpu.VMEM((kv_heads, rows * slots, HD), F32),
            pltpu.VMEM((batch * slots, context), F32),
            pltpu.VMEM((batch * slots, HD), F32),
            pltpu.VMEM((batch * slots, context), BF16),
            pltpu.VMEM((batch * slots, HD), F32),
            pltpu.VMEM((kv_heads, batch * slots, HD), F32),
            pltpu.SemaphoreType.DMA((2, rows // batch)),
        ],
        compiler_params=pltpu.CompilerParams(vmem_limit_bytes=53 * MIB),
        cost_estimate=pl.CostEstimate(flops=1024, bytes_accessed=1024, transcendentals=0),
        name="attend",
    )(lengths, queries, new_kv, kv_cache, after)


def pair_kernel(own_ref, other_ref, out_ref):
    out_ref[0] = own_ref[...]
    out_ref[1] = other_ref[...]


def gather_pair(owned, others, after):
    pairs = []
    for own, other in zip(owned, others):
        out = jax.ShapeDtypeStruct((2, *own.shape), own.dtype)
        after = pairs[-1] if pairs else after
        pairs.append(local_call(pair_kernel, out, [VMEM] * 2, name="pair", after=after)(own, other))
    return pairs


def by_distance(pair_ref, second_ref):
    return pair_ref.at[0], second_ref.at[0], pair_ref.at[1], second_ref.at[1]


def project_kernel(
    place_ref, pair_ref, second_ref, weight_ref, own_ref, cross_ref, far_ref, held
):
    shards = by_distance(pair_ref, second_ref)
    rows = own_ref.shape[0]
    turn = place_ref[0] ^ place_ref[1]
    block = jnp.concatenate([shard[...] for shard in shards], axis=0)
    pieces = jnp.dot(block, weight_ref[...], preferred_element_type=F32)
    for s in range(len(shards)):
        held[turn ^ s] = pieces[s * rows : (s + 1) * rows, :]
    own_ref[...] = held[0]
    cross_ref[...] = held[2]
    far_ref[0] = held[1].astype(BF16)
    far_ref[1] = held[3].astype(BF16)


def cross_kernel(cross_ref, near_ref, out_ref):
    out_ref[...] = (cross_ref[...] + near_ref[1].astype(F32)).astype(BF16)


def close_kernel(own_ref, near_ref, crossed_ref, out_ref):
    total = own_ref[...] + near_ref[0].astype(F32) + crossed_ref[...].astype(F32)
    out_ref[...] = total.astype(BF16)


def norm_kernel(place_ref, gain_ref, pair_ref, second_ref, out, held):
    width = pair_ref.shape[2]
    for s, shard in enumerate(by_distance(pair_ref, second_ref)):
        first = pl.multiple_of((place_ref[0] ^ s) * width, HD)
        held[:, pl.ds(first, width)] = shard[...].astype(F32)
    values = held[...]
    center = values - jnp.mean(values, axis=1, keepdims=True)
    spread = jnp.mean(center * center, axis=1, keepdims=True)
    out[...] = (center * lax.rsqrt(spread + 1e-05) * gain_ref[...]).astype(BF16)


def lift_kernel(chunks, place_ref, *refs):
    count = 2 * chunks
    shards, (up_hbm, down_hbm) = refs[:count], refs[count : count + 2]
    active_ref, far_ref, held, up, down, sems = refs[count + 2 :]
    hidden = active_ref.shape[1]
    share = far_ref.shape[2]
    rows = shards[0].shape[1]
    tile = up.shape[0] // (sems.shape[0] - 2)
    tiles = hidden // tile

    def fetch(k):
        part = pl.ds(k * tile, tile)
        return pltpu.make_async_copy(up_hbm.at[part], up.at[part], sems.at[k])

    def fetch_down(k):
        first = pl.multiple_of((place_ref[1] ^ (2 * k + 1)) * share, HD)
        return pltpu.make_async_copy(
            down_hbm.at[:, pl.ds(first, share)], down.at[k], sems.at[tiles + k]
        )

    for k in range(tiles):
        fetch(k).start()
    for k in range(2):
        fetch_down(k).start()
    for c in range(chunks):
        for t, shard in enumerate(by_distance(*shards[2 * c : 2 * c + 2])):
            first = pl.multiple_of(((place_ref[1] ^ t) * chunks + c) * rows, rows)
            held[pl.ds(first, rows), :] = shard[...]
    for k in range(tiles):
        fetch(k).wait()
        raised = lax.dot_general(
            held[...], up[k * tile : (k + 1) * tile, :], (((1,), (1,)), ((), ())),
            preferred_element_type=F32,
        )
        active_ref[:, k * tile : (k + 1) * tile] = (raised / (1.0 + jnp.exp(-raised))).astype(BF16)
    for k in range(2):
        fetch_down(k).wait()
        far_ref[k] = jnp.dot(active_ref[...], down[k], preferred_element_type=F32).astype(BF16)


def lower_kernel(place_ref, active_ref, down_hbm, cross_ref, own_ref, down, sems):
    share = own_ref.shape[1]

    def fetch(k):
        first = pl.multiple_of((place_ref[1] ^ (2 - 2 * k)) * share, HD)
        return pltpu.make_async_copy(down_hbm.at[:, pl.ds(first, share)], down.at[k], sems.at[k])

    for k in range(2):
        fetch(k).start()
    for k, out_ref in enumerate((cross_ref, own_ref)):
        fetch(k).wait()
        out_ref[...] = jnp.dot(active_ref[...], down[k], preferred_element_type=F32)


def turn_kernel(place_ref, cross_ref, near_ref, far_ref, close_ref):
    half = far_ref.shape[0]
    mine = place_ref[0] // 2
    for out_ref, side in ((far_ref, 1 - mine), (close_ref, mine)):
        here = pl.ds(pl.multiple_of(side * half, half), half)
        out_ref[...] = (cross_ref[here, :] + near_ref[1, here, :].astype(F32)).astype(BF16)


def split_kernel(side, place_ref, own_ref, near_ref, crossed_ref, *outs):
    rows = outs[0].shape[0]
    for s, out_ref in enumerate(outs):
        z = place_ref[0] ^ (2 * side + s)
        here = pl.ds(pl.multiple_of(z * rows, rows), rows)
        there = pl.ds(pl.multiple_of(z % 2 * rows, rows), rows)
        total = own_ref[here, :] + near_ref[0, here, :].astype(F32)
        out_ref[...] = (total + crossed_ref[there, :].astype(F32)).astype(BF16)


def mix_kernel(parts, place_ref, ids_ref, gates_ref, *refs):
    terms, out = refs[:parts], refs[parts]
    rows = out.shape[0]
    ids = ids_ref[pl.ds(pl.multiple_of(place_ref[0] * rows, rows), rows), :]
    total = jnp.zeros(out.shape, F32)
    for s in range(parts):
        gate = jnp.sum(
            jnp.where(ids == (place_ref[0] ^ s), gates_ref[...], 0.0), axis=1, keepdims=True
        )
        total = total + gate * terms[s][...].astype(F32)
    out[...] = total.astype(BF16)


def trade(array, axis, turn):
    count = lax.axis_size(axis)
    return lax.ppermute(array, axis, [(k, k ^ turn) for k in range(count)])


def every_row_body(
    queries, new_kv, kv_cache, lengths, out_proj, norm_gain, expert_ids, gate_weights, w_up, w_down
):
    gx_count = lax.axis_size("gx")
    ta_count = lax.axis_size("ta")
    chunks = 2
    block_rows = queries.shape[0]
    rows = block_rows // chunks
    width = out_proj.shape[1]
    model = norm_gain.shape[0]
    hidden_share = w_up.shape[2]
    share = model // ta_count
    all_rows = block_rows * gx_count
    place = jnp.stack([lax.axis_index("gx"), lax.axis_index("ta")]).astype(jnp.int32)
    shape = jax.ShapeDtypeStruct
    gain = norm_gain.reshape(1, model)
    attended = []
    for c in range(chunks):
        after = attended[-1] if attended else lengths
        attended.append(attend(queries, new_kv, kv_cache, lengths, c * rows, rows, after))
    first = [trade(part, "gx", 2) for part in attended]
    pairs = gather_pair(attended, first, attended[-1])
    second = [trade(pair, "gx", 1) for pair in pairs]
    pieces, nears, crossings, hidden, normed = [], [], [], [], []
    for c in range(chunks):
        pieces.append(
            local_call(
                project_kernel,
                [shape((rows, width), F32), shape((rows, width), F32), shape((2, rows, width), BF16)],
                [SMEM] + [VMEM] * 3,
                [pltpu.VMEM((ta_count, rows, width), F32)],
                name="project",
                after=pieces[-1][0] if pieces else None,
            )(place, pairs[c], second[c], out_proj)
        )
        nears.append(trade(pieces[c][2], "ta", 1))
    for c in range(chunks):
        crossings.append(
            local_call(
                cross_kernel,
                shape((rows, width), BF16),
                [VMEM] * 2,
                name="cross",
                after=crossings[-1] if crossings else None,
            )(pieces[c][1], nears[c])
        )
    crossed = [trade(part, "ta", 2) for part in crossings]
    for c in range(chunks):
        hidden.append(
            local_call(
                close_kernel,
                shape((rows, width), BF16),
                [VMEM] * 3,
                name="close",
                after=hidden[-1] if hidden else None,
            )(pieces[c][0], nears[c], crossed[c])
        )
    first = [trade(part, "gx", 2) for part in hidden]
    pairs = gather_pair(hidden, first, None)
    second = [trade(pair, "gx", 1) for pair in pairs]
    blocks, after = [], None
    for c in range(chunks):
        normed = local_call(
            norm_kernel,
            shape((rows, model), BF16),
            [SMEM] + [VMEM] * 3,
            [pltpu.VMEM((rows, model), F32)],
            name="norm",
            after=after,
        )(place, gain, pairs[c], second[c])
        (pair,) = gather_pair([normed], [trade(normed, "ta", 2)], None)
        blocks += [pair, trade(pair, "ta", 1)]
        after = pair
    tile = math.gcd(hidden_share, 7 * 64)
    down = w_down[0]
    active, far = local_call(
        functools.partial(lift_kernel, chunks),
        [shape((all_rows, hidden_share), BF16), shape((2, all_rows, share), BF16)],
        [SMEM] + [VMEM] * (2 * chunks) + [ANYWHERE] * 2,
        [
            pltpu.VMEM((all_rows, model), BF16),
            pltpu.VMEM((hidden_share, model), BF16),
            pltpu.VMEM((2, hidden_share, share), BF16),
            pltpu.SemaphoreType.DMA((hidden_share // tile + 2,)),
        ],
        vmem=48,
        name="lift",
    )(place, *blocks, jnp.swapaxes(w_up[0], 0, 1), down)
    near = trade(far, "ta", 1)
    cross, own = local_call(
        lower_kernel,
        [shape((all_rows, share), F32)] * 2,
        [SMEM, VMEM, ANYWHERE],
        [pltpu.VMEM((2, hidden_share, share), BF16), pltpu.SemaphoreType.DMA((2,))],
        vmem=48,
        name="lower",
    )(place, active, down)
    half = all_rows // 2
    far_side, close_side = local_call(
        turn_kernel,
        [shape((half, share), BF16)] * 2,
        [SMEM] + [VMEM] * 2,
        name="turn",
    )(place, cross, near)
    terms = {}
    for side, crossing in ((1, far_side), (0, close_side)):
        crossed = trade(crossing, "ta", 2)
        terms[2 * side], terms[2 * side + 1] = local_call(
            functools.partial(split_kernel, side),
            [shape((block_rows, share), BF16)] * 2,
            [SMEM] + [VMEM] * 3,
            name="split",
        )(place, own, near, crossed)
    terms = [terms[s] if s == 0 else trade(terms[s], "gx", s) for s in range(gx_count)]
    return local_call(
        functools.partial(mix_kernel, gx_count),
        shape((block_rows, share), BF16),
        [SMEM] + [VMEM] * (gx_count + 2),
        name="mix",
    )(place, expert_ids, gate_weights, *terms)


def route_tables(expert_ids, expert_count, block_rows, capacity):
    blocks = expert_ids.shape[0] // block_rows
    expert_range = jnp.arange(expert_count, dtype=jnp.int32)
    matches = (expert_ids[:, :, None] == expert_range[None, None, :]).astype(jnp.int32)
    routed = jnp.sum(matches, axis=1).reshape(blocks, block_rows, expert_count)
    position = jnp.cumsum(routed, axis=1) - routed
    slot_range = jnp.arange(capacity, dtype=jnp.int32)
    slot_hits = routed[:, :, :, None] * (
        position[:, :, :, None] == slot_range[None, None, None, :]
    ).astype(jnp.int32)
    row_range = jnp.arange(block_rows, dtype=jnp.int32)
    block_start = (jnp.arange(blocks, dtype=jnp.int32) * block_rows)[:, None, None]
    source_row = jnp.sum(slot_hits * row_range[None, :, None, None], axis=1) + block_start
    filled = jnp.sum(slot_hits, axis=1)
    source_row = jnp.transpose(source_row, (1, 0, 2)).reshape(expert_count, blocks * capacity)
    filled = jnp.transpose(filled, (1, 0, 2)).reshape(expert_count, blocks * capacity)
    pick_slot = jnp.sum(matches * position.reshape(blocks * block_rows, 1, expert_count), axis=2)
    return (source_row, filled, pick_slot)


def layer_norm(hidden, norm_gain):
    values = hidden.astype(jnp.float32)
    center = values - jnp.mean(values, axis=1, keepdims=True)
    spread = jnp.mean(center * center, axis=1, keepdims=True)
    return (center * lax.rsqrt(spread + 1e-05) * norm_gain).astype(jnp.bfloat16)


def body(
    queries, new_kv, kv_cache, lengths, out_proj, norm_gain, expert_ids, gate_weights, w_up, w_down
):
    gx_count = lax.axis_size("gx")
    ta_count = lax.axis_size("ta")
    block_rows = queries.shape[0]
    top_count = expert_ids.shape[1]
    capacity = min(block_rows, 2 * block_rows * top_count // gx_count)
    slot_count = gx_count * capacity
    model_width = norm_gain.shape[0]
    width_share = model_width // ta_count
    if gx_count == top_count and ta_count == gx_count == 4:
        return every_row_body(
            queries, new_kv, kv_cache, lengths, out_proj, norm_gain, expert_ids, gate_weights,
            w_up, w_down,
        )
    attended = attend(queries, new_kv, kv_cache, lengths, 0, block_rows, lengths)
    projected = jnp.dot(
        lax.all_gather(attended, "gx", axis=0, tiled=True),
        out_proj,
        preferred_element_type=jnp.float32,
    ).astype(jnp.bfloat16)
    source_row, filled, pick_slot = route_tables(expert_ids, gx_count, block_rows, capacity)
    live_slots = (filled > 0)[:, :, None]
    widened = lax.optimization_barrier(projected).astype(jnp.float32)
    hidden_share = lax.psum_scatter(
        widened.astype(jnp.bfloat16), "ta", scatter_dimension=1, tiled=True
    )
    outgoing = jnp.where(live_slots, hidden_share[source_row], jnp.zeros((), jnp.bfloat16))[
        :, :, None, :
    ]
    arrived = lax.all_to_all(outgoing, "gx", split_axis=0, concat_axis=2, tiled=True)
    gathered = lax.all_gather(arrived, "ta", axis=3, tiled=True)
    hidden = gathered.reshape(slot_count, model_width)
    normed = layer_norm(hidden, norm_gain)
    raised = jnp.dot(normed, w_up[0], preferred_element_type=jnp.float32)
    active = jax.nn.silu(raised).astype(jnp.bfloat16)
    terms = jnp.dot(active, w_down[0], preferred_element_type=jnp.float32)
    mine = lax.psum_scatter(terms, "ta", scatter_dimension=1, tiled=True)
    result = mine.astype(jnp.bfloat16).reshape(gx_count, capacity, width_share)
    returned = lax.all_to_all(result, "gx", split_axis=0, concat_axis=0, tiled=True)
    first_row = lax.axis_index("gx") * block_rows
    local_ids = lax.dynamic_slice_in_dim(expert_ids, first_row, block_rows, 0)
    local_slot = lax.dynamic_slice_in_dim(pick_slot, first_row, block_rows, 0)
    flat_rows = returned.reshape(gx_count * capacity, width_share)
    picked = flat_rows[local_ids * capacity + local_slot]
    return jnp.sum(picked.astype(jnp.float32) * gate_weights[:, :, None], axis=1).astype(
        jnp.bfloat16
    )


def solution(mesh):
    return jax.shard_map(
        body,
        mesh=mesh,
        in_specs=(
            P(("groups", "gx"), "ta"),
            P(None, ("groups", "gx"), "ta"),
            P(None, ("groups", "gx"), None, "ta"),
            P(("groups", "gx")),
            P("ta", "gx"),
            P(),
            P("groups", None),
            P(("groups", "gx"), None),
            P("gx", None, "ta"),
            P("gx", "ta", None),
        ),
        out_specs=P(("groups", "gx"), "ta"),
        check_vma=False,
    )
```

```python
import functools
import math

import jax
import jax.numpy as jnp
from jax import lax
from jax.experimental import pallas as pl
from jax.experimental.pallas import tpu as pltpu
from jax.sharding import PartitionSpec as P

HD = 128
MIB = 1 << 20
VMEM = pl.BlockSpec(memory_space=pltpu.VMEM)
SMEM = pl.BlockSpec(memory_space=pltpu.SMEM)
F32 = jnp.float32
BF16 = jnp.bfloat16


ANYWHERE = pl.BlockSpec(memory_space=pl.ANY)


def local_call(kernel, out_shape, in_specs, scratch=(), vmem=12, name=None, after=None):
    several = isinstance(out_shape, (tuple, list))
    if after is not None:
        count, inner = len(in_specs), kernel
        in_specs = [*in_specs, ANYWHERE]
        kernel = lambda *refs: inner(*refs[:count], *refs[count + 1 :])
    call = pl.pallas_call(
        kernel,
        out_shape=out_shape,
        in_specs=in_specs,
        out_specs=[VMEM] * len(out_shape) if several else VMEM,
        scratch_shapes=list(scratch),
        compiler_params=pltpu.CompilerParams(vmem_limit_bytes=vmem * MIB),
        cost_estimate=pl.CostEstimate(flops=1024, bytes_accessed=1024, transcendentals=0),
        name=name,
    )
    return call if after is None else lambda *args: call(*args, after)


def attend_kernel(
    kv_heads, group, slots, batch, begin,
    lengths_ref, q_ref, fresh_ref, cache_ref, after_ref, out_ref, again_ref,
    keys, values, q_rows, scores, own_scores, probs, own_probs, mixed, sems,
):
    rows = out_ref.shape[0]
    context = keys.shape[1]
    width = kv_heads * HD
    heads = kv_heads * group
    steps = rows // batch
    scale = 1.0 / math.sqrt(HD)

    def fetch(step, kind):
        buffer = (keys, values)[kind]
        return pltpu.make_async_copy(
            cache_ref.at[kind, pl.ds(begin + step * batch, batch)],
            buffer.at[pl.ds(step * batch, batch)],
            sems.at[kind, step],
        )

    for step in range(steps):
        for kind in range(2):
            fetch(step, kind).start()
    q_rows[...] = jnp.zeros_like(q_rows)
    for head in range(heads):
        q_rows[head // group, pl.ds(head, rows, stride=slots), :] = q_ref[
            begin : begin + rows, head * HD : (head + 1) * HD
        ].astype(F32)
    place = lax.broadcasted_iota(jnp.int32, (slots, context), 1)
    for step in range(steps):
        fetch(step, 0).wait()
        for k in range(batch):
            row = step * batch + k
            mine = jnp.concatenate(
                [q_rows[g, row * slots : (row + 1) * slots, :] for g in range(kv_heads)], axis=1
            )
            cached = lax.dot_general(
                mine.astype(BF16), keys[row], (((1,), (1,)), ((), ())),
                preferred_element_type=F32,
            )
            here = slice(k * slots, (k + 1) * slots)
            scores[here, :] = jnp.where(place < lengths_ref[begin + row], cached * scale, -jnp.inf)
            fresh_key = fresh_ref[0, begin + row : begin + row + 1, :].astype(F32)
            own_scores[here, :] = jnp.broadcast_to(
                jnp.sum(mine * fresh_key, axis=1, keepdims=True) * scale, (slots, HD)
            )
        cached = scores[...]
        own = own_scores[:, :1]
        largest = jnp.maximum(jnp.max(cached, axis=1, keepdims=True), own)
        lifted = jnp.exp(cached - largest)
        own_lifted = jnp.exp(own - largest)
        total = jnp.sum(lifted, axis=1, keepdims=True) + own_lifted
        probs[...] = (lifted / total).astype(BF16)
        own_probs[...] = jnp.broadcast_to(
            (own_lifted / total).astype(BF16).astype(F32), own_probs.shape
        )
        fetch(step, 1).wait()
        for k in range(batch):
            row = step * batch + k
            here = slice(k * slots, (k + 1) * slots)
            weighted = jnp.dot(probs[here, :], values[row], preferred_element_type=F32)
            fresh_value = fresh_ref[1, begin + row : begin + row + 1, :].astype(F32)
            total = weighted + own_probs[here, :1] * fresh_value
            for g in range(kv_heads):
                mixed[g, here, :] = total[:, g * HD : (g + 1) * HD]
        for head in range(heads):
            there = (slice(step * batch, (step + 1) * batch), slice(head * HD, (head + 1) * HD))
            done = mixed[head // group, pl.ds(head, batch, stride=slots), :].astype(BF16)
            out_ref[there] = done
            again_ref[there] = done


def attend(queries, new_kv, kv_cache, lengths, begin, rows, after):
    features = queries.shape[1]
    context, width = kv_cache.shape[2:]
    kv_heads = width // HD
    heads = features // HD
    slots = -(-heads // 8) * 8
    batch = 16
    return pl.pallas_call(
        functools.partial(attend_kernel, kv_heads, heads // kv_heads, slots, batch, begin),
        out_shape=[jax.ShapeDtypeStruct((rows, features), BF16)] * 2,
        in_specs=[SMEM, VMEM, VMEM, ANYWHERE, ANYWHERE],
        out_specs=[VMEM] * 2,
        scratch_shapes=[
            pltpu.VMEM((rows, context, width), BF16),
            pltpu.VMEM((rows, context, width), BF16),
            pltpu.VMEM((kv_heads, rows * slots, HD), F32),
            pltpu.VMEM((batch * slots, context), F32),
            pltpu.VMEM((batch * slots, HD), F32),
            pltpu.VMEM((batch * slots, context), BF16),
            pltpu.VMEM((batch * slots, HD), F32),
            pltpu.VMEM((kv_heads, batch * slots, HD), F32),
            pltpu.SemaphoreType.DMA((2, rows // batch)),
        ],
        compiler_params=pltpu.CompilerParams(vmem_limit_bytes=58 * MIB),
        cost_estimate=pl.CostEstimate(flops=1024, bytes_accessed=1024, transcendentals=0),
        name="attend",
    )(lengths, queries, new_kv, kv_cache, after)


def pair_kernel(own_ref, other_ref, out_ref):
    out_ref[0] = own_ref[...]
    out_ref[1] = other_ref[...]


def gate_kernel(place_ref, ids_ref, gates_ref, gate_ref):
    parts, rows, lanes = gate_ref.shape
    ids = ids_ref[pl.ds(pl.multiple_of(place_ref[0] * rows, rows), rows), :]
    for s in range(parts):
        gate = jnp.sum(
            jnp.where(ids == (place_ref[0] ^ s), gates_ref[...], 0.0), axis=1, keepdims=True
        )
        gate_ref[s] = jnp.broadcast_to(gate, (rows, lanes))


def project_kernel(parts, place_ref, *refs):
    shards, weight_ref = refs[:parts], refs[parts]
    outs, held = refs[parts + 1 : -1], refs[-1]
    rows = shards[0].shape[0]
    turn = place_ref[0] ^ place_ref[1]
    block = jnp.concatenate([shard[...] for shard in shards], axis=0)
    pieces = jnp.dot(block, weight_ref[...], preferred_element_type=F32).astype(BF16)
    for s in range(parts):
        held[turn ^ s] = pieces[s * rows : (s + 1) * rows, :]
    for t in range(parts):
        outs[t][...] = held[t]


def add_kernel(*refs):
    terms, out = refs[:-1], refs[-1]
    total = terms[0][...].astype(F32)
    for term in terms[1:]:
        total = total + term[...].astype(F32)
    out[...] = total.astype(BF16)


def norm_kernel(parts, place_ref, gain_ref, *refs):
    shards, out, held = refs[:parts], refs[parts], refs[parts + 1]
    width = shards[0].shape[1]
    for s in range(parts):
        first = pl.multiple_of((place_ref[0] ^ s) * width, HD)
        held[:, pl.ds(first, width)] = shards[s][...].astype(F32)
    values = held[...]
    center = values - jnp.mean(values, axis=1, keepdims=True)
    spread = jnp.mean(center * center, axis=1, keepdims=True)
    out[...] = (center * lax.rsqrt(spread + 1e-05) * gain_ref[...]).astype(BF16)


def by_distance(pair_ref, second_ref):
    return pair_ref.at[0], second_ref.at[0], pair_ref.at[1], second_ref.at[1]


def lift_kernel(chunks, tile, place_ref, *refs):
    count = 2 * chunks
    shards, (up_hbm, down_hbm) = refs[:count], refs[count : count + 2]
    active_ref, far_ref, rest_ref, held, up, down, up_sems, down_sems = refs[count + 2 :]
    hidden = active_ref.shape[1]
    share = far_ref.shape[2]
    rows = shards[0].shape[1]

    def fetch_up(first):
        part = pl.ds(first, tile)
        return pltpu.make_async_copy(
            up_hbm.at[part], up.at[part], up_sems.at[first // tile]
        )

    def fetch_down(k, turn, into):
        first = pl.multiple_of((place_ref[1] ^ turn) * share, HD)
        return pltpu.make_async_copy(
            down_hbm.at[:, pl.ds(first, share)], into, down_sems.at[k]
        )

    ups = [fetch_up(first) for first in range(0, hidden, tile)]
    downs = [fetch_down(k, 2 * k + 1, down.at[k]) for k in range(2)]
    rests = [fetch_down(2 + k, 2 - 2 * k, rest_ref.at[k]) for k in range(2)]
    for copy in ups + downs + rests:
        copy.start()
    for c in range(chunks):
        for t, shard in enumerate(by_distance(*shards[2 * c : 2 * c + 2])):
            first = pl.multiple_of(((place_ref[1] ^ t) * chunks + c) * rows, rows)
            held[pl.ds(first, rows), :] = shard[...]
    arrived = 0
    for first in range(0, hidden, 2 * HD):
        last = min(first + 2 * HD, hidden)
        while arrived < last:
            ups[arrived // tile].wait()
            arrived += tile
        raised = lax.dot_general(
            up[first:last, :], held[...], (((1,), (1,)), ((), ())), preferred_element_type=F32
        )
        active_ref[:, first:last] = (raised / (1.0 + jnp.exp(-raised))).T.astype(BF16)
    for k in range(2):
        downs[k].wait()
        far_ref[k] = jnp.dot(active_ref[...], down[k], preferred_element_type=F32).astype(BF16)
    for copy in rests:
        copy.wait()


def lower_kernel(active_ref, rest_ref, cross_ref, own_ref):
    for k, out_ref in enumerate((cross_ref, own_ref)):
        out_ref[...] = jnp.dot(active_ref[...], rest_ref[k], preferred_element_type=F32)


def turn_kernel(place_ref, cross_ref, near_ref, far_ref, close_ref):
    half = far_ref.shape[0]
    mine = place_ref[0] // 2
    for out_ref, side in ((far_ref, 1 - mine), (close_ref, mine)):
        here = pl.ds(pl.multiple_of(side * half, half), half)
        out_ref[...] = (cross_ref[here, :] + near_ref[1, here, :].astype(F32)).astype(BF16)


def split_kernel(side, place_ref, own_ref, near_ref, crossed_ref, *outs):
    rows = outs[0].shape[0]
    for s, out_ref in enumerate(outs):
        z = place_ref[0] ^ (2 * side + s)
        here = pl.ds(pl.multiple_of(z * rows, rows), rows)
        there = pl.ds(pl.multiple_of(z % 2 * rows, rows), rows)
        total = own_ref[here, :] + near_ref[0, here, :].astype(F32)
        out_ref[...] = (total + crossed_ref[there, :].astype(F32)).astype(BF16)


def mix_kernel(parts, gate_ref, *refs):
    terms, out = refs[:parts], refs[parts]
    lanes = gate_ref.shape[2]
    for first in range(0, out.shape[1], lanes):
        part = slice(first, first + lanes)
        total = gate_ref[0] * terms[0][:, part].astype(F32)
        for s in range(1, parts):
            total = total + gate_ref[s] * terms[s][:, part].astype(F32)
        out[:, part] = total.astype(BF16)


def trade(array, axis, turn):
    count = lax.axis_size(axis)
    return lax.ppermute(array, axis, [(k, k ^ turn) for k in range(count)])


def every_row_body(
    queries, new_kv, kv_cache, lengths, out_proj, norm_gain, expert_ids, gate_weights, w_up, w_down
):
    gx_count = lax.axis_size("gx")
    ta_count = lax.axis_size("ta")
    chunks = 2
    block_rows = queries.shape[0]
    rows = block_rows // chunks
    width = out_proj.shape[1]
    model = norm_gain.shape[0]
    hidden_share = w_up.shape[2]
    share = model // ta_count
    all_rows = block_rows * gx_count
    place = jnp.stack([lax.axis_index("gx"), lax.axis_index("ta")]).astype(jnp.int32)
    shape = jax.ShapeDtypeStruct
    gain = norm_gain.reshape(1, model)
    attended = []
    for c in range(chunks):
        after = attended[-1][1] if attended else lengths
        attended.append(attend(queries, new_kv, kv_cache, lengths, c * rows, rows, after))
    order = [s for s in range(gx_count - 1, 0, -1)]

    def spread(array, axis):
        parts = {0: array, **{s: trade(array, axis, s) for s in order}}
        return [parts[s] for s in range(len(parts))]

    shards = [[kept] + spread(sent, "gx")[1:] for sent, kept in attended]
    gates = local_call(
        gate_kernel,
        shape((gx_count, block_rows, HD), F32),
        [SMEM, VMEM, VMEM],
        name="gates",
        after=attended[-1][1],
    )(place, expert_ids, gate_weights)
    pieces, hidden = [], []
    for c in range(chunks):
        pieces.append(
            local_call(
                functools.partial(project_kernel, gx_count),
                [shape((rows, width), BF16)] * ta_count,
                [SMEM] + [VMEM] * (gx_count + 1),
                [pltpu.VMEM((ta_count, rows, width), BF16)],
                name="project",
                after=pieces[-1][0] if pieces else gates,
            )(place, *shards[c], out_proj)
        )
    for c in range(chunks):
        parts = [pieces[c][0]] + [trade(pieces[c][t], "ta", t) for t in range(1, ta_count)]
        hidden.append(
            local_call(
                add_kernel,
                shape((rows, width), BF16),
                [VMEM] * ta_count,
                name="add",
                after=hidden[-1] if hidden else pieces[-1][0],
            )(*parts)
        )
    shards = [spread(part, "gx") for part in hidden]
    normed, pairs = [], []
    for c in range(chunks):
        normed.append(
            local_call(
                functools.partial(norm_kernel, gx_count),
                shape((rows, model), BF16),
                [SMEM] + [VMEM] * (gx_count + 1),
                [pltpu.VMEM((rows, model), F32)],
                name="norm",
                after=normed[-1] if normed else hidden[-1],
            )(place, gain, *shards[c])
        )
    for c in range(chunks):
        pairs.append(
            local_call(
                pair_kernel,
                shape((2, rows, model), BF16),
                [VMEM] * 2,
                name="pair",
                after=pairs[-1] if pairs else normed[-1],
            )(normed[c], trade(normed[c], "ta", 2))
        )
    blocks = [block for pair in pairs for block in (pair, trade(pair, "ta", 1))]
    tile = math.gcd(hidden_share, 3 * 64)
    active, far, rest = local_call(
        functools.partial(lift_kernel, chunks, tile),
        [
            shape((all_rows, hidden_share), BF16),
            shape((2, all_rows, share), BF16),
            shape((2, hidden_share, share), BF16),
        ],
        [SMEM] + [VMEM] * (2 * chunks) + [ANYWHERE] * 2,
        [
            pltpu.VMEM((all_rows, model), BF16),
            pltpu.VMEM((hidden_share, model), BF16),
            pltpu.VMEM((2, hidden_share, share), BF16),
            pltpu.SemaphoreType.DMA((hidden_share // tile,)),
            pltpu.SemaphoreType.DMA((4,)),
        ],
        vmem=40,
        name="lift",
    )(place, *blocks, jnp.swapaxes(w_up[0], 0, 1), w_down[0])
    near = trade(far, "ta", 1)
    cross, own = local_call(
        lower_kernel,
        [shape((all_rows, share), F32)] * 2,
        [VMEM, VMEM],
        vmem=16,
        name="lower",
    )(active, rest)
    half = all_rows // 2
    far_side, close_side = local_call(
        turn_kernel,
        [shape((half, share), BF16)] * 2,
        [SMEM] + [VMEM] * 2,
        name="turn",
    )(place, cross, near)
    terms = {}
    for side, crossing in ((1, far_side), (0, close_side)):
        crossed = trade(crossing, "ta", 2)
        terms[2 * side], terms[2 * side + 1] = local_call(
            functools.partial(split_kernel, side),
            [shape((block_rows, share), BF16)] * 2,
            [SMEM] + [VMEM] * 3,
            name="split",
        )(place, own, near, crossed)
    terms = [terms[s] if s == 0 else trade(terms[s], "gx", s) for s in range(gx_count)]
    return local_call(
        functools.partial(mix_kernel, gx_count),
        shape((block_rows, share), BF16),
        [VMEM] * (gx_count + 1),
        name="mix",
    )(gates, *terms)


def route_tables(expert_ids, expert_count, block_rows, capacity):
    blocks = expert_ids.shape[0] // block_rows
    expert_range = jnp.arange(expert_count, dtype=jnp.int32)
    matches = (expert_ids[:, :, None] == expert_range[None, None, :]).astype(jnp.int32)
    routed = jnp.sum(matches, axis=1).reshape(blocks, block_rows, expert_count)
    position = jnp.cumsum(routed, axis=1) - routed
    slot_range = jnp.arange(capacity, dtype=jnp.int32)
    slot_hits = routed[:, :, :, None] * (
        position[:, :, :, None] == slot_range[None, None, None, :]
    ).astype(jnp.int32)
    row_range = jnp.arange(block_rows, dtype=jnp.int32)
    block_start = (jnp.arange(blocks, dtype=jnp.int32) * block_rows)[:, None, None]
    source_row = jnp.sum(slot_hits * row_range[None, :, None, None], axis=1) + block_start
    filled = jnp.sum(slot_hits, axis=1)
    source_row = jnp.transpose(source_row, (1, 0, 2)).reshape(expert_count, blocks * capacity)
    filled = jnp.transpose(filled, (1, 0, 2)).reshape(expert_count, blocks * capacity)
    pick_slot = jnp.sum(matches * position.reshape(blocks * block_rows, 1, expert_count), axis=2)
    return (source_row, filled, pick_slot)


def layer_norm(hidden, norm_gain):
    values = hidden.astype(jnp.float32)
    center = values - jnp.mean(values, axis=1, keepdims=True)
    spread = jnp.mean(center * center, axis=1, keepdims=True)
    return (center * lax.rsqrt(spread + 1e-05) * norm_gain).astype(jnp.bfloat16)


def body(
    queries, new_kv, kv_cache, lengths, out_proj, norm_gain, expert_ids, gate_weights, w_up, w_down
):
    gx_count = lax.axis_size("gx")
    ta_count = lax.axis_size("ta")
    block_rows = queries.shape[0]
    top_count = expert_ids.shape[1]
    capacity = min(block_rows, 2 * block_rows * top_count // gx_count)
    slot_count = gx_count * capacity
    model_width = norm_gain.shape[0]
    width_share = model_width // ta_count
    if gx_count == top_count and ta_count == gx_count == 4:
        return every_row_body(
            queries, new_kv, kv_cache, lengths, out_proj, norm_gain, expert_ids, gate_weights,
            w_up, w_down,
        )
    attended, _ = attend(queries, new_kv, kv_cache, lengths, 0, block_rows, lengths)
    projected = jnp.dot(
        lax.all_gather(attended, "gx", axis=0, tiled=True),
        out_proj,
        preferred_element_type=jnp.float32,
    ).astype(jnp.bfloat16)
    source_row, filled, pick_slot = route_tables(expert_ids, gx_count, block_rows, capacity)
    live_slots = (filled > 0)[:, :, None]
    widened = lax.optimization_barrier(projected).astype(jnp.float32)
    hidden_share = lax.psum_scatter(
        widened.astype(jnp.bfloat16), "ta", scatter_dimension=1, tiled=True
    )
    outgoing = jnp.where(live_slots, hidden_share[source_row], jnp.zeros((), jnp.bfloat16))[
        :, :, None, :
    ]
    arrived = lax.all_to_all(outgoing, "gx", split_axis=0, concat_axis=2, tiled=True)
    gathered = lax.all_gather(arrived, "ta", axis=3, tiled=True)
    hidden = gathered.reshape(slot_count, model_width)
    normed = layer_norm(hidden, norm_gain)
    raised = jnp.dot(normed, w_up[0], preferred_element_type=jnp.float32)
    active = jax.nn.silu(raised).astype(jnp.bfloat16)
    terms = jnp.dot(active, w_down[0], preferred_element_type=jnp.float32)
    mine = lax.psum_scatter(terms, "ta", scatter_dimension=1, tiled=True)
    result = mine.astype(jnp.bfloat16).reshape(gx_count, capacity, width_share)
    returned = lax.all_to_all(result, "gx", split_axis=0, concat_axis=0, tiled=True)
    first_row = lax.axis_index("gx") * block_rows
    local_ids = lax.dynamic_slice_in_dim(expert_ids, first_row, block_rows, 0)
    local_slot = lax.dynamic_slice_in_dim(pick_slot, first_row, block_rows, 0)
    flat_rows = returned.reshape(gx_count * capacity, width_share)
    picked = flat_rows[local_ids * capacity + local_slot]
    return jnp.sum(picked.astype(jnp.float32) * gate_weights[:, :, None], axis=1).astype(
        jnp.bfloat16
    )


def solution(mesh):
    return jax.shard_map(
        body,
        mesh=mesh,
        in_specs=(
            P(("groups", "gx"), "ta"),
            P(None, ("groups", "gx"), "ta"),
            P(None, ("groups", "gx"), None, "ta"),
            P(("groups", "gx")),
            P("ta", "gx"),
            P(),
            P("groups", None),
            P(("groups", "gx"), None),
            P("gx", None, "ta"),
            P("gx", "ta", None),
        ),
        out_specs=P(("groups", "gx"), "ta"),
        check_vma=False,
    )
```

```python
import functools
import math

import jax
import jax.numpy as jnp
from jax import lax
from jax.experimental import pallas as pl
from jax.experimental.pallas import tpu as pltpu
from jax.sharding import PartitionSpec as P

HD = 128
MIB = 1 << 20
MIX_COST = 1 << 22
VMEM = pl.BlockSpec(memory_space=pltpu.VMEM)
SMEM = pl.BlockSpec(memory_space=pltpu.SMEM)
F32 = jnp.float32
BF16 = jnp.bfloat16


ANYWHERE = pl.BlockSpec(memory_space=pl.ANY)


def local_call(kernel, out_shape, in_specs, scratch=(), vmem=8, name=None, after=None, cost=1024):
    several = isinstance(out_shape, (tuple, list))
    if after is not None:
        count, inner = len(in_specs), kernel
        in_specs = [*in_specs, ANYWHERE]
        kernel = lambda *refs: inner(*refs[:count], *refs[count + 1 :])
    call = pl.pallas_call(
        kernel,
        out_shape=out_shape,
        in_specs=in_specs,
        out_specs=[VMEM] * len(out_shape) if several else VMEM,
        scratch_shapes=list(scratch),
        compiler_params=pltpu.CompilerParams(vmem_limit_bytes=vmem * MIB),
        cost_estimate=pl.CostEstimate(flops=1024, bytes_accessed=cost, transcendentals=0),
        name=name,
    )
    return call if after is None else lambda *args: call(*args, after)


def attend_kernel(
    kv_heads, group, slots, batch, begin,
    lengths_hbm, q_hbm, fresh_hbm, cache_ref, after_ref, out_ref, again_ref,
    lengths_ref, q_ref, fresh_ref, keys, values, q_rows, scores, own_scores, probs, own_probs,
    mixed, sems, small_sems,
):
    rows = out_ref.shape[0]
    context = keys.shape[1]
    width = kv_heads * HD
    heads = kv_heads * group
    steps = rows // batch
    scale = 1.0 / math.sqrt(HD)

    def fetch(step, kind):
        buffer = (keys, values)[kind]
        return pltpu.make_async_copy(
            cache_ref.at[kind, pl.ds(begin + step * batch, batch)],
            buffer.at[pl.ds(step * batch, batch)],
            sems.at[kind, step],
        )

    part = pl.ds(begin, rows)
    small = [
        pltpu.make_async_copy(q_hbm.at[part], q_ref, small_sems.at[0]),
        pltpu.make_async_copy(lengths_hbm, lengths_ref, small_sems.at[1]),
        pltpu.make_async_copy(fresh_hbm.at[:, part], fresh_ref, small_sems.at[2]),
    ]
    for copy in small:
        copy.start()
    for step in range(steps):
        for kind in range(2):
            fetch(step, kind).start()
    q_rows[...] = jnp.zeros_like(q_rows)
    for copy in small:
        copy.wait()
    for head in range(heads):
        q_rows[head // group, pl.ds(head, rows, stride=slots), :] = q_ref[
            :, head * HD : (head + 1) * HD
        ].astype(F32)
    place = lax.broadcasted_iota(jnp.int32, (slots, context), 1)
    for step in range(steps):
        fetch(step, 0).wait()
        for k in range(batch):
            row = step * batch + k
            mine = jnp.concatenate(
                [q_rows[g, row * slots : (row + 1) * slots, :] for g in range(kv_heads)], axis=1
            )
            cached = lax.dot_general(
                mine.astype(BF16), keys[row], (((1,), (1,)), ((), ())),
                preferred_element_type=F32,
            )
            here = slice(k * slots, (k + 1) * slots)
            scores[here, :] = jnp.where(place < lengths_ref[begin + row], cached * scale, -jnp.inf)
            fresh_key = fresh_ref[0, row : row + 1, :].astype(F32)
            own_scores[here, :] = jnp.broadcast_to(
                jnp.sum(mine * fresh_key, axis=1, keepdims=True) * scale, (slots, HD)
            )
        cached = scores[...]
        own = own_scores[:, :1]
        largest = jnp.maximum(jnp.max(cached, axis=1, keepdims=True), own)
        lifted = jnp.exp(cached - largest)
        own_lifted = jnp.exp(own - largest)
        total = jnp.sum(lifted, axis=1, keepdims=True) + own_lifted
        probs[...] = (lifted / total).astype(BF16)
        own_probs[...] = jnp.broadcast_to(
            (own_lifted / total).astype(BF16).astype(F32), own_probs.shape
        )
        fetch(step, 1).wait()
        for k in range(batch):
            row = step * batch + k
            here = slice(k * slots, (k + 1) * slots)
            weighted = jnp.dot(probs[here, :], values[row], preferred_element_type=F32)
            fresh_value = fresh_ref[1, row : row + 1, :].astype(F32)
            total = weighted + own_probs[here, :1] * fresh_value
            for g in range(kv_heads):
                mixed[g, here, :] = total[:, g * HD : (g + 1) * HD]
        for head in range(heads):
            there = (slice(step * batch, (step + 1) * batch), slice(head * HD, (head + 1) * HD))
            done = mixed[head // group, pl.ds(head, batch, stride=slots), :].astype(BF16)
            out_ref[there] = done
            again_ref[there] = done


def attend(queries, new_kv, kv_cache, lengths, begin, rows, after):
    features = queries.shape[1]
    context, width = kv_cache.shape[2:]
    kv_heads = width // HD
    heads = features // HD
    slots = -(-heads // 8) * 8
    batch = 16
    return pl.pallas_call(
        functools.partial(attend_kernel, kv_heads, heads // kv_heads, slots, batch, begin),
        out_shape=[jax.ShapeDtypeStruct((rows, features), BF16)] * 2,
        in_specs=[ANYWHERE] * 5,
        out_specs=[VMEM] * 2,
        scratch_shapes=[
            pltpu.SMEM(lengths.shape, jnp.int32),
            pltpu.VMEM((rows, features), BF16),
            pltpu.VMEM((2, rows, width), BF16),
            pltpu.VMEM((rows, context, width), BF16),
            pltpu.VMEM((rows, context, width), BF16),
            pltpu.VMEM((kv_heads, rows * slots, HD), F32),
            pltpu.VMEM((batch * slots, context), F32),
            pltpu.VMEM((batch * slots, HD), F32),
            pltpu.VMEM((batch * slots, context), BF16),
            pltpu.VMEM((batch * slots, HD), F32),
            pltpu.VMEM((kv_heads, batch * slots, HD), F32),
            pltpu.SemaphoreType.DMA((2, rows // batch)),
            pltpu.SemaphoreType.DMA((3,)),
        ],
        compiler_params=pltpu.CompilerParams(vmem_limit_bytes=58 * MIB),
        cost_estimate=pl.CostEstimate(flops=1024, bytes_accessed=1024, transcendentals=0),
        name="attend",
    )(lengths, queries, new_kv, kv_cache, after)


def pair_kernel(own_ref, other_ref, out_ref):
    out_ref[0] = own_ref[...]
    out_ref[1] = other_ref[...]


def gate_kernel(place_ref, ids_ref, gates_ref, gate_ref):
    parts, rows, lanes = gate_ref.shape
    ids = ids_ref[pl.ds(pl.multiple_of(place_ref[0] * rows, rows), rows), :]
    for s in range(parts):
        gate = jnp.sum(
            jnp.where(ids == (place_ref[0] ^ s), gates_ref[...], 0.0), axis=1, keepdims=True
        )
        gate_ref[s] = jnp.broadcast_to(gate, (rows, lanes))


def project_kernel(parts, place_ref, *refs):
    shards, weight_ref = refs[:parts], refs[parts]
    outs, held = refs[parts + 1 : -1], refs[-1]
    rows = shards[0].shape[0]
    turn = place_ref[0] ^ place_ref[1]
    block = jnp.concatenate([shard[...] for shard in shards], axis=0)
    pieces = jnp.dot(block, weight_ref[...], preferred_element_type=F32).astype(BF16)
    for s in range(parts):
        held[turn ^ s] = pieces[s * rows : (s + 1) * rows, :]
    for t in range(parts):
        outs[t][...] = held[t]


def add_kernel(*refs):
    terms, out = refs[:-1], refs[-1]
    total = terms[0][...].astype(F32)
    for term in terms[1:]:
        total = total + term[...].astype(F32)
    out[...] = total.astype(BF16)


def norm_kernel(parts, place_ref, gain_ref, *refs):
    shards, out, held = refs[:parts], refs[parts], refs[parts + 1]
    width = shards[0].shape[1]
    for s in range(parts):
        first = pl.multiple_of((place_ref[0] ^ s) * width, HD)
        held[:, pl.ds(first, width)] = shards[s][...].astype(F32)
    values = held[...]
    center = values - jnp.mean(values, axis=1, keepdims=True)
    spread = jnp.mean(center * center, axis=1, keepdims=True)
    out[...] = (center * lax.rsqrt(spread + 1e-05) * gain_ref[...]).astype(BF16)


def by_distance(pair_ref, second_ref):
    return pair_ref.at[0], second_ref.at[0], pair_ref.at[1], second_ref.at[1]


def load_kernel(source_hbm, out_ref, sem):
    copy = pltpu.make_async_copy(source_hbm, out_ref, sem)
    copy.start()
    copy.wait()


def lift_kernel(chunks, tile, place_ref, *refs):
    count = 2 * chunks
    shards, (up_ref, down_hbm) = refs[:count], refs[count : count + 2]
    active_ref, far_ref, down_ref, held, sems = refs[count + 2 :]
    hidden = active_ref.shape[1]
    share = far_ref.shape[2]
    rows = shards[0].shape[1]
    copies = []
    for first in range(0, hidden, tile):
        part = pl.ds(first, tile)
        copies.append(
            pltpu.make_async_copy(down_hbm.at[part], down_ref.at[part], sems.at[first // tile])
        )
        copies[-1].start()
    for c in range(chunks):
        for t, shard in enumerate(by_distance(*shards[2 * c : 2 * c + 2])):
            first = pl.multiple_of(((place_ref[1] ^ t) * chunks + c) * rows, rows)
            held[pl.ds(first, rows), :] = shard[...]
    for first in range(0, hidden, 2 * HD):
        last = min(first + 2 * HD, hidden)
        raised = lax.dot_general(
            up_ref[first:last, :], held[...], (((1,), (1,)), ((), ())), preferred_element_type=F32
        )
        active_ref[:, first:last] = (raised / (1.0 + jnp.exp(-raised))).T.astype(BF16)
    for copy in copies:
        copy.wait()
    for k in range(2):
        first = pl.multiple_of((place_ref[1] ^ (2 * k + 1)) * share, HD)
        far_ref[k] = jnp.dot(
            active_ref[...], down_ref[:, pl.ds(first, share)], preferred_element_type=F32
        ).astype(BF16)


def lower_kernel(place_ref, active_ref, down_ref, cross_ref, own_ref):
    share = own_ref.shape[1]
    for out_ref, turn in ((cross_ref, 2), (own_ref, 0)):
        first = pl.multiple_of((place_ref[1] ^ turn) * share, HD)
        out_ref[...] = jnp.dot(
            active_ref[...], down_ref[:, pl.ds(first, share)], preferred_element_type=F32
        )


def turn_kernel(place_ref, cross_ref, near_ref, far_ref, close_ref):
    half = far_ref.shape[0]
    mine = place_ref[0] // 2
    for out_ref, side in ((far_ref, 1 - mine), (close_ref, mine)):
        here = pl.ds(pl.multiple_of(side * half, half), half)
        out_ref[...] = (cross_ref[here, :] + near_ref[1, here, :].astype(F32)).astype(BF16)


def split_kernel(side, place_ref, own_ref, near_ref, crossed_ref, *outs):
    rows = outs[0].shape[0]
    for s, out_ref in enumerate(outs):
        z = place_ref[0] ^ (2 * side + s)
        here = pl.ds(pl.multiple_of(z * rows, rows), rows)
        there = pl.ds(pl.multiple_of(z % 2 * rows, rows), rows)
        total = own_ref[here, :] + near_ref[0, here, :].astype(F32)
        out_ref[...] = (total + crossed_ref[there, :].astype(F32)).astype(BF16)


def mix_kernel(first, gate_ref, *refs):
    out = refs[-1]
    terms = refs[:2]
    earlier = refs[2:-1]
    lanes = gate_ref.shape[2]
    for begin in range(0, out.shape[1], lanes):
        part = slice(begin, begin + lanes)
        total = gate_ref[first] * terms[0][:, part].astype(F32)
        total = total + gate_ref[first + 1] * terms[1][:, part].astype(F32)
        for ref in earlier:
            total = total + ref[:, part]
        out[:, part] = total.astype(out.dtype)


def trade(array, axis, turn):
    count = lax.axis_size(axis)
    return lax.ppermute(array, axis, [(k, k ^ turn) for k in range(count)])


def every_row_body(
    queries, new_kv, kv_cache, lengths, out_proj, norm_gain, expert_ids, gate_weights, w_up, w_down
):
    gx_count = lax.axis_size("gx")
    ta_count = lax.axis_size("ta")
    chunks = 2
    block_rows = queries.shape[0]
    rows = block_rows // chunks
    width = out_proj.shape[1]
    model = norm_gain.shape[0]
    hidden_share = w_up.shape[2]
    share = model // ta_count
    all_rows = block_rows * gx_count
    place = jnp.stack([lax.axis_index("gx"), lax.axis_index("ta")]).astype(jnp.int32)
    shape = jax.ShapeDtypeStruct
    gain = norm_gain.reshape(1, model)
    attended = []
    for c in range(chunks):
        after = attended[-1][1] if attended else lengths
        attended.append(attend(queries, new_kv, kv_cache, lengths, c * rows, rows, after))
    order = [s for s in range(gx_count - 1, 0, -1)]

    def spread(array, axis):
        parts = {0: array, **{s: trade(array, axis, s) for s in order}}
        return [parts[s] for s in range(len(parts))]

    shards = [[kept] + spread(sent, "gx")[1:] for sent, kept in attended]
    pieces, hidden = [], []
    for c in range(chunks):
        pieces.append(
            local_call(
                functools.partial(project_kernel, gx_count),
                [shape((rows, width), BF16)] * ta_count,
                [SMEM] + [VMEM] * (gx_count + 1),
                [pltpu.VMEM((ta_count, rows, width), BF16)],
                name="project",
                after=pieces[-1][0] if pieces else attended[-1][1],
            )(place, *shards[c], out_proj)
        )
    for c in range(chunks):
        parts = [pieces[c][0]] + [trade(pieces[c][t], "ta", t) for t in range(1, ta_count)]
        hidden.append(
            local_call(
                add_kernel,
                shape((rows, width), BF16),
                [VMEM] * ta_count,
                name="add",
                after=hidden[-1] if hidden else pieces[-1][0],
            )(*parts)
        )
    shards = [spread(part, "gx") for part in hidden]
    normed, pairs = [], []
    for c in range(chunks):
        normed.append(
            local_call(
                functools.partial(norm_kernel, gx_count),
                shape((rows, model), BF16),
                [SMEM] + [VMEM] * (gx_count + 1),
                [pltpu.VMEM((rows, model), F32)],
                name="norm",
                after=normed[-1] if normed else hidden[-1],
            )(place, gain, *shards[c])
        )
    gates = local_call(
        gate_kernel,
        shape((gx_count, block_rows, HD), F32),
        [SMEM, VMEM, VMEM],
        name="gates",
        after=normed[-1],
    )(place, expert_ids, gate_weights)
    up = local_call(
        load_kernel,
        shape((hidden_share, model), BF16),
        [ANYWHERE],
        [pltpu.SemaphoreType.DMA],
        vmem=40,
        name="load",
        after=gates,
    )(jnp.swapaxes(w_up[0], 0, 1))
    for c in range(chunks):
        pairs.append(
            local_call(
                pair_kernel,
                shape((2, rows, model), BF16),
                [VMEM] * 2,
                name="pair",
                after=pairs[-1] if pairs else up,
            )(normed[c], trade(normed[c], "ta", 2))
        )
    blocks = [block for pair in pairs for block in (pair, trade(pair, "ta", 1))]
    tile = math.gcd(hidden_share, 3 * 64)
    active, far, down = local_call(
        functools.partial(lift_kernel, chunks, tile),
        [
            shape((all_rows, hidden_share), BF16),
            shape((2, all_rows, share), BF16),
            shape((hidden_share, model), BF16),
        ],
        [SMEM] + [VMEM] * (2 * chunks + 1) + [ANYWHERE],
        [
            pltpu.VMEM((all_rows, model), BF16),
            pltpu.SemaphoreType.DMA((hidden_share // tile,)),
        ],
        vmem=30,
        name="lift",
    )(place, *blocks, up, w_down[0])
    near = trade(far, "ta", 1)
    cross, own = local_call(
        lower_kernel,
        [shape((all_rows, share), F32)] * 2,
        [SMEM, VMEM, VMEM],
        vmem=16,
        name="lower",
    )(place, active, down)
    half = all_rows // 2
    far_side, close_side = local_call(
        turn_kernel,
        [shape((half, share), BF16)] * 2,
        [SMEM] + [VMEM] * 2,
        name="turn",
    )(place, cross, near)
    terms, after = {}, None
    for side, crossing in ((1, far_side), (0, close_side)):
        crossed = trade(crossing, "ta", 2)
        terms[2 * side], terms[2 * side + 1] = local_call(
            functools.partial(split_kernel, side),
            [shape((block_rows, share), BF16)] * 2,
            [SMEM] + [VMEM] * 3,
            name="split",
            after=after,
        )(place, own, near, crossed)
        after = terms[2 * side]
    terms = [terms[s] if s == 0 else trade(terms[s], "gx", s) for s in range(gx_count)]
    far_sum = local_call(
        functools.partial(mix_kernel, 2),
        shape((block_rows, share), F32),
        [VMEM] * 3,
        name="mix_far",
        cost=MIX_COST,
    )(gates, *terms[2:])
    return local_call(
        functools.partial(mix_kernel, 0),
        shape((block_rows, share), BF16),
        [VMEM] * 4,
        name="mix",
    )(gates, *terms[:2], far_sum)


def route_tables(expert_ids, expert_count, block_rows, capacity):
    blocks = expert_ids.shape[0] // block_rows
    expert_range = jnp.arange(expert_count, dtype=jnp.int32)
    matches = (expert_ids[:, :, None] == expert_range[None, None, :]).astype(jnp.int32)
    routed = jnp.sum(matches, axis=1).reshape(blocks, block_rows, expert_count)
    position = jnp.cumsum(routed, axis=1) - routed
    slot_range = jnp.arange(capacity, dtype=jnp.int32)
    slot_hits = routed[:, :, :, None] * (
        position[:, :, :, None] == slot_range[None, None, None, :]
    ).astype(jnp.int32)
    row_range = jnp.arange(block_rows, dtype=jnp.int32)
    block_start = (jnp.arange(blocks, dtype=jnp.int32) * block_rows)[:, None, None]
    source_row = jnp.sum(slot_hits * row_range[None, :, None, None], axis=1) + block_start
    filled = jnp.sum(slot_hits, axis=1)
    source_row = jnp.transpose(source_row, (1, 0, 2)).reshape(expert_count, blocks * capacity)
    filled = jnp.transpose(filled, (1, 0, 2)).reshape(expert_count, blocks * capacity)
    pick_slot = jnp.sum(matches * position.reshape(blocks * block_rows, 1, expert_count), axis=2)
    return (source_row, filled, pick_slot)


def layer_norm(hidden, norm_gain):
    values = hidden.astype(jnp.float32)
    center = values - jnp.mean(values, axis=1, keepdims=True)
    spread = jnp.mean(center * center, axis=1, keepdims=True)
    return (center * lax.rsqrt(spread + 1e-05) * norm_gain).astype(jnp.bfloat16)


def body(
    queries, new_kv, kv_cache, lengths, out_proj, norm_gain, expert_ids, gate_weights, w_up, w_down
):
    gx_count = lax.axis_size("gx")
    ta_count = lax.axis_size("ta")
    block_rows = queries.shape[0]
    top_count = expert_ids.shape[1]
    capacity = min(block_rows, 2 * block_rows * top_count // gx_count)
    slot_count = gx_count * capacity
    model_width = norm_gain.shape[0]
    width_share = model_width // ta_count
    if gx_count == top_count and ta_count == gx_count == 4:
        return every_row_body(
            queries, new_kv, kv_cache, lengths, out_proj, norm_gain, expert_ids, gate_weights,
            w_up, w_down,
        )
    attended, _ = attend(queries, new_kv, kv_cache, lengths, 0, block_rows, lengths)
    projected = jnp.dot(
        lax.all_gather(attended, "gx", axis=0, tiled=True),
        out_proj,
        preferred_element_type=jnp.float32,
    ).astype(jnp.bfloat16)
    source_row, filled, pick_slot = route_tables(expert_ids, gx_count, block_rows, capacity)
    live_slots = (filled > 0)[:, :, None]
    widened = lax.optimization_barrier(projected).astype(jnp.float32)
    hidden_share = lax.psum_scatter(
        widened.astype(jnp.bfloat16), "ta", scatter_dimension=1, tiled=True
    )
    outgoing = jnp.where(live_slots, hidden_share[source_row], jnp.zeros((), jnp.bfloat16))[
        :, :, None, :
    ]
    arrived = lax.all_to_all(outgoing, "gx", split_axis=0, concat_axis=2, tiled=True)
    gathered = lax.all_gather(arrived, "ta", axis=3, tiled=True)
    hidden = gathered.reshape(slot_count, model_width)
    normed = layer_norm(hidden, norm_gain)
    raised = jnp.dot(normed, w_up[0], preferred_element_type=jnp.float32)
    active = jax.nn.silu(raised).astype(jnp.bfloat16)
    terms = jnp.dot(active, w_down[0], preferred_element_type=jnp.float32)
    mine = lax.psum_scatter(terms, "ta", scatter_dimension=1, tiled=True)
    result = mine.astype(jnp.bfloat16).reshape(gx_count, capacity, width_share)
    returned = lax.all_to_all(result, "gx", split_axis=0, concat_axis=0, tiled=True)
    first_row = lax.axis_index("gx") * block_rows
    local_ids = lax.dynamic_slice_in_dim(expert_ids, first_row, block_rows, 0)
    local_slot = lax.dynamic_slice_in_dim(pick_slot, first_row, block_rows, 0)
    flat_rows = returned.reshape(gx_count * capacity, width_share)
    picked = flat_rows[local_ids * capacity + local_slot]
    return jnp.sum(picked.astype(jnp.float32) * gate_weights[:, :, None], axis=1).astype(
        jnp.bfloat16
    )


def solution(mesh):
    return jax.shard_map(
        body,
        mesh=mesh,
        in_specs=(
            P(("groups", "gx"), "ta"),
            P(None, ("groups", "gx"), "ta"),
            P(None, ("groups", "gx"), None, "ta"),
            P(("groups", "gx")),
            P("ta", "gx"),
            P(),
            P("groups", None),
            P(("groups", "gx"), None),
            P("gx", None, "ta"),
            P("gx", "ta", None),
        ),
        out_specs=P(("groups", "gx"), "ta"),
        check_vma=False,
    )
```

```python
import functools
import math

import jax
import jax.numpy as jnp
from jax import lax
from jax.experimental import pallas as pl
from jax.experimental.pallas import tpu as pltpu
from jax.sharding import PartitionSpec as P

HD = 128
MIB = 1 << 20
MIX_COST = 1 << 22
VMEM = pl.BlockSpec(memory_space=pltpu.VMEM)
SMEM = pl.BlockSpec(memory_space=pltpu.SMEM)
F32 = jnp.float32
BF16 = jnp.bfloat16


ANYWHERE = pl.BlockSpec(memory_space=pl.ANY)


def local_call(kernel, out_shape, in_specs, scratch=(), vmem=8, name=None, after=None, cost=1024):
    several = isinstance(out_shape, (tuple, list))
    if after is not None:
        count, inner = len(in_specs), kernel
        in_specs = [*in_specs, ANYWHERE]
        kernel = lambda *refs: inner(*refs[:count], *refs[count + 1 :])
    call = pl.pallas_call(
        kernel,
        out_shape=out_shape,
        in_specs=in_specs,
        out_specs=[VMEM] * len(out_shape) if several else VMEM,
        scratch_shapes=list(scratch),
        compiler_params=pltpu.CompilerParams(vmem_limit_bytes=vmem * MIB),
        cost_estimate=pl.CostEstimate(flops=1024, bytes_accessed=cost, transcendentals=0),
        name=name,
    )
    return call if after is None else lambda *args: call(*args, after)


def attend_kernel(
    kv_heads, group, slots, batch, begin,
    small_ref, cache_ref, after_ref, out_ref,
    keys, values, q_rows, scores, own_scores, probs, own_probs, mixed, sems,
):
    rows = out_ref.shape[0]
    context = keys.shape[1]
    width = kv_heads * HD
    heads = kv_heads * group
    steps = rows // batch
    scale = 1.0 / math.sqrt(HD)
    fresh = [slice(heads * HD + k * width, heads * HD + (k + 1) * width) for k in range(2)]
    spans = slice(heads * HD + 2 * width, heads * HD + 2 * width + context)

    def fetch(step, kind):
        buffer = (keys, values)[kind]
        return pltpu.make_async_copy(
            cache_ref.at[kind, pl.ds(begin + step * batch, batch)],
            buffer.at[pl.ds(step * batch, batch)],
            sems.at[kind, step],
        )

    for step in range(steps):
        for kind in range(2):
            fetch(step, kind).start()
    q_rows[...] = jnp.zeros_like(q_rows)
    for head in range(heads):
        q_rows[head // group, pl.ds(head, rows, stride=slots), :] = small_ref[
            begin : begin + rows, head * HD : (head + 1) * HD
        ].astype(F32)
    place = lax.broadcasted_iota(jnp.int32, (slots, context), 1).astype(F32)
    for step in range(steps):
        fetch(step, 0).wait()
        for k in range(batch):
            row = step * batch + k
            whole = slice(begin + row, begin + row + 1)
            mine = jnp.concatenate(
                [q_rows[g, row * slots : (row + 1) * slots, :] for g in range(kv_heads)], axis=1
            )
            cached = lax.dot_general(
                mine.astype(BF16), keys[row], (((1,), (1,)), ((), ())),
                preferred_element_type=F32,
            )
            here = slice(k * slots, (k + 1) * slots)
            seen = place < small_ref[whole, spans].astype(F32)
            scores[here, :] = jnp.where(seen, cached * scale, -jnp.inf)
            fresh_key = small_ref[whole, fresh[0]].astype(F32)
            own_scores[here, :] = jnp.broadcast_to(
                jnp.sum(mine * fresh_key, axis=1, keepdims=True) * scale, (slots, HD)
            )
        cached = scores[...]
        own = own_scores[:, :1]
        largest = jnp.maximum(jnp.max(cached, axis=1, keepdims=True), own)
        lifted = jnp.exp(cached - largest)
        own_lifted = jnp.exp(own - largest)
        total = jnp.sum(lifted, axis=1, keepdims=True) + own_lifted
        probs[...] = (lifted / total).astype(BF16)
        own_probs[...] = jnp.broadcast_to(
            (own_lifted / total).astype(BF16).astype(F32), own_probs.shape
        )
        fetch(step, 1).wait()
        for k in range(batch):
            row = step * batch + k
            whole = slice(begin + row, begin + row + 1)
            here = slice(k * slots, (k + 1) * slots)
            weighted = jnp.dot(probs[here, :], values[row], preferred_element_type=F32)
            fresh_value = small_ref[whole, fresh[1]].astype(F32)
            total = weighted + own_probs[here, :1] * fresh_value
            for g in range(kv_heads):
                mixed[g, here, :] = total[:, g * HD : (g + 1) * HD]
        for head in range(heads):
            out_ref[step * batch : (step + 1) * batch, head * HD : (head + 1) * HD] = mixed[
                head // group, pl.ds(head, batch, stride=slots), :
            ].astype(BF16)


def beside(queries, new_kv, lengths, context):
    lanes = -(-context // HD) * HD
    spans = jnp.broadcast_to(lengths.astype(BF16)[:, None], (lengths.shape[0], lanes))
    return jnp.concatenate([queries, new_kv[0], new_kv[1], spans], axis=1)


def attend(small, kv_cache, heads, begin, rows, after):
    context, width = kv_cache.shape[2:]
    kv_heads = width // HD
    slots = -(-heads // 8) * 8
    batch = 16
    shape = jax.ShapeDtypeStruct((rows, heads * HD), BF16)
    return pl.pallas_call(
        functools.partial(attend_kernel, kv_heads, heads // kv_heads, slots, batch, begin),
        out_shape=shape,
        in_specs=[VMEM, ANYWHERE, ANYWHERE],
        out_specs=VMEM,
        scratch_shapes=[
            pltpu.VMEM((rows, context, width), BF16),
            pltpu.VMEM((rows, context, width), BF16),
            pltpu.VMEM((kv_heads, rows * slots, HD), F32),
            pltpu.VMEM((batch * slots, context), F32),
            pltpu.VMEM((batch * slots, HD), F32),
            pltpu.VMEM((batch * slots, context), BF16),
            pltpu.VMEM((batch * slots, HD), F32),
            pltpu.VMEM((kv_heads, batch * slots, HD), F32),
            pltpu.SemaphoreType.DMA((2, rows // batch)),
        ],
        compiler_params=pltpu.CompilerParams(vmem_limit_bytes=50 * MIB),
        cost_estimate=pl.CostEstimate(flops=1024, bytes_accessed=1024, transcendentals=0),
        name="attend",
    )(small, kv_cache, after)


def pair_kernel(own_ref, other_ref, out_ref):
    out_ref[0] = own_ref[...]
    out_ref[1] = other_ref[...]


def gate_kernel(place_ref, ids_ref, gates_ref, gate_ref):
    parts, rows, lanes = gate_ref.shape
    ids = ids_ref[pl.ds(pl.multiple_of(place_ref[0] * rows, rows), rows), :]
    for s in range(parts):
        gate = jnp.sum(
            jnp.where(ids == (place_ref[0] ^ s), gates_ref[...], 0.0), axis=1, keepdims=True
        )
        gate_ref[s] = jnp.broadcast_to(gate, (rows, lanes))


def project_kernel(parts, place_ref, *refs):
    shards, weight_ref = refs[:parts], refs[parts]
    outs, held = refs[parts + 1 : -1], refs[-1]
    rows = shards[0].shape[0]
    turn = place_ref[0] ^ place_ref[1]
    block = jnp.concatenate([shard[...] for shard in shards], axis=0)
    pieces = jnp.dot(block, weight_ref[...], preferred_element_type=F32).astype(BF16)
    for s in range(parts):
        held[turn ^ s] = pieces[s * rows : (s + 1) * rows, :]
    for t in range(parts):
        outs[t][...] = held[t]


def add_kernel(*refs):
    terms, out = refs[:-1], refs[-1]
    total = terms[0][...].astype(F32)
    for term in terms[1:]:
        total = total + term[...].astype(F32)
    out[...] = total.astype(BF16)


def norm_kernel(parts, place_ref, gain_ref, *refs):
    shards, out = refs[:parts], refs[parts]
    width = shards[0].shape[1]
    values = [shard[...].astype(F32) for shard in shards]
    center = sum(jnp.sum(part, axis=1, keepdims=True) for part in values) / out.shape[1]
    values = [part - center for part in values]
    spread = sum(jnp.sum(part * part, axis=1, keepdims=True) for part in values) / out.shape[1]
    scale = lax.rsqrt(spread + 1e-05)
    for s in range(parts):
        here = pl.ds(pl.multiple_of((place_ref[0] ^ s) * width, HD), width)
        out[:, here] = (values[s] * scale * gain_ref[:, here]).astype(BF16)


def by_distance(pair_ref, second_ref):
    return pair_ref.at[0], second_ref.at[0], pair_ref.at[1], second_ref.at[1]


def load_kernel(rows, source_hbm, out_ref, sem):
    copy = pltpu.make_async_copy(source_hbm.at[pl.ds(0, rows)], out_ref, sem)
    copy.start()
    copy.wait()


def lift_kernel(chunks, place_ref, *refs):
    count = 2 * chunks
    shards, (up_ref, down_ref, down_hbm) = refs[:count], refs[count : count + 3]
    active_ref, far_ref, close_ref, rest_ref, held, passed, sem = refs[count + 3 :]
    hidden = active_ref.shape[1]
    share = far_ref.shape[2]
    half = far_ref.shape[1]
    rows = shards[0].shape[1]
    cut = down_ref.shape[0]
    copy = pltpu.make_async_copy(down_hbm.at[pl.ds(cut, hidden - cut)], rest_ref, sem)
    copy.start()
    for c in range(chunks):
        for t, shard in enumerate(by_distance(*shards[2 * c : 2 * c + 2])):
            first = pl.multiple_of(((place_ref[1] ^ t) * chunks + c) * rows, rows)
            held[pl.ds(first, rows), :] = shard[...]
    for first in range(0, hidden, 2 * HD):
        last = min(first + 2 * HD, hidden)
        raised = lax.dot_general(
            up_ref[first:last, :], held[...], (((1,), (1,)), ((), ())), preferred_element_type=F32
        )
        active_ref[:, first:last] = (raised / (1.0 + jnp.exp(-raised))).T.astype(BF16)
    copy.wait()
    mine = place_ref[0] // 2
    for k in range(2):
        passed[...] = lowered(place_ref, 2 * k + 1, active_ref, down_ref, rest_ref, share).astype(BF16)
        for out_ref, side in ((far_ref, 1 - mine), (close_ref, mine)):
            out_ref[k] = passed[pl.ds(pl.multiple_of(side * half, half), half), :]


def lowered(place_ref, turn, active_ref, down_ref, rest_ref, share):
    cut = down_ref.shape[0]
    here = pl.ds(pl.multiple_of((place_ref[1] ^ turn) * share, HD), share)
    return jnp.dot(
        active_ref[:, :cut], down_ref[:, here], preferred_element_type=F32
    ) + jnp.dot(active_ref[:, cut:], rest_ref[:, here], preferred_element_type=F32)


def lower_kernel(turn, place_ref, active_ref, down_ref, rest_ref, out_ref):
    out_ref[...] = lowered(place_ref, turn, active_ref, down_ref, rest_ref, out_ref.shape[1])


def turn_kernel(distances, place_ref, cross_ref, near_ref, *outs):
    rows = outs[0].shape[0]
    for distance, out_ref in zip(distances, outs):
        z = place_ref[0] ^ distance
        here = pl.ds(pl.multiple_of(z * rows, rows), rows)
        there = pl.ds(pl.multiple_of(z % 2 * rows, rows), rows)
        out_ref[...] = (cross_ref[here, :] + near_ref[1, there, :].astype(F32)).astype(BF16)


def split_kernel(distances, place_ref, own_ref, near_ref, *refs):
    count = len(distances)
    rows = refs[0].shape[0]
    for distance, crossed_ref, out_ref in zip(distances, refs[:count], refs[count:]):
        z = place_ref[0] ^ distance
        here = pl.ds(pl.multiple_of(z * rows, rows), rows)
        there = pl.ds(pl.multiple_of(z % 2 * rows, rows), rows)
        total = own_ref[here, :] + near_ref[0, there, :].astype(F32)
        out_ref[...] = (total + crossed_ref[...].astype(F32)).astype(BF16)


def mix_kernel(distances, gate_ref, *refs):
    out = refs[-1]
    lanes = gate_ref.shape[2]
    for begin in range(0, out.shape[1], lanes):
        part = slice(begin, begin + lanes)
        total = sum(
            gate_ref[s] * term[:, part].astype(F32) for s, term in zip(distances, refs)
        )
        for ref in refs[len(distances) : -1]:
            total = total + ref[:, part]
        out[:, part] = total.astype(out.dtype)


def trade(array, axis, turn):
    count = lax.axis_size(axis)
    return lax.ppermute(array, axis, [(k, k ^ turn) for k in range(count)])


def every_row_body(
    queries, new_kv, kv_cache, lengths, out_proj, norm_gain, expert_ids, gate_weights, w_up, w_down
):
    gx_count = lax.axis_size("gx")
    ta_count = lax.axis_size("ta")
    chunks = 2
    block_rows = queries.shape[0]
    rows = block_rows // chunks
    width = out_proj.shape[1]
    model = norm_gain.shape[0]
    hidden_share = w_up.shape[2]
    share = model // ta_count
    all_rows = block_rows * gx_count
    place = jnp.stack([lax.axis_index("gx"), lax.axis_index("ta")]).astype(jnp.int32)
    shape = jax.ShapeDtypeStruct
    gain = norm_gain.reshape(1, model)
    heads = queries.shape[1] // HD
    small = beside(queries, new_kv, lengths, kv_cache.shape[2])
    attended = []
    for c in range(chunks):
        after = attended[-1] if attended else small
        attended.append(attend(small, kv_cache, heads, c * rows, rows, after))
    order = [s for s in range(gx_count - 1, 0, -1)]

    def spread(array, axis):
        parts = {0: array, **{s: trade(array, axis, s) for s in order}}
        return [parts[s] for s in range(len(parts))]

    shards = [spread(part, "gx") for part in attended]
    pieces, hidden = [], []
    for c in range(chunks):
        pieces.append(
            local_call(
                functools.partial(project_kernel, gx_count),
                [shape((rows, width), BF16)] * ta_count,
                [SMEM] + [VMEM] * (gx_count + 1),
                [pltpu.VMEM((ta_count, rows, width), BF16)],
                name="project",
                after=pieces[-1][0] if pieces else attended[-1],
            )(place, *shards[c], out_proj)
        )
    for c in range(chunks):
        parts = [pieces[c][0]] + [trade(pieces[c][t], "ta", t) for t in range(1, ta_count)]
        hidden.append(
            local_call(
                add_kernel,
                shape((rows, width), BF16),
                [VMEM] * ta_count,
                name="add",
                after=hidden[-1] if hidden else pieces[-1][0],
            )(*parts)
        )
    shards = [spread(part, "gx") for part in hidden]
    normed, pairs = [], []
    for c in range(chunks):
        normed.append(
            local_call(
                functools.partial(norm_kernel, gx_count),
                shape((rows, model), BF16),
                [SMEM] + [VMEM] * (gx_count + 1),
                name="norm",
                after=normed[-1] if normed else hidden[-1],
            )(place, gain, *shards[c])
        )
    gates = local_call(
        gate_kernel,
        shape((gx_count, block_rows, HD), F32),
        [SMEM, VMEM, VMEM],
        name="gates",
        after=normed[-1],
    )(place, expert_ids, gate_weights)
    up = local_call(
        functools.partial(load_kernel, hidden_share),
        shape((hidden_share, model), BF16),
        [ANYWHERE],
        [pltpu.SemaphoreType.DMA],
        vmem=40,
        name="load_up",
        after=gates,
    )(jnp.swapaxes(w_up[0], 0, 1))
    for c in range(chunks):
        pairs.append(
            local_call(
                pair_kernel,
                shape((2, rows, model), BF16),
                [VMEM] * 2,
                name="pair",
                after=pairs[-1] if pairs else up,
            )(normed[c], trade(normed[c], "ta", 2))
        )
    blocks = [block for pair in pairs for block in (pair, trade(pair, "ta", 1))]
    cut = -(-hidden_share // (4 * HD)) * 2 * HD
    part = local_call(
        functools.partial(load_kernel, cut),
        shape((cut, model), BF16),
        [ANYWHERE],
        [pltpu.SemaphoreType.DMA],
        vmem=37,
        name="load_down",
        after=pairs[-1],
    )(w_down[0])
    half = all_rows // 2
    active, far, close, rest = local_call(
        functools.partial(lift_kernel, chunks),
        [
            shape((all_rows, hidden_share), BF16),
            shape((2, half, share), BF16),
            shape((2, half, share), BF16),
            shape((hidden_share - cut, model), BF16),
        ],
        [SMEM] + [VMEM] * (2 * chunks + 2) + [ANYWHERE],
        [
            pltpu.VMEM((all_rows, model), BF16),
            pltpu.VMEM((all_rows, share), BF16),
            pltpu.SemaphoreType.DMA,
        ],
        vmem=30,
        name="lift",
    )(place, *blocks, up, part, w_down[0])
    near = {1: trade(far, "ta", 1), 0: trade(close, "ta", 1)}

    def lower(turn, after):
        return local_call(
            functools.partial(lower_kernel, turn),
            shape((all_rows, share), F32),
            [SMEM] + [VMEM] * 3,
            name="lower",
            after=after,
        )(place, active, part, rest)

    def on_rows(kernel, distances, after, *arrays):
        return local_call(
            functools.partial(kernel, distances),
            [shape((block_rows, share), BF16)] * len(distances),
            [SMEM] + [VMEM] * len(arrays),
            name=kernel.__name__[:-7],
            after=after,
        )(place, *arrays)

    cross = lower(2, None)
    groups = ((3,), (2,), (1, 0))
    turned = [cross]
    crossed = {}
    for distances in groups:
        sums = on_rows(turn_kernel, distances, turned[0], cross, near[distances[0] // 2])
        turned = sums
        crossed.update({s: trade(part, "ta", 2) for s, part in zip(distances, sums)})
    own = lower(0, turned[0])
    gathered, total, after = {}, [], None
    for distances in groups:
        terms = on_rows(
            split_kernel, distances, after, own, near[distances[0] // 2],
            *[crossed[s] for s in distances],
        )
        after = terms[0]
        for s, term in zip(distances, terms):
            gathered[s] = trade(term, "gx", s) if s else term
    for distances in groups:
        last = 0 in distances
        total = [
            local_call(
                functools.partial(mix_kernel, distances),
                shape((block_rows, share), BF16 if last else F32),
                [VMEM] * (1 + len(distances) + len(total)),
                name="mix",
                cost=1024 if last else MIX_COST,
            )(gates, *[gathered[s] for s in distances], *total)
        ]
    return total[0]


def route_tables(expert_ids, expert_count, block_rows, capacity):
    blocks = expert_ids.shape[0] // block_rows
    expert_range = jnp.arange(expert_count, dtype=jnp.int32)
    matches = (expert_ids[:, :, None] == expert_range[None, None, :]).astype(jnp.int32)
    routed = jnp.sum(matches, axis=1).reshape(blocks, block_rows, expert_count)
    position = jnp.cumsum(routed, axis=1) - routed
    slot_range = jnp.arange(capacity, dtype=jnp.int32)
    slot_hits = routed[:, :, :, None] * (
        position[:, :, :, None] == slot_range[None, None, None, :]
    ).astype(jnp.int32)
    row_range = jnp.arange(block_rows, dtype=jnp.int32)
    block_start = (jnp.arange(blocks, dtype=jnp.int32) * block_rows)[:, None, None]
    source_row = jnp.sum(slot_hits * row_range[None, :, None, None], axis=1) + block_start
    filled = jnp.sum(slot_hits, axis=1)
    source_row = jnp.transpose(source_row, (1, 0, 2)).reshape(expert_count, blocks * capacity)
    filled = jnp.transpose(filled, (1, 0, 2)).reshape(expert_count, blocks * capacity)
    pick_slot = jnp.sum(matches * position.reshape(blocks * block_rows, 1, expert_count), axis=2)
    return (source_row, filled, pick_slot)


def layer_norm(hidden, norm_gain):
    values = hidden.astype(jnp.float32)
    center = values - jnp.mean(values, axis=1, keepdims=True)
    spread = jnp.mean(center * center, axis=1, keepdims=True)
    return (center * lax.rsqrt(spread + 1e-05) * norm_gain).astype(jnp.bfloat16)


def body(
    queries, new_kv, kv_cache, lengths, out_proj, norm_gain, expert_ids, gate_weights, w_up, w_down
):
    gx_count = lax.axis_size("gx")
    ta_count = lax.axis_size("ta")
    block_rows = queries.shape[0]
    top_count = expert_ids.shape[1]
    capacity = min(block_rows, 2 * block_rows * top_count // gx_count)
    slot_count = gx_count * capacity
    model_width = norm_gain.shape[0]
    width_share = model_width // ta_count
    if gx_count == top_count and ta_count == gx_count == 4:
        return every_row_body(
            queries, new_kv, kv_cache, lengths, out_proj, norm_gain, expert_ids, gate_weights,
            w_up, w_down,
        )
    small = beside(queries, new_kv, lengths, kv_cache.shape[2])
    attended = attend(small, kv_cache, queries.shape[1] // HD, 0, block_rows, small)
    projected = jnp.dot(
        lax.all_gather(attended, "gx", axis=0, tiled=True),
        out_proj,
        preferred_element_type=jnp.float32,
    ).astype(jnp.bfloat16)
    source_row, filled, pick_slot = route_tables(expert_ids, gx_count, block_rows, capacity)
    live_slots = (filled > 0)[:, :, None]
    widened = lax.optimization_barrier(projected).astype(jnp.float32)
    hidden_share = lax.psum_scatter(
        widened.astype(jnp.bfloat16), "ta", scatter_dimension=1, tiled=True
    )
    outgoing = jnp.where(live_slots, hidden_share[source_row], jnp.zeros((), jnp.bfloat16))[
        :, :, None, :
    ]
    arrived = lax.all_to_all(outgoing, "gx", split_axis=0, concat_axis=2, tiled=True)
    gathered = lax.all_gather(arrived, "ta", axis=3, tiled=True)
    hidden = gathered.reshape(slot_count, model_width)
    normed = layer_norm(hidden, norm_gain)
    raised = jnp.dot(normed, w_up[0], preferred_element_type=jnp.float32)
    active = jax.nn.silu(raised).astype(jnp.bfloat16)
    terms = jnp.dot(active, w_down[0], preferred_element_type=jnp.float32)
    mine = lax.psum_scatter(terms, "ta", scatter_dimension=1, tiled=True)
    result = mine.astype(jnp.bfloat16).reshape(gx_count, capacity, width_share)
    returned = lax.all_to_all(result, "gx", split_axis=0, concat_axis=0, tiled=True)
    first_row = lax.axis_index("gx") * block_rows
    local_ids = lax.dynamic_slice_in_dim(expert_ids, first_row, block_rows, 0)
    local_slot = lax.dynamic_slice_in_dim(pick_slot, first_row, block_rows, 0)
    flat_rows = returned.reshape(gx_count * capacity, width_share)
    picked = flat_rows[local_ids * capacity + local_slot]
    return jnp.sum(picked.astype(jnp.float32) * gate_weights[:, :, None], axis=1).astype(
        jnp.bfloat16
    )


def solution(mesh):
    return jax.shard_map(
        body,
        mesh=mesh,
        in_specs=(
            P(("groups", "gx"), "ta"),
            P(None, ("groups", "gx"), "ta"),
            P(None, ("groups", "gx"), None, "ta"),
            P(("groups", "gx")),
            P("ta", "gx"),
            P(),
            P("groups", None),
            P(("groups", "gx"), None),
            P("gx", None, "ta"),
            P("gx", "ta", None),
        ),
        out_specs=P(("groups", "gx"), "ta"),
        check_vma=False,
    )
```

```python
import functools
import math

import jax
import jax.numpy as jnp
from jax import lax
from jax.experimental import pallas as pl
from jax.experimental.pallas import tpu as pltpu
from jax.sharding import PartitionSpec as P

HD = 128
MIB = 1 << 20
MIX_COST = 1 << 22
PROJECT_COST = 1 << 21
VMEM = pl.BlockSpec(memory_space=pltpu.VMEM)
F32 = jnp.float32
BF16 = jnp.bfloat16


ANYWHERE = pl.BlockSpec(memory_space=pl.ANY)


def local_call(kernel, out_shape, in_specs, scratch=(), vmem=8, name=None, after=None, cost=1024):
    several = isinstance(out_shape, (tuple, list))
    if after is not None:
        count, inner = len(in_specs), kernel
        in_specs = [*in_specs, ANYWHERE]
        kernel = lambda *refs: inner(*refs[:count], *refs[count + 1 :])
    call = pl.pallas_call(
        kernel,
        out_shape=out_shape,
        in_specs=in_specs,
        out_specs=[VMEM] * len(out_shape) if several else VMEM,
        scratch_shapes=list(scratch),
        compiler_params=pltpu.CompilerParams(vmem_limit_bytes=vmem * MIB),
        cost_estimate=pl.CostEstimate(flops=1024, bytes_accessed=cost, transcendentals=0),
        name=name,
    )
    return call if after is None else lambda *args: call(*args, after)


def attend_kernel(
    kv_heads, group, slots, batch, begin,
    small_ref, cache_ref, after_ref, out_ref,
    keys, values, q_rows, scores, own_scores, probs, own_probs, mixed, sems,
):
    rows = out_ref.shape[0]
    context = keys.shape[1]
    width = kv_heads * HD
    heads = kv_heads * group
    steps = rows // batch
    scale = 1.0 / math.sqrt(HD)
    fresh = [slice(heads * HD + k * width, heads * HD + (k + 1) * width) for k in range(2)]
    spans = slice(heads * HD + 2 * width, heads * HD + 2 * width + context)

    def fetch(step, kind):
        buffer = (keys, values)[kind]
        return pltpu.make_async_copy(
            cache_ref.at[kind, pl.ds(begin + step * batch, batch)],
            buffer.at[pl.ds(step * batch, batch)],
            sems.at[kind, step],
        )

    for step in range(steps):
        for kind in range(2):
            fetch(step, kind).start()
    q_rows[...] = jnp.zeros_like(q_rows)
    for head in range(heads):
        q_rows[head // group, pl.ds(head, rows, stride=slots), :] = small_ref[
            begin : begin + rows, head * HD : (head + 1) * HD
        ].astype(F32)
    place = lax.broadcasted_iota(jnp.int32, (slots, context), 1).astype(F32)
    for step in range(steps):
        fetch(step, 0).wait()
        for k in range(batch):
            row = step * batch + k
            whole = slice(begin + row, begin + row + 1)
            mine = jnp.concatenate(
                [q_rows[g, row * slots : (row + 1) * slots, :] for g in range(kv_heads)], axis=1
            )
            cached = lax.dot_general(
                mine.astype(BF16), keys[row], (((1,), (1,)), ((), ())),
                preferred_element_type=F32,
            )
            here = slice(k * slots, (k + 1) * slots)
            seen = place < small_ref[whole, spans].astype(F32)
            scores[here, :] = jnp.where(seen, cached * scale, -jnp.inf)
            fresh_key = small_ref[whole, fresh[0]].astype(F32)
            own_scores[here, :] = jnp.broadcast_to(
                jnp.sum(mine * fresh_key, axis=1, keepdims=True) * scale, (slots, HD)
            )
        cached = scores[...]
        own = own_scores[:, :1]
        largest = jnp.maximum(jnp.max(cached, axis=1, keepdims=True), own)
        lifted = jnp.exp(cached - largest)
        own_lifted = jnp.exp(own - largest)
        total = jnp.sum(lifted, axis=1, keepdims=True) + own_lifted
        probs[...] = (lifted / total).astype(BF16)
        own_probs[...] = jnp.broadcast_to(
            (own_lifted / total).astype(BF16).astype(F32), own_probs.shape
        )
        fetch(step, 1).wait()
        for k in range(batch):
            row = step * batch + k
            whole = slice(begin + row, begin + row + 1)
            here = slice(k * slots, (k + 1) * slots)
            weighted = jnp.dot(probs[here, :], values[row], preferred_element_type=F32)
            fresh_value = small_ref[whole, fresh[1]].astype(F32)
            total = weighted + own_probs[here, :1] * fresh_value
            for g in range(kv_heads):
                mixed[g, here, :] = total[:, g * HD : (g + 1) * HD]
        for head in range(heads):
            out_ref[step * batch : (step + 1) * batch, head * HD : (head + 1) * HD] = mixed[
                head // group, pl.ds(head, batch, stride=slots), :
            ].astype(BF16)


def beside(queries, new_kv, lengths, context):
    lanes = -(-context // HD) * HD
    spans = jnp.broadcast_to(lengths.astype(BF16)[:, None], (lengths.shape[0], lanes))
    return jnp.concatenate([queries, new_kv[0], new_kv[1], spans], axis=1)


def attend(small, kv_cache, heads, begin, rows, after):
    context, width = kv_cache.shape[2:]
    kv_heads = width // HD
    slots = -(-heads // 8) * 8
    batch = 16
    shape = jax.ShapeDtypeStruct((rows, heads * HD), BF16)
    return pl.pallas_call(
        functools.partial(attend_kernel, kv_heads, heads // kv_heads, slots, batch, begin),
        out_shape=shape,
        in_specs=[VMEM, ANYWHERE, ANYWHERE],
        out_specs=VMEM,
        scratch_shapes=[
            pltpu.VMEM((rows, context, width), BF16),
            pltpu.VMEM((rows, context, width), BF16),
            pltpu.VMEM((kv_heads, rows * slots, HD), F32),
            pltpu.VMEM((batch * slots, context), F32),
            pltpu.VMEM((batch * slots, HD), F32),
            pltpu.VMEM((batch * slots, context), BF16),
            pltpu.VMEM((batch * slots, HD), F32),
            pltpu.VMEM((kv_heads, batch * slots, HD), F32),
            pltpu.SemaphoreType.DMA((2, rows // batch)),
        ],
        compiler_params=pltpu.CompilerParams(vmem_limit_bytes=50 * MIB),
        cost_estimate=pl.CostEstimate(flops=1024, bytes_accessed=1024, transcendentals=0),
        name="attend",
    )(small, kv_cache, after)


def pair_kernel(own_ref, other_ref, out_ref):
    out_ref[0] = own_ref[...]
    out_ref[1] = other_ref[...]


def gate_kernel(ids_ref, gates_ref, gate_ref):
    parts, rows, lanes = gate_ref.shape
    ids = ids_ref[pl.ds(pl.multiple_of(lax.axis_index("gx") * rows, rows), rows), :]
    for s in range(parts):
        gate = jnp.sum(
            jnp.where(ids == (lax.axis_index("gx") ^ s), gates_ref[...], 0.0), axis=1, keepdims=True
        )
        gate_ref[s] = jnp.broadcast_to(gate, (rows, lanes))


def project_kernel(parts, *refs):
    shards, weight_ref = refs[:parts], refs[parts]
    outs, held = refs[parts + 1 : -1], refs[-1]
    rows = shards[0].shape[0]
    turn = lax.axis_index("gx") ^ lax.axis_index("ta")
    block = jnp.concatenate([shard[...] for shard in shards], axis=0)
    pieces = jnp.dot(block, weight_ref[...], preferred_element_type=F32).astype(BF16)
    for s in range(parts):
        held[turn ^ s] = pieces[s * rows : (s + 1) * rows, :]
    for t in range(parts):
        outs[t][...] = held[t]


def add_kernel(*refs):
    terms, out = refs[:-1], refs[-1]
    total = terms[0][...].astype(F32)
    for term in terms[1:]:
        total = total + term[...].astype(F32)
    out[...] = total.astype(BF16)


def norm_kernel(parts, gain_ref, *refs):
    shards, out = refs[:parts], refs[parts]
    width = shards[0].shape[1]
    values = [shard[...].astype(F32) for shard in shards]
    center = sum(jnp.sum(part, axis=1, keepdims=True) for part in values) / out.shape[1]
    values = [part - center for part in values]
    spread = sum(jnp.sum(part * part, axis=1, keepdims=True) for part in values) / out.shape[1]
    scale = lax.rsqrt(spread + 1e-05)
    for s in range(parts):
        here = pl.ds(pl.multiple_of((lax.axis_index("gx") ^ s) * width, HD), width)
        out[:, here] = (values[s] * scale * gain_ref[:, here]).astype(BF16)


def by_distance(pair_ref, second_ref):
    return pair_ref.at[0], second_ref.at[0], pair_ref.at[1], second_ref.at[1]


def load_kernel(rows, source_hbm, out_ref, sem):
    copy = pltpu.make_async_copy(source_hbm.at[pl.ds(0, rows)], out_ref, sem)
    copy.start()
    copy.wait()


def lift_kernel(chunks, *refs):
    count = 2 * chunks
    shards, (up_ref, down_ref, down_hbm) = refs[:count], refs[count : count + 3]
    active_ref, far_ref, close_ref, rest_ref, held, passed, sem = refs[count + 3 :]
    hidden = active_ref.shape[1]
    share = far_ref.shape[2]
    half = far_ref.shape[1]
    rows = shards[0].shape[1]
    cut = down_ref.shape[0]
    copy = pltpu.make_async_copy(down_hbm.at[pl.ds(cut, hidden - cut)], rest_ref, sem)
    copy.start()
    for c in range(chunks):
        for t, shard in enumerate(by_distance(*shards[2 * c : 2 * c + 2])):
            first = pl.multiple_of(((lax.axis_index("ta") ^ t) * chunks + c) * rows, rows)
            held[pl.ds(first, rows), :] = shard[...]
    for first in range(0, hidden, 2 * HD):
        last = min(first + 2 * HD, hidden)
        raised = lax.dot_general(
            up_ref[first:last, :], held[...], (((1,), (1,)), ((), ())), preferred_element_type=F32
        )
        active_ref[:, first:last] = (raised / (1.0 + jnp.exp(-raised))).T.astype(BF16)
    copy.wait()
    mine = lax.axis_index("gx") // 2
    for k in range(2):
        passed[...] = lowered(2 * k + 1, active_ref, down_ref, rest_ref, share).astype(BF16)
        for out_ref, side in ((far_ref, 1 - mine), (close_ref, mine)):
            out_ref[k] = passed[pl.ds(pl.multiple_of(side * half, half), half), :]


def lowered(turn, active_ref, down_ref, rest_ref, share):
    cut = down_ref.shape[0]
    here = pl.ds(pl.multiple_of((lax.axis_index("ta") ^ turn) * share, HD), share)
    return jnp.dot(
        active_ref[:, :cut], down_ref[:, here], preferred_element_type=F32
    ) + jnp.dot(active_ref[:, cut:], rest_ref[:, here], preferred_element_type=F32)


def lower_kernel(turn, active_ref, down_ref, rest_ref, out_ref):
    out_ref[...] = lowered(turn, active_ref, down_ref, rest_ref, out_ref.shape[1])


def turn_kernel(distances, cross_ref, near_ref, *outs):
    rows = outs[0].shape[0]
    for distance, out_ref in zip(distances, outs):
        z = lax.axis_index("gx") ^ distance
        here = pl.ds(pl.multiple_of(z * rows, rows), rows)
        there = pl.ds(pl.multiple_of(z % 2 * rows, rows), rows)
        out_ref[...] = (cross_ref[here, :] + near_ref[1, there, :].astype(F32)).astype(BF16)


def split_kernel(distances, own_ref, near_ref, *refs):
    count = len(distances)
    rows = refs[0].shape[0]
    for distance, crossed_ref, out_ref in zip(distances, refs[:count], refs[count:]):
        z = lax.axis_index("gx") ^ distance
        here = pl.ds(pl.multiple_of(z * rows, rows), rows)
        there = pl.ds(pl.multiple_of(z % 2 * rows, rows), rows)
        total = own_ref[here, :] + near_ref[0, there, :].astype(F32)
        out_ref[...] = (total + crossed_ref[...].astype(F32)).astype(BF16)


def mix_kernel(distances, gate_ref, *refs):
    out = refs[-1]
    lanes = gate_ref.shape[2]
    for begin in range(0, out.shape[1], lanes):
        part = slice(begin, begin + lanes)
        total = sum(
            gate_ref[s] * term[:, part].astype(F32) for s, term in zip(distances, refs)
        )
        for ref in refs[len(distances) : -1]:
            total = total + ref[:, part]
        out[:, part] = total.astype(out.dtype)


def trade(array, axis, turn):
    count = lax.axis_size(axis)
    return lax.ppermute(array, axis, [(k, k ^ turn) for k in range(count)])


def every_row_body(
    queries, new_kv, kv_cache, lengths, out_proj, norm_gain, expert_ids, gate_weights, w_up, w_down
):
    gx_count = lax.axis_size("gx")
    ta_count = lax.axis_size("ta")
    chunks = 2
    block_rows = queries.shape[0]
    rows = block_rows // chunks
    width = out_proj.shape[1]
    model = norm_gain.shape[0]
    hidden_share = w_up.shape[2]
    share = model // ta_count
    all_rows = block_rows * gx_count
    shape = jax.ShapeDtypeStruct
    gain = norm_gain.reshape(1, model)
    heads = queries.shape[1] // HD
    small = beside(queries, new_kv, lengths, kv_cache.shape[2])
    attended = []
    for c in range(chunks):
        after = attended[-1] if attended else small
        attended.append(attend(small, kv_cache, heads, c * rows, rows, after))
    order = [s for s in range(gx_count - 1, 0, -1)]

    def spread(array, axis):
        parts = {0: array, **{s: trade(array, axis, s) for s in order}}
        return [parts[s] for s in range(len(parts))]

    shards = [spread(part, "gx") for part in attended]
    pieces, hidden = [], []
    for c in range(chunks):
        pieces.append(
            local_call(
                functools.partial(project_kernel, gx_count),
                [shape((rows, width), BF16)] * ta_count,
                [VMEM] * (gx_count + 1),
                [pltpu.VMEM((ta_count, rows, width), BF16)],
                name="project",
                after=pieces[-1][0] if pieces else attended[-1],
                cost=PROJECT_COST,
            )(*shards[c], out_proj)
        )
    for c in range(chunks):
        parts = [pieces[c][0]] + [trade(pieces[c][t], "ta", t) for t in range(1, ta_count)]
        hidden.append(
            local_call(
                add_kernel,
                shape((rows, width), BF16),
                [VMEM] * ta_count,
                name="add",
                after=hidden[-1] if hidden else pieces[-1][0],
            )(*parts)
        )
    shards = [spread(part, "gx") for part in hidden]
    normed, pairs = [], []
    for c in range(chunks):
        normed.append(
            local_call(
                functools.partial(norm_kernel, gx_count),
                shape((rows, model), BF16),
                [VMEM] * (gx_count + 1),
                name="norm",
                after=normed[-1] if normed else hidden[-1],
            )(gain, *shards[c])
        )
    gates = local_call(
        gate_kernel,
        shape((gx_count, block_rows, HD), F32),
        [VMEM, VMEM],
        name="gates",
        after=normed[-1],
    )(expert_ids, gate_weights)
    up = local_call(
        functools.partial(load_kernel, hidden_share),
        shape((hidden_share, model), BF16),
        [ANYWHERE],
        [pltpu.SemaphoreType.DMA],
        vmem=40,
        name="load_up",
        after=gates,
    )(jnp.swapaxes(w_up[0], 0, 1))
    for c in range(chunks):
        pairs.append(
            local_call(
                pair_kernel,
                shape((2, rows, model), BF16),
                [VMEM] * 2,
                name="pair",
                after=pairs[-1] if pairs else up,
            )(normed[c], trade(normed[c], "ta", 2))
        )
    blocks = [block for pair in pairs for block in (pair, trade(pair, "ta", 1))]
    cut = -(-hidden_share // (4 * HD)) * 2 * HD
    part = local_call(
        functools.partial(load_kernel, cut),
        shape((cut, model), BF16),
        [ANYWHERE],
        [pltpu.SemaphoreType.DMA],
        vmem=42,
        name="load_down",
        after=pairs[-1],
    )(w_down[0])
    half = all_rows // 2
    active, far, close, rest = local_call(
        functools.partial(lift_kernel, chunks),
        [
            shape((all_rows, hidden_share), BF16),
            shape((2, half, share), BF16),
            shape((2, half, share), BF16),
            shape((hidden_share - cut, model), BF16),
        ],
        [VMEM] * (2 * chunks + 2) + [ANYWHERE],
        [
            pltpu.VMEM((all_rows, model), BF16),
            pltpu.VMEM((all_rows, share), BF16),
            pltpu.SemaphoreType.DMA,
        ],
        vmem=30,
        name="lift",
    )(*blocks, up, part, w_down[0])
    near = {1: trade(far, "ta", 1), 0: trade(close, "ta", 1)}

    def lower(turn, after):
        return local_call(
            functools.partial(lower_kernel, turn),
            shape((all_rows, share), F32),
            [VMEM] * 3,
            name="lower",
            after=after,
        )(active, part, rest)

    def on_rows(kernel, distances, after, *arrays):
        return local_call(
            functools.partial(kernel, distances),
            [shape((block_rows, share), BF16)] * len(distances),
            [VMEM] * len(arrays),
            name=kernel.__name__[:-7],
            after=after,
        )(*arrays)

    cross = lower(2, None)
    groups = ((3,), (2,), (1, 0))
    turned = [cross]
    crossed = {}
    for distances in groups:
        sums = on_rows(turn_kernel, distances, turned[0], cross, near[distances[0] // 2])
        turned = sums
        crossed.update({s: trade(part, "ta", 2) for s, part in zip(distances, sums)})
    own = lower(0, turned[0])
    gathered, total, after = {}, [], None
    for distances in groups:
        terms = on_rows(
            split_kernel, distances, after, own, near[distances[0] // 2],
            *[crossed[s] for s in distances],
        )
        after = terms[0]
        for s, term in zip(distances, terms):
            gathered[s] = trade(term, "gx", s) if s else term
    for distances in groups:
        last = 0 in distances
        total = [
            local_call(
                functools.partial(mix_kernel, distances),
                shape((block_rows, share), BF16 if last else F32),
                [VMEM] * (1 + len(distances) + len(total)),
                name="mix",
                cost=1024 if last else MIX_COST,
            )(gates, *[gathered[s] for s in distances], *total)
        ]
    return total[0]


def route_tables(expert_ids, expert_count, block_rows, capacity):
    blocks = expert_ids.shape[0] // block_rows
    expert_range = jnp.arange(expert_count, dtype=jnp.int32)
    matches = (expert_ids[:, :, None] == expert_range[None, None, :]).astype(jnp.int32)
    routed = jnp.sum(matches, axis=1).reshape(blocks, block_rows, expert_count)
    position = jnp.cumsum(routed, axis=1) - routed
    slot_range = jnp.arange(capacity, dtype=jnp.int32)
    slot_hits = routed[:, :, :, None] * (
        position[:, :, :, None] == slot_range[None, None, None, :]
    ).astype(jnp.int32)
    row_range = jnp.arange(block_rows, dtype=jnp.int32)
    block_start = (jnp.arange(blocks, dtype=jnp.int32) * block_rows)[:, None, None]
    source_row = jnp.sum(slot_hits * row_range[None, :, None, None], axis=1) + block_start
    filled = jnp.sum(slot_hits, axis=1)
    source_row = jnp.transpose(source_row, (1, 0, 2)).reshape(expert_count, blocks * capacity)
    filled = jnp.transpose(filled, (1, 0, 2)).reshape(expert_count, blocks * capacity)
    pick_slot = jnp.sum(matches * position.reshape(blocks * block_rows, 1, expert_count), axis=2)
    return (source_row, filled, pick_slot)


def layer_norm(hidden, norm_gain):
    values = hidden.astype(jnp.float32)
    center = values - jnp.mean(values, axis=1, keepdims=True)
    spread = jnp.mean(center * center, axis=1, keepdims=True)
    return (center * lax.rsqrt(spread + 1e-05) * norm_gain).astype(jnp.bfloat16)


def body(
    queries, new_kv, kv_cache, lengths, out_proj, norm_gain, expert_ids, gate_weights, w_up, w_down
):
    gx_count = lax.axis_size("gx")
    ta_count = lax.axis_size("ta")
    block_rows = queries.shape[0]
    top_count = expert_ids.shape[1]
    capacity = min(block_rows, 2 * block_rows * top_count // gx_count)
    slot_count = gx_count * capacity
    model_width = norm_gain.shape[0]
    width_share = model_width // ta_count
    if gx_count == top_count and ta_count == gx_count == 4:
        return every_row_body(
            queries, new_kv, kv_cache, lengths, out_proj, norm_gain, expert_ids, gate_weights,
            w_up, w_down,
        )
    small = beside(queries, new_kv, lengths, kv_cache.shape[2])
    attended = attend(small, kv_cache, queries.shape[1] // HD, 0, block_rows, small)
    projected = jnp.dot(
        lax.all_gather(attended, "gx", axis=0, tiled=True),
        out_proj,
        preferred_element_type=jnp.float32,
    ).astype(jnp.bfloat16)
    source_row, filled, pick_slot = route_tables(expert_ids, gx_count, block_rows, capacity)
    live_slots = (filled > 0)[:, :, None]
    widened = lax.optimization_barrier(projected).astype(jnp.float32)
    hidden_share = lax.psum_scatter(
        widened.astype(jnp.bfloat16), "ta", scatter_dimension=1, tiled=True
    )
    outgoing = jnp.where(live_slots, hidden_share[source_row], jnp.zeros((), jnp.bfloat16))[
        :, :, None, :
    ]
    arrived = lax.all_to_all(outgoing, "gx", split_axis=0, concat_axis=2, tiled=True)
    gathered = lax.all_gather(arrived, "ta", axis=3, tiled=True)
    hidden = gathered.reshape(slot_count, model_width)
    normed = layer_norm(hidden, norm_gain)
    raised = jnp.dot(normed, w_up[0], preferred_element_type=jnp.float32)
    active = jax.nn.silu(raised).astype(jnp.bfloat16)
    terms = jnp.dot(active, w_down[0], preferred_element_type=jnp.float32)
    mine = lax.psum_scatter(terms, "ta", scatter_dimension=1, tiled=True)
    result = mine.astype(jnp.bfloat16).reshape(gx_count, capacity, width_share)
    returned = lax.all_to_all(result, "gx", split_axis=0, concat_axis=0, tiled=True)
    first_row = lax.axis_index("gx") * block_rows
    local_ids = lax.dynamic_slice_in_dim(expert_ids, first_row, block_rows, 0)
    local_slot = lax.dynamic_slice_in_dim(pick_slot, first_row, block_rows, 0)
    flat_rows = returned.reshape(gx_count * capacity, width_share)
    picked = flat_rows[local_ids * capacity + local_slot]
    return jnp.sum(picked.astype(jnp.float32) * gate_weights[:, :, None], axis=1).astype(
        jnp.bfloat16
    )


def solution(mesh):
    return jax.shard_map(
        body,
        mesh=mesh,
        in_specs=(
            P(("groups", "gx"), "ta"),
            P(None, ("groups", "gx"), "ta"),
            P(None, ("groups", "gx"), None, "ta"),
            P(("groups", "gx")),
            P("ta", "gx"),
            P(),
            P("groups", None),
            P(("groups", "gx"), None),
            P("gx", None, "ta"),
            P("gx", "ta", None),
        ),
        out_specs=P(("groups", "gx"), "ta"),
        check_vma=False,
    )
```

```python
import functools
import math

import jax
import jax.numpy as jnp
from jax import lax
from jax.experimental import pallas as pl
from jax.experimental.pallas import tpu as pltpu
from jax.sharding import PartitionSpec as P

HD = 128
MIB = 1 << 20
MIX_COST = 1 << 22
VMEM = pl.BlockSpec(memory_space=pltpu.VMEM)
F32 = jnp.float32
BF16 = jnp.bfloat16


ANYWHERE = pl.BlockSpec(memory_space=pl.ANY)


def local_call(kernel, out_shape, in_specs, scratch=(), vmem=8, name=None, after=None, cost=1024):
    several = isinstance(out_shape, (tuple, list))
    if after is not None:
        count, inner = len(in_specs), kernel
        in_specs = [*in_specs, ANYWHERE]
        kernel = lambda *refs: inner(*refs[:count], *refs[count + 1 :])
    call = pl.pallas_call(
        kernel,
        out_shape=out_shape,
        in_specs=in_specs,
        out_specs=[VMEM] * len(out_shape) if several else VMEM,
        scratch_shapes=list(scratch),
        compiler_params=pltpu.CompilerParams(vmem_limit_bytes=vmem * MIB),
        cost_estimate=pl.CostEstimate(flops=1024, bytes_accessed=cost, transcendentals=0),
        name=name,
    )
    return call if after is None else lambda *args: call(*args, after)


def attend_kernel(
    kv_heads, group, slots, batch, begin,
    small_ref, cache_ref, after_ref, out_ref,
    keys, values, q_rows, scores, own_scores, probs, own_probs, mixed, sems,
):
    rows = out_ref.shape[0]
    context = keys.shape[1]
    width = kv_heads * HD
    heads = kv_heads * group
    steps = rows // batch
    scale = 1.0 / math.sqrt(HD)
    fresh = [slice(heads * HD + k * width, heads * HD + (k + 1) * width) for k in range(2)]
    spans = slice(heads * HD + 2 * width, heads * HD + 2 * width + context)

    def fetch(step, kind):
        buffer = (keys, values)[kind]
        return pltpu.make_async_copy(
            cache_ref.at[kind, pl.ds(begin + step * batch, batch)],
            buffer.at[pl.ds(step * batch, batch)],
            sems.at[kind, step],
        )

    for step in range(steps):
        for kind in range(2):
            fetch(step, kind).start()
    q_rows[...] = jnp.zeros_like(q_rows)
    for head in range(heads):
        q_rows[head // group, pl.ds(head, rows, stride=slots), :] = small_ref[
            begin : begin + rows, head * HD : (head + 1) * HD
        ].astype(F32)
    place = lax.broadcasted_iota(jnp.int32, (slots, context), 1).astype(F32)
    for step in range(steps):
        fetch(step, 0).wait()
        for k in range(batch):
            row = step * batch + k
            whole = slice(begin + row, begin + row + 1)
            mine = jnp.concatenate(
                [q_rows[g, row * slots : (row + 1) * slots, :] for g in range(kv_heads)], axis=1
            )
            cached = lax.dot_general(
                mine.astype(BF16), keys[row], (((1,), (1,)), ((), ())),
                preferred_element_type=F32,
            )
            here = slice(k * slots, (k + 1) * slots)
            seen = place < small_ref[whole, spans].astype(F32)
            scores[here, :] = jnp.where(seen, cached * scale, -jnp.inf)
            fresh_key = small_ref[whole, fresh[0]].astype(F32)
            own_scores[here, :] = jnp.broadcast_to(
                jnp.sum(mine * fresh_key, axis=1, keepdims=True) * scale, (slots, HD)
            )
        cached = scores[...]
        own = own_scores[:, :1]
        largest = jnp.maximum(jnp.max(cached, axis=1, keepdims=True), own)
        lifted = jnp.exp(cached - largest)
        own_lifted = jnp.exp(own - largest)
        total = jnp.sum(lifted, axis=1, keepdims=True) + own_lifted
        probs[...] = (lifted / total).astype(BF16)
        own_probs[...] = jnp.broadcast_to(
            (own_lifted / total).astype(BF16).astype(F32), own_probs.shape
        )
        fetch(step, 1).wait()
        for k in range(batch):
            row = step * batch + k
            whole = slice(begin + row, begin + row + 1)
            here = slice(k * slots, (k + 1) * slots)
            weighted = jnp.dot(probs[here, :], values[row], preferred_element_type=F32)
            fresh_value = small_ref[whole, fresh[1]].astype(F32)
            total = weighted + own_probs[here, :1] * fresh_value
            for g in range(kv_heads):
                mixed[g, here, :] = total[:, g * HD : (g + 1) * HD]
        for head in range(heads):
            out_ref[step * batch : (step + 1) * batch, head * HD : (head + 1) * HD] = mixed[
                head // group, pl.ds(head, batch, stride=slots), :
            ].astype(BF16)


def beside(queries, new_kv, lengths, context):
    lanes = -(-context // HD) * HD
    spans = jnp.broadcast_to(lengths.astype(BF16)[:, None], (lengths.shape[0], lanes))
    return jnp.concatenate([queries, new_kv[0], new_kv[1], spans], axis=1)


def attend(small, kv_cache, heads, begin, rows, after):
    context, width = kv_cache.shape[2:]
    kv_heads = width // HD
    slots = -(-heads // 8) * 8
    batch = 16
    shape = jax.ShapeDtypeStruct((rows, heads * HD), BF16)
    return pl.pallas_call(
        functools.partial(attend_kernel, kv_heads, heads // kv_heads, slots, batch, begin),
        out_shape=shape,
        in_specs=[VMEM, ANYWHERE, ANYWHERE],
        out_specs=VMEM,
        scratch_shapes=[
            pltpu.VMEM((rows, context, width), BF16),
            pltpu.VMEM((rows, context, width), BF16),
            pltpu.VMEM((kv_heads, rows * slots, HD), F32),
            pltpu.VMEM((batch * slots, context), F32),
            pltpu.VMEM((batch * slots, HD), F32),
            pltpu.VMEM((batch * slots, context), BF16),
            pltpu.VMEM((batch * slots, HD), F32),
            pltpu.VMEM((kv_heads, batch * slots, HD), F32),
            pltpu.SemaphoreType.DMA((2, rows // batch)),
        ],
        compiler_params=pltpu.CompilerParams(vmem_limit_bytes=50 * MIB),
        cost_estimate=pl.CostEstimate(flops=1024, bytes_accessed=1024, transcendentals=0),
        name="attend",
    )(small, kv_cache, after)


def pair_kernel(own_ref, other_ref, out_ref):
    out_ref[0] = own_ref[...]
    out_ref[1] = other_ref[...]


def pass_kernel(source_ref, out_ref):
    out_ref[...] = source_ref[...]


def gate_kernel(ids_ref, gates_ref, gate_ref):
    parts, rows, lanes = gate_ref.shape
    ids = ids_ref[pl.ds(pl.multiple_of(lax.axis_index("gx") * rows, rows), rows), :]
    for s in range(parts):
        gate = jnp.sum(
            jnp.where(ids == (lax.axis_index("gx") ^ s), gates_ref[...], 0.0), axis=1, keepdims=True
        )
        gate_ref[s] = jnp.broadcast_to(gate, (rows, lanes))


def project_kernel(parts, *refs):
    shards, weight_ref = refs[:parts], refs[parts]
    outs, held = refs[parts + 1 : -1], refs[-1]
    rows = shards[0].shape[0]
    turn = lax.axis_index("gx") ^ lax.axis_index("ta")
    block = jnp.concatenate([shard[...] for shard in shards], axis=0)
    pieces = jnp.dot(block, weight_ref[...], preferred_element_type=F32).astype(BF16)
    for s in range(parts):
        held[turn ^ s] = pieces[s * rows : (s + 1) * rows, :]
    for t in range(parts):
        outs[t][...] = held[t]


def add_kernel(*refs):
    terms, out = refs[:-1], refs[-1]
    total = terms[0][...].astype(F32)
    for term in terms[1:]:
        total = total + term[...].astype(F32)
    out[...] = total.astype(BF16)


def norm_kernel(parts, gain_ref, *refs):
    shards, out = refs[:parts], refs[parts]
    width = shards[0].shape[1]
    values = [shard[...].astype(F32) for shard in shards]
    center = sum(jnp.sum(part, axis=1, keepdims=True) for part in values) / out.shape[1]
    values = [part - center for part in values]
    spread = sum(jnp.sum(part * part, axis=1, keepdims=True) for part in values) / out.shape[1]
    scale = lax.rsqrt(spread + 1e-05)
    for s in range(parts):
        here = pl.ds(pl.multiple_of((lax.axis_index("gx") ^ s) * width, HD), width)
        out[:, here] = (values[s] * scale * gain_ref[:, here]).astype(BF16)


def by_distance(pair_ref, second_ref):
    return pair_ref.at[0], second_ref.at[0], pair_ref.at[1], second_ref.at[1]


def load_kernel(rows, source_hbm, out_ref, sem):
    copy = pltpu.make_async_copy(source_hbm.at[pl.ds(0, rows)], out_ref, sem)
    copy.start()
    copy.wait()


def lift_kernel(chunks, *refs):
    count = 2 * chunks
    shards, (up_ref, down_ref, down_hbm) = refs[:count], refs[count : count + 3]
    active_ref, far_ref, close_ref, rest_ref, held, passed, sem = refs[count + 3 :]
    hidden = active_ref.shape[1]
    share = far_ref.shape[2]
    half = far_ref.shape[1]
    rows = shards[0].shape[1]
    cut = down_ref.shape[0]
    copy = pltpu.make_async_copy(down_hbm.at[pl.ds(cut, hidden - cut)], rest_ref, sem)
    copy.start()
    for c in range(chunks):
        for t, shard in enumerate(by_distance(*shards[2 * c : 2 * c + 2])):
            first = pl.multiple_of(((lax.axis_index("ta") ^ t) * chunks + c) * rows, rows)
            held[pl.ds(first, rows), :] = shard[...]
    for first in range(0, hidden, 2 * HD):
        last = min(first + 2 * HD, hidden)
        raised = lax.dot_general(
            up_ref[first:last, :], held[...], (((1,), (1,)), ((), ())), preferred_element_type=F32
        )
        active_ref[:, first:last] = (raised / (1.0 + jnp.exp(-raised))).T.astype(BF16)
    copy.wait()
    mine = lax.axis_index("gx") // 2
    for k in range(2):
        passed[...] = lowered(2 * k + 1, active_ref, down_ref, rest_ref, share).astype(BF16)
        for out_ref, side in ((far_ref, 1 - mine), (close_ref, mine)):
            out_ref[k] = passed[pl.ds(pl.multiple_of(side * half, half), half), :]


def lowered(turn, active_ref, down_ref, rest_ref, share):
    cut = down_ref.shape[0]
    here = pl.ds(pl.multiple_of((lax.axis_index("ta") ^ turn) * share, HD), share)
    return jnp.dot(
        active_ref[:, :cut], down_ref[:, here], preferred_element_type=F32
    ) + jnp.dot(active_ref[:, cut:], rest_ref[:, here], preferred_element_type=F32)


def lower_kernel(turn, active_ref, down_ref, rest_ref, out_ref):
    out_ref[...] = lowered(turn, active_ref, down_ref, rest_ref, out_ref.shape[1])


def turn_kernel(distances, cross_ref, near_ref, *outs):
    rows = outs[0].shape[0]
    for distance, out_ref in zip(distances, outs):
        z = lax.axis_index("gx") ^ distance
        here = pl.ds(pl.multiple_of(z * rows, rows), rows)
        there = pl.ds(pl.multiple_of(z % 2 * rows, rows), rows)
        out_ref[...] = (cross_ref[here, :] + near_ref[1, there, :].astype(F32)).astype(BF16)


def split_kernel(distances, own_ref, near_ref, *refs):
    count = len(distances)
    rows = refs[0].shape[0]
    for distance, crossed_ref, out_ref in zip(distances, refs[:count], refs[count:]):
        z = lax.axis_index("gx") ^ distance
        here = pl.ds(pl.multiple_of(z * rows, rows), rows)
        there = pl.ds(pl.multiple_of(z % 2 * rows, rows), rows)
        total = own_ref[here, :] + near_ref[0, there, :].astype(F32)
        out_ref[...] = (total + crossed_ref[...].astype(F32)).astype(BF16)


def mix_kernel(distances, gate_ref, *refs):
    out = refs[-1]
    lanes = gate_ref.shape[2]
    for begin in range(0, out.shape[1], lanes):
        part = slice(begin, begin + lanes)
        total = sum(
            gate_ref[s] * term[:, part].astype(F32) for s, term in zip(distances, refs)
        )
        for ref in refs[len(distances) : -1]:
            total = total + ref[:, part]
        out[:, part] = total.astype(out.dtype)


def trade(array, axis, turn):
    count = lax.axis_size(axis)
    return lax.ppermute(array, axis, [(k, k ^ turn) for k in range(count)])


def every_row_body(
    queries, new_kv, kv_cache, lengths, out_proj, norm_gain, expert_ids, gate_weights, w_up, w_down
):
    gx_count = lax.axis_size("gx")
    ta_count = lax.axis_size("ta")
    chunks = 2
    block_rows = queries.shape[0]
    rows = block_rows // chunks
    width = out_proj.shape[1]
    model = norm_gain.shape[0]
    hidden_share = w_up.shape[2]
    share = model // ta_count
    all_rows = block_rows * gx_count
    shape = jax.ShapeDtypeStruct
    gain = norm_gain.reshape(1, model)
    heads = queries.shape[1] // HD
    small = beside(queries, new_kv, lengths, kv_cache.shape[2])
    attended = []
    for c in range(chunks):
        after = attended[-1] if attended else small
        attended.append(attend(small, kv_cache, heads, c * rows, rows, after))
    order = [s for s in range(gx_count - 1, 0, -1)]

    def spread(array, axis):
        parts = {0: array, **{s: trade(array, axis, s) for s in order}}
        return [parts[s] for s in range(len(parts))]

    shards = []
    for part in attended:
        one, two = trade(part, "gx", 1), trade(part, "gx", 2)
        onward = local_call(
            pass_kernel, shape(two.shape, BF16), [VMEM], name="pass", after=one
        )(two)
        shards.append([part, one, two, trade(onward, "gx", 1)])

    def project(c, after):
        pieces = local_call(
            functools.partial(project_kernel, gx_count),
            [shape((rows, width), BF16)] * ta_count,
            [VMEM] * (gx_count + 1),
            [pltpu.VMEM((ta_count, rows, width), BF16)],
            name="project",
            after=after,
        )(*shards[c], out_proj)
        return [pieces[0]] + [trade(pieces[t], "ta", t) for t in range(1, ta_count)]

    def close(pieces, after):
        hidden = local_call(
            add_kernel,
            shape((rows, width), BF16),
            [VMEM] * ta_count,
            name="add",
            after=after,
        )(*pieces)
        return spread(hidden, "gx")

    def norm(hidden, after):
        return local_call(
            functools.partial(norm_kernel, gx_count),
            shape((rows, model), BF16),
            [VMEM] * (gx_count + 1),
            name="norm",
            after=after,
        )(gain, *hidden)

    hidden = close(project(0, attended[1]), None)
    pieces = project(1, hidden[0])
    normed = [norm(hidden, pieces[0])]
    hidden = close(pieces, normed[0])
    normed.append(norm(hidden, None))
    pairs = []
    gates = local_call(
        gate_kernel,
        shape((gx_count, block_rows, HD), F32),
        [VMEM, VMEM],
        name="gates",
        after=normed[-1],
    )(expert_ids, gate_weights)
    up = local_call(
        functools.partial(load_kernel, hidden_share),
        shape((hidden_share, model), BF16),
        [ANYWHERE],
        [pltpu.SemaphoreType.DMA],
        vmem=40,
        name="load_up",
        after=gates,
    )(jnp.swapaxes(w_up[0], 0, 1))
    for c in range(chunks):
        pairs.append(
            local_call(
                pair_kernel,
                shape((2, rows, model), BF16),
                [VMEM] * 2,
                name="pair",
                after=pairs[-1] if pairs else up,
            )(normed[c], trade(normed[c], "ta", 2))
        )
    blocks = [block for pair in pairs for block in (pair, trade(pair, "ta", 1))]
    cut = hidden_share // (4 * HD) * 2 * HD
    part = local_call(
        functools.partial(load_kernel, cut),
        shape((cut, model), BF16),
        [ANYWHERE],
        [pltpu.SemaphoreType.DMA],
        vmem=46,
        name="load_down",
        after=pairs[-1],
    )(w_down[0])
    half = all_rows // 2
    active, far, close, rest = local_call(
        functools.partial(lift_kernel, chunks),
        [
            shape((all_rows, hidden_share), BF16),
            shape((2, half, share), BF16),
            shape((2, half, share), BF16),
            shape((hidden_share - cut, model), BF16),
        ],
        [VMEM] * (2 * chunks + 2) + [ANYWHERE],
        [
            pltpu.VMEM((all_rows, model), BF16),
            pltpu.VMEM((all_rows, share), BF16),
            pltpu.SemaphoreType.DMA,
        ],
        vmem=30,
        name="lift",
    )(*blocks, up, part, w_down[0])
    near = {1: trade(far, "ta", 1), 0: trade(close, "ta", 1)}

    def lower(turn, after):
        return local_call(
            functools.partial(lower_kernel, turn),
            shape((all_rows, share), F32),
            [VMEM] * 3,
            name="lower",
            after=after,
        )(active, part, rest)

    def on_rows(kernel, distances, after, *arrays):
        return local_call(
            functools.partial(kernel, distances),
            [shape((block_rows, share), BF16)] * len(distances),
            [VMEM] * len(arrays),
            name=kernel.__name__[:-7],
            after=after,
        )(*arrays)

    cross = lower(2, None)
    groups = ((3,), (2,), (1, 0))
    turned = [cross]
    crossed = {}
    for distances in groups:
        sums = on_rows(turn_kernel, distances, turned[0], cross, near[distances[0] // 2])
        turned = sums
        crossed.update({s: trade(part, "ta", 2) for s, part in zip(distances, sums)})
    own = lower(0, turned[0])
    gathered, total, after = {}, [], None
    for distances in groups:
        terms = on_rows(
            split_kernel, distances, after, own, near[distances[0] // 2],
            *[crossed[s] for s in distances],
        )
        after = terms[0]
        for s, term in zip(distances, terms):
            gathered[s] = trade(term, "gx", s) if s else term
    for distances in groups:
        last = 0 in distances
        total = [
            local_call(
                functools.partial(mix_kernel, distances),
                shape((block_rows, share), BF16 if last else F32),
                [VMEM] * (1 + len(distances) + len(total)),
                name="mix",
                cost=1024 if last else MIX_COST,
            )(gates, *[gathered[s] for s in distances], *total)
        ]
    return total[0]


def route_tables(expert_ids, expert_count, block_rows, capacity):
    blocks = expert_ids.shape[0] // block_rows
    expert_range = jnp.arange(expert_count, dtype=jnp.int32)
    matches = (expert_ids[:, :, None] == expert_range[None, None, :]).astype(jnp.int32)
    routed = jnp.sum(matches, axis=1).reshape(blocks, block_rows, expert_count)
    position = jnp.cumsum(routed, axis=1) - routed
    slot_range = jnp.arange(capacity, dtype=jnp.int32)
    slot_hits = routed[:, :, :, None] * (
        position[:, :, :, None] == slot_range[None, None, None, :]
    ).astype(jnp.int32)
    row_range = jnp.arange(block_rows, dtype=jnp.int32)
    block_start = (jnp.arange(blocks, dtype=jnp.int32) * block_rows)[:, None, None]
    source_row = jnp.sum(slot_hits * row_range[None, :, None, None], axis=1) + block_start
    filled = jnp.sum(slot_hits, axis=1)
    source_row = jnp.transpose(source_row, (1, 0, 2)).reshape(expert_count, blocks * capacity)
    filled = jnp.transpose(filled, (1, 0, 2)).reshape(expert_count, blocks * capacity)
    pick_slot = jnp.sum(matches * position.reshape(blocks * block_rows, 1, expert_count), axis=2)
    return (source_row, filled, pick_slot)


def layer_norm(hidden, norm_gain):
    values = hidden.astype(jnp.float32)
    center = values - jnp.mean(values, axis=1, keepdims=True)
    spread = jnp.mean(center * center, axis=1, keepdims=True)
    return (center * lax.rsqrt(spread + 1e-05) * norm_gain).astype(jnp.bfloat16)


def body(
    queries, new_kv, kv_cache, lengths, out_proj, norm_gain, expert_ids, gate_weights, w_up, w_down
):
    gx_count = lax.axis_size("gx")
    ta_count = lax.axis_size("ta")
    block_rows = queries.shape[0]
    top_count = expert_ids.shape[1]
    capacity = min(block_rows, 2 * block_rows * top_count // gx_count)
    slot_count = gx_count * capacity
    model_width = norm_gain.shape[0]
    width_share = model_width // ta_count
    if gx_count == top_count and ta_count == gx_count == 4:
        return every_row_body(
            queries, new_kv, kv_cache, lengths, out_proj, norm_gain, expert_ids, gate_weights,
            w_up, w_down,
        )
    small = beside(queries, new_kv, lengths, kv_cache.shape[2])
    attended = attend(small, kv_cache, queries.shape[1] // HD, 0, block_rows, small)
    projected = jnp.dot(
        lax.all_gather(attended, "gx", axis=0, tiled=True),
        out_proj,
        preferred_element_type=jnp.float32,
    ).astype(jnp.bfloat16)
    source_row, filled, pick_slot = route_tables(expert_ids, gx_count, block_rows, capacity)
    live_slots = (filled > 0)[:, :, None]
    widened = lax.optimization_barrier(projected).astype(jnp.float32)
    hidden_share = lax.psum_scatter(
        widened.astype(jnp.bfloat16), "ta", scatter_dimension=1, tiled=True
    )
    outgoing = jnp.where(live_slots, hidden_share[source_row], jnp.zeros((), jnp.bfloat16))[
        :, :, None, :
    ]
    arrived = lax.all_to_all(outgoing, "gx", split_axis=0, concat_axis=2, tiled=True)
    gathered = lax.all_gather(arrived, "ta", axis=3, tiled=True)
    hidden = gathered.reshape(slot_count, model_width)
    normed = layer_norm(hidden, norm_gain)
    raised = jnp.dot(normed, w_up[0], preferred_element_type=jnp.float32)
    active = jax.nn.silu(raised).astype(jnp.bfloat16)
    terms = jnp.dot(active, w_down[0], preferred_element_type=jnp.float32)
    mine = lax.psum_scatter(terms, "ta", scatter_dimension=1, tiled=True)
    result = mine.astype(jnp.bfloat16).reshape(gx_count, capacity, width_share)
    returned = lax.all_to_all(result, "gx", split_axis=0, concat_axis=0, tiled=True)
    first_row = lax.axis_index("gx") * block_rows
    local_ids = lax.dynamic_slice_in_dim(expert_ids, first_row, block_rows, 0)
    local_slot = lax.dynamic_slice_in_dim(pick_slot, first_row, block_rows, 0)
    flat_rows = returned.reshape(gx_count * capacity, width_share)
    picked = flat_rows[local_ids * capacity + local_slot]
    return jnp.sum(picked.astype(jnp.float32) * gate_weights[:, :, None], axis=1).astype(
        jnp.bfloat16
    )


def solution(mesh):
    return jax.shard_map(
        body,
        mesh=mesh,
        in_specs=(
            P(("groups", "gx"), "ta"),
            P(None, ("groups", "gx"), "ta"),
            P(None, ("groups", "gx"), None, "ta"),
            P(("groups", "gx")),
            P("ta", "gx"),
            P(),
            P("groups", None),
            P(("groups", "gx"), None),
            P("gx", None, "ta"),
            P("gx", "ta", None),
        ),
        out_specs=P(("groups", "gx"), "ta"),
        check_vma=False,
    )
```

```python
import functools
import math

import jax
import jax.numpy as jnp
from jax import lax
from jax.experimental import pallas as pl
from jax.experimental.pallas import tpu as pltpu
from jax.sharding import PartitionSpec as P

HD = 128
MIB = 1 << 20
MIX_COST = 1 << 22
PROJECT_COST = 1 << 21
VMEM = pl.BlockSpec(memory_space=pltpu.VMEM)
F32 = jnp.float32
BF16 = jnp.bfloat16


ANYWHERE = pl.BlockSpec(memory_space=pl.ANY)


def local_call(kernel, out_shape, in_specs, scratch=(), vmem=8, name=None, after=None, cost=1024):
    several = isinstance(out_shape, (tuple, list))
    if after is not None:
        count, inner = len(in_specs), kernel
        in_specs = [*in_specs, ANYWHERE]
        kernel = lambda *refs: inner(*refs[:count], *refs[count + 1 :])
    call = pl.pallas_call(
        kernel,
        out_shape=out_shape,
        in_specs=in_specs,
        out_specs=[VMEM] * len(out_shape) if several else VMEM,
        scratch_shapes=list(scratch),
        compiler_params=pltpu.CompilerParams(vmem_limit_bytes=vmem * MIB),
        cost_estimate=pl.CostEstimate(flops=1024, bytes_accessed=cost, transcendentals=0),
        name=name,
    )
    return call if after is None else lambda *args: call(*args, after)


def attend_kernel(
    kv_heads, group, slots, batch, begin,
    small_ref, cache_ref, after_ref, out_ref,
    keys, values, q_rows, scores, own_scores, probs, own_probs, mixed, sems,
):
    rows = out_ref.shape[0]
    context = keys.shape[1]
    width = kv_heads * HD
    heads = kv_heads * group
    steps = rows // batch
    scale = 1.0 / math.sqrt(HD)
    fresh = [slice(heads * HD + k * width, heads * HD + (k + 1) * width) for k in range(2)]
    spans = slice(heads * HD + 2 * width, heads * HD + 2 * width + context)

    def fetch(step, kind):
        buffer = (keys, values)[kind]
        return pltpu.make_async_copy(
            cache_ref.at[kind, pl.ds(begin + step * batch, batch)],
            buffer.at[pl.ds(step * batch, batch)],
            sems.at[kind, step],
        )

    for step in range(steps):
        for kind in range(2):
            fetch(step, kind).start()
    q_rows[...] = jnp.zeros_like(q_rows)
    for head in range(heads):
        q_rows[head // group, pl.ds(head, rows, stride=slots), :] = small_ref[
            begin : begin + rows, head * HD : (head + 1) * HD
        ].astype(F32)
    place = lax.broadcasted_iota(jnp.int32, (slots, context), 1).astype(F32)
    for step in range(steps):
        fetch(step, 0).wait()
        for k in range(batch):
            row = step * batch + k
            whole = slice(begin + row, begin + row + 1)
            mine = jnp.concatenate(
                [q_rows[g, row * slots : (row + 1) * slots, :] for g in range(kv_heads)], axis=1
            )
            cached = lax.dot_general(
                mine.astype(BF16), keys[row], (((1,), (1,)), ((), ())),
                preferred_element_type=F32,
            )
            here = slice(k * slots, (k + 1) * slots)
            seen = place < small_ref[whole, spans].astype(F32)
            scores[here, :] = jnp.where(seen, cached * scale, -jnp.inf)
            fresh_key = small_ref[whole, fresh[0]].astype(F32)
            own_scores[here, :] = jnp.broadcast_to(
                jnp.sum(mine * fresh_key, axis=1, keepdims=True) * scale, (slots, HD)
            )
        cached = scores[...]
        own = own_scores[:, :1]
        largest = jnp.maximum(jnp.max(cached, axis=1, keepdims=True), own)
        lifted = jnp.exp(cached - largest)
        own_lifted = jnp.exp(own - largest)
        total = jnp.sum(lifted, axis=1, keepdims=True) + own_lifted
        probs[...] = (lifted / total).astype(BF16)
        own_probs[...] = jnp.broadcast_to(
            (own_lifted / total).astype(BF16).astype(F32), own_probs.shape
        )
        fetch(step, 1).wait()
        for k in range(batch):
            row = step * batch + k
            whole = slice(begin + row, begin + row + 1)
            here = slice(k * slots, (k + 1) * slots)
            weighted = jnp.dot(probs[here, :], values[row], preferred_element_type=F32)
            fresh_value = small_ref[whole, fresh[1]].astype(F32)
            total = weighted + own_probs[here, :1] * fresh_value
            for g in range(kv_heads):
                mixed[g, here, :] = total[:, g * HD : (g + 1) * HD]
        for head in range(heads):
            out_ref[step * batch : (step + 1) * batch, head * HD : (head + 1) * HD] = mixed[
                head // group, pl.ds(head, batch, stride=slots), :
            ].astype(BF16)


def beside(queries, new_kv, lengths, context):
    lanes = -(-context // HD) * HD
    spans = jnp.broadcast_to(lengths.astype(BF16)[:, None], (lengths.shape[0], lanes))
    return jnp.concatenate([queries, new_kv[0], new_kv[1], spans], axis=1)


def attend(small, kv_cache, heads, begin, rows, after):
    context, width = kv_cache.shape[2:]
    kv_heads = width // HD
    slots = -(-heads // 8) * 8
    batch = 16
    shape = jax.ShapeDtypeStruct((rows, heads * HD), BF16)
    return pl.pallas_call(
        functools.partial(attend_kernel, kv_heads, heads // kv_heads, slots, batch, begin),
        out_shape=shape,
        in_specs=[VMEM, ANYWHERE, ANYWHERE],
        out_specs=VMEM,
        scratch_shapes=[
            pltpu.VMEM((rows, context, width), BF16),
            pltpu.VMEM((rows, context, width), BF16),
            pltpu.VMEM((kv_heads, rows * slots, HD), F32),
            pltpu.VMEM((batch * slots, context), F32),
            pltpu.VMEM((batch * slots, HD), F32),
            pltpu.VMEM((batch * slots, context), BF16),
            pltpu.VMEM((batch * slots, HD), F32),
            pltpu.VMEM((kv_heads, batch * slots, HD), F32),
            pltpu.SemaphoreType.DMA((2, rows // batch)),
        ],
        compiler_params=pltpu.CompilerParams(vmem_limit_bytes=50 * MIB),
        cost_estimate=pl.CostEstimate(flops=1024, bytes_accessed=1024, transcendentals=0),
        name="attend",
    )(small, kv_cache, after)


def pair_kernel(own_ref, other_ref, out_ref):
    out_ref[0] = own_ref[...]
    out_ref[1] = other_ref[...]


def gate_kernel(ids_ref, gates_ref, gate_ref):
    parts, rows, lanes = gate_ref.shape
    ids = ids_ref[pl.ds(pl.multiple_of(lax.axis_index("gx") * rows, rows), rows), :]
    for s in range(parts):
        gate = jnp.sum(
            jnp.where(ids == (lax.axis_index("gx") ^ s), gates_ref[...], 0.0), axis=1, keepdims=True
        )
        gate_ref[s] = jnp.broadcast_to(gate, (rows, lanes))


def project_kernel(parts, *refs):
    shards, weight_ref = refs[:parts], refs[parts]
    outs, held = refs[parts + 1 : -1], refs[-1]
    rows = shards[0].shape[0]
    turn = lax.axis_index("gx") ^ lax.axis_index("ta")
    block = jnp.concatenate([shard[...] for shard in shards], axis=0)
    pieces = jnp.dot(block, weight_ref[...], preferred_element_type=F32).astype(BF16)
    for s in range(parts):
        held[turn ^ s] = pieces[s * rows : (s + 1) * rows, :]
    for t in range(parts):
        outs[t][...] = held[t]


def add_kernel(*refs):
    terms, out = refs[:-1], refs[-1]
    total = terms[0][...].astype(F32)
    for term in terms[1:]:
        total = total + term[...].astype(F32)
    out[...] = total.astype(BF16)


def norm_kernel(parts, gain_ref, *refs):
    shards, out = refs[:parts], refs[parts]
    width = shards[0].shape[1]
    values = [shard[...].astype(F32) for shard in shards]
    center = sum(jnp.sum(part, axis=1, keepdims=True) for part in values) / out.shape[1]
    values = [part - center for part in values]
    spread = sum(jnp.sum(part * part, axis=1, keepdims=True) for part in values) / out.shape[1]
    scale = lax.rsqrt(spread + 1e-05)
    for s in range(parts):
        here = pl.ds(pl.multiple_of((lax.axis_index("gx") ^ s) * width, HD), width)
        out[:, here] = (values[s] * scale * gain_ref[:, here]).astype(BF16)


def by_distance(pair_ref, second_ref):
    return pair_ref.at[0], second_ref.at[0], pair_ref.at[1], second_ref.at[1]


def load_kernel(rows, source_hbm, out_ref, sem):
    copy = pltpu.make_async_copy(source_hbm.at[pl.ds(0, rows)], out_ref, sem)
    copy.start()
    copy.wait()


def lift_kernel(chunks, *refs):
    count = 2 * chunks
    shards, (up_ref, down_ref, down_hbm) = refs[:count], refs[count : count + 3]
    active_ref, far_ref, close_ref, rest_ref, held, passed, sem = refs[count + 3 :]
    hidden = active_ref.shape[1]
    share = far_ref.shape[2]
    half = far_ref.shape[1]
    rows = shards[0].shape[1]
    cut = down_ref.shape[0]
    copy = pltpu.make_async_copy(down_hbm.at[pl.ds(cut, hidden - cut)], rest_ref, sem)
    copy.start()
    for c in range(chunks):
        for t, shard in enumerate(by_distance(*shards[2 * c : 2 * c + 2])):
            first = pl.multiple_of(((lax.axis_index("ta") ^ t) * chunks + c) * rows, rows)
            held[pl.ds(first, rows), :] = shard[...]
    for first in range(0, hidden, 2 * HD):
        last = min(first + 2 * HD, hidden)
        raised = lax.dot_general(
            up_ref[first:last, :], held[...], (((1,), (1,)), ((), ())), preferred_element_type=F32
        )
        active_ref[:, first:last] = (raised / (1.0 + jnp.exp(-raised))).T.astype(BF16)
    copy.wait()
    mine = lax.axis_index("gx") // 2
    for k in range(2):
        passed[...] = lowered(2 * k + 1, active_ref, down_ref, rest_ref, share).astype(BF16)
        for out_ref, side in ((far_ref, 1 - mine), (close_ref, mine)):
            out_ref[k] = passed[pl.ds(pl.multiple_of(side * half, half), half), :]


def lowered(turn, active_ref, down_ref, rest_ref, share):
    cut = down_ref.shape[0]
    here = pl.ds(pl.multiple_of((lax.axis_index("ta") ^ turn) * share, HD), share)
    return jnp.dot(
        active_ref[:, :cut], down_ref[:, here], preferred_element_type=F32
    ) + jnp.dot(active_ref[:, cut:], rest_ref[:, here], preferred_element_type=F32)


def lower_kernel(turn, active_ref, down_ref, rest_ref, out_ref):
    out_ref[...] = lowered(turn, active_ref, down_ref, rest_ref, out_ref.shape[1])


def turn_kernel(distances, cross_ref, near_ref, *outs):
    rows = outs[0].shape[0]
    for distance, out_ref in zip(distances, outs):
        z = lax.axis_index("gx") ^ distance
        here = pl.ds(pl.multiple_of(z * rows, rows), rows)
        there = pl.ds(pl.multiple_of(z % 2 * rows, rows), rows)
        out_ref[...] = (cross_ref[here, :] + near_ref[1, there, :].astype(F32)).astype(BF16)


def split_kernel(distances, own_ref, near_ref, *refs):
    count = len(distances)
    rows = refs[0].shape[0]
    for distance, crossed_ref, out_ref in zip(distances, refs[:count], refs[count:]):
        z = lax.axis_index("gx") ^ distance
        here = pl.ds(pl.multiple_of(z * rows, rows), rows)
        there = pl.ds(pl.multiple_of(z % 2 * rows, rows), rows)
        total = own_ref[here, :] + near_ref[0, there, :].astype(F32)
        out_ref[...] = (total + crossed_ref[...].astype(F32)).astype(BF16)


def mix_kernel(distances, gate_ref, *refs):
    out = refs[-1]
    lanes = gate_ref.shape[2]
    for begin in range(0, out.shape[1], lanes):
        part = slice(begin, begin + lanes)
        total = sum(
            gate_ref[s] * term[:, part].astype(F32) for s, term in zip(distances, refs)
        )
        for ref in refs[len(distances) : -1]:
            total = total + ref[:, part]
        out[:, part] = total.astype(out.dtype)


def trade(array, axis, turn):
    count = lax.axis_size(axis)
    return lax.ppermute(array, axis, [(k, k ^ turn) for k in range(count)])


def every_row_body(
    queries, new_kv, kv_cache, lengths, out_proj, norm_gain, expert_ids, gate_weights, w_up, w_down
):
    gx_count = lax.axis_size("gx")
    ta_count = lax.axis_size("ta")
    chunks = 2
    block_rows = queries.shape[0]
    rows = block_rows // chunks
    width = out_proj.shape[1]
    model = norm_gain.shape[0]
    hidden_share = w_up.shape[2]
    share = model // ta_count
    all_rows = block_rows * gx_count
    shape = jax.ShapeDtypeStruct
    gain = norm_gain.reshape(1, model)
    heads = queries.shape[1] // HD
    small = beside(queries, new_kv, lengths, kv_cache.shape[2])
    attended = []
    for c in range(chunks):
        after = attended[-1] if attended else small
        attended.append(attend(small, kv_cache, heads, c * rows, rows, after))
    order = [s for s in range(gx_count - 1, 0, -1)]

    def spread(array, axis):
        parts = {0: array, **{s: trade(array, axis, s) for s in order}}
        return [parts[s] for s in range(len(parts))]

    shards = [spread(part, "gx") for part in attended]
    pieces, hidden = [], []
    for c in range(chunks):
        pieces.append(
            local_call(
                functools.partial(project_kernel, gx_count),
                [shape((rows, width), BF16)] * ta_count,
                [VMEM] * (gx_count + 1),
                [pltpu.VMEM((ta_count, rows, width), BF16)],
                name="project",
                after=pieces[-1][0] if pieces else attended[-1],
                cost=PROJECT_COST,
            )(*shards[c], out_proj)
        )
    for c in range(chunks):
        parts = [pieces[c][0]] + [trade(pieces[c][t], "ta", t) for t in range(1, ta_count)]
        hidden.append(
            local_call(
                add_kernel,
                shape((rows, width), BF16),
                [VMEM] * ta_count,
                name="add",
                after=hidden[-1] if hidden else pieces[-1][0],
            )(*parts)
        )
    shards = [spread(part, "gx") for part in hidden]
    normed, pairs = [], []
    for c in range(chunks):
        normed.append(
            local_call(
                functools.partial(norm_kernel, gx_count),
                shape((rows, model), BF16),
                [VMEM] * (gx_count + 1),
                name="norm",
                after=normed[-1] if normed else hidden[-1],
            )(gain, *shards[c])
        )
    gates = local_call(
        gate_kernel,
        shape((gx_count, block_rows, HD), F32),
        [VMEM, VMEM],
        name="gates",
        after=normed[-1],
    )(expert_ids, gate_weights)
    up = local_call(
        functools.partial(load_kernel, hidden_share),
        shape((hidden_share, model), BF16),
        [ANYWHERE],
        [pltpu.SemaphoreType.DMA],
        vmem=40,
        name="load_up",
        after=gates,
    )(jnp.swapaxes(w_up[0], 0, 1))
    for c in range(chunks):
        pairs.append(
            local_call(
                pair_kernel,
                shape((2, rows, model), BF16),
                [VMEM] * 2,
                name="pair",
                after=pairs[-1] if pairs else up,
            )(normed[c], trade(normed[c], "ta", 2))
        )
    blocks = [block for pair in pairs for block in (pair, trade(pair, "ta", 1))]
    cut = hidden_share // (4 * HD) * 2 * HD
    part = local_call(
        functools.partial(load_kernel, cut),
        shape((cut, model), BF16),
        [ANYWHERE],
        [pltpu.SemaphoreType.DMA],
        vmem=46,
        name="load_down",
        after=pairs[-1],
    )(w_down[0])
    half = all_rows // 2
    active, far, close, rest = local_call(
        functools.partial(lift_kernel, chunks),
        [
            shape((all_rows, hidden_share), BF16),
            shape((2, half, share), BF16),
            shape((2, half, share), BF16),
            shape((hidden_share - cut, model), BF16),
        ],
        [VMEM] * (2 * chunks + 2) + [ANYWHERE],
        [
            pltpu.VMEM((all_rows, model), BF16),
            pltpu.VMEM((all_rows, share), BF16),
            pltpu.SemaphoreType.DMA,
        ],
        vmem=30,
        name="lift",
    )(*blocks, up, part, w_down[0])
    near = {1: trade(far, "ta", 1), 0: trade(close, "ta", 1)}

    def lower(turn, after):
        return local_call(
            functools.partial(lower_kernel, turn),
            shape((all_rows, share), F32),
            [VMEM] * 3,
            name="lower",
            after=after,
        )(active, part, rest)

    def on_rows(kernel, distances, after, *arrays):
        return local_call(
            functools.partial(kernel, distances),
            [shape((block_rows, share), BF16)] * len(distances),
            [VMEM] * len(arrays),
            name=kernel.__name__[:-7],
            after=after,
        )(*arrays)

    gathered = {}

    def turn(distances, after):
        sums = on_rows(turn_kernel, distances, after, cross, near[distances[0] // 2])
        return sums, [trade(part, "ta", 2) for part in sums]

    def split(distances, after, crossed):
        terms = on_rows(split_kernel, distances, after, own, near[distances[0] // 2], *crossed)
        for s, term in zip(distances, terms):
            gathered[s] = trade(term, "gx", s) if s else term
        return terms

    def mix(distances, after, earlier, kind=F32):
        return local_call(
            functools.partial(mix_kernel, distances),
            shape((block_rows, share), kind),
            [VMEM] * (1 + len(distances) + len(earlier)),
            name="mix",
            after=after,
            cost=1024 if kind == BF16 else MIX_COST,
        )(gates, *[gathered[s] for s in distances], *earlier)

    cross = lower(2, None)
    sums, first = turn((3,), None)
    sums, second = turn((2,), sums[0])
    own = lower(0, sums[0])
    terms = split((3,), None, first)
    sums, third = turn((1, 0), terms[0])
    terms = split((2,), sums[0], second)
    partial = mix((3,), terms[0], [])
    split((1, 0), partial, third)
    partial = mix((2,), None, [partial])
    return mix((1, 0), None, [partial], BF16)


def route_tables(expert_ids, expert_count, block_rows, capacity):
    blocks = expert_ids.shape[0] // block_rows
    expert_range = jnp.arange(expert_count, dtype=jnp.int32)
    matches = (expert_ids[:, :, None] == expert_range[None, None, :]).astype(jnp.int32)
    routed = jnp.sum(matches, axis=1).reshape(blocks, block_rows, expert_count)
    position = jnp.cumsum(routed, axis=1) - routed
    slot_range = jnp.arange(capacity, dtype=jnp.int32)
    slot_hits = routed[:, :, :, None] * (
        position[:, :, :, None] == slot_range[None, None, None, :]
    ).astype(jnp.int32)
    row_range = jnp.arange(block_rows, dtype=jnp.int32)
    block_start = (jnp.arange(blocks, dtype=jnp.int32) * block_rows)[:, None, None]
    source_row = jnp.sum(slot_hits * row_range[None, :, None, None], axis=1) + block_start
    filled = jnp.sum(slot_hits, axis=1)
    source_row = jnp.transpose(source_row, (1, 0, 2)).reshape(expert_count, blocks * capacity)
    filled = jnp.transpose(filled, (1, 0, 2)).reshape(expert_count, blocks * capacity)
    pick_slot = jnp.sum(matches * position.reshape(blocks * block_rows, 1, expert_count), axis=2)
    return (source_row, filled, pick_slot)


def layer_norm(hidden, norm_gain):
    values = hidden.astype(jnp.float32)
    center = values - jnp.mean(values, axis=1, keepdims=True)
    spread = jnp.mean(center * center, axis=1, keepdims=True)
    return (center * lax.rsqrt(spread + 1e-05) * norm_gain).astype(jnp.bfloat16)


def body(
    queries, new_kv, kv_cache, lengths, out_proj, norm_gain, expert_ids, gate_weights, w_up, w_down
):
    gx_count = lax.axis_size("gx")
    ta_count = lax.axis_size("ta")
    block_rows = queries.shape[0]
    top_count = expert_ids.shape[1]
    capacity = min(block_rows, 2 * block_rows * top_count // gx_count)
    slot_count = gx_count * capacity
    model_width = norm_gain.shape[0]
    width_share = model_width // ta_count
    if gx_count == top_count and ta_count == gx_count == 4:
        return every_row_body(
            queries, new_kv, kv_cache, lengths, out_proj, norm_gain, expert_ids, gate_weights,
            w_up, w_down,
        )
    small = beside(queries, new_kv, lengths, kv_cache.shape[2])
    attended = attend(small, kv_cache, queries.shape[1] // HD, 0, block_rows, small)
    projected = jnp.dot(
        lax.all_gather(attended, "gx", axis=0, tiled=True),
        out_proj,
        preferred_element_type=jnp.float32,
    ).astype(jnp.bfloat16)
    source_row, filled, pick_slot = route_tables(expert_ids, gx_count, block_rows, capacity)
    live_slots = (filled > 0)[:, :, None]
    widened = lax.optimization_barrier(projected).astype(jnp.float32)
    hidden_share = lax.psum_scatter(
        widened.astype(jnp.bfloat16), "ta", scatter_dimension=1, tiled=True
    )
    outgoing = jnp.where(live_slots, hidden_share[source_row], jnp.zeros((), jnp.bfloat16))[
        :, :, None, :
    ]
    arrived = lax.all_to_all(outgoing, "gx", split_axis=0, concat_axis=2, tiled=True)
    gathered = lax.all_gather(arrived, "ta", axis=3, tiled=True)
    hidden = gathered.reshape(slot_count, model_width)
    normed = layer_norm(hidden, norm_gain)
    raised = jnp.dot(normed, w_up[0], preferred_element_type=jnp.float32)
    active = jax.nn.silu(raised).astype(jnp.bfloat16)
    terms = jnp.dot(active, w_down[0], preferred_element_type=jnp.float32)
    mine = lax.psum_scatter(terms, "ta", scatter_dimension=1, tiled=True)
    result = mine.astype(jnp.bfloat16).reshape(gx_count, capacity, width_share)
    returned = lax.all_to_all(result, "gx", split_axis=0, concat_axis=0, tiled=True)
    first_row = lax.axis_index("gx") * block_rows
    local_ids = lax.dynamic_slice_in_dim(expert_ids, first_row, block_rows, 0)
    local_slot = lax.dynamic_slice_in_dim(pick_slot, first_row, block_rows, 0)
    flat_rows = returned.reshape(gx_count * capacity, width_share)
    picked = flat_rows[local_ids * capacity + local_slot]
    return jnp.sum(picked.astype(jnp.float32) * gate_weights[:, :, None], axis=1).astype(
        jnp.bfloat16
    )


def solution(mesh):
    return jax.shard_map(
        body,
        mesh=mesh,
        in_specs=(
            P(("groups", "gx"), "ta"),
            P(None, ("groups", "gx"), "ta"),
            P(None, ("groups", "gx"), None, "ta"),
            P(("groups", "gx")),
            P("ta", "gx"),
            P(),
            P("groups", None),
            P(("groups", "gx"), None),
            P("gx", None, "ta"),
            P("gx", "ta", None),
        ),
        out_specs=P(("groups", "gx"), "ta"),
        check_vma=False,
    )
```

```python
import functools
import math

import jax
import jax.numpy as jnp
from jax import lax
from jax.experimental import pallas as pl
from jax.experimental.pallas import tpu as pltpu
from jax.sharding import PartitionSpec as P

HD = 128
MIB = 1 << 20
MIX_COST = 1 << 22
PROJECT_COST = 1 << 21
VMEM = pl.BlockSpec(memory_space=pltpu.VMEM)
F32 = jnp.float32
BF16 = jnp.bfloat16


ANYWHERE = pl.BlockSpec(memory_space=pl.ANY)


def local_call(kernel, out_shape, in_specs, scratch=(), vmem=8, name=None, after=None, cost=1024):
    several = isinstance(out_shape, (tuple, list))
    if after is not None:
        count, inner = len(in_specs), kernel
        in_specs = [*in_specs, ANYWHERE]
        kernel = lambda *refs: inner(*refs[:count], *refs[count + 1 :])
    call = pl.pallas_call(
        kernel,
        out_shape=out_shape,
        in_specs=in_specs,
        out_specs=[VMEM] * len(out_shape) if several else VMEM,
        scratch_shapes=list(scratch),
        compiler_params=pltpu.CompilerParams(vmem_limit_bytes=vmem * MIB),
        cost_estimate=pl.CostEstimate(flops=1024, bytes_accessed=cost, transcendentals=0),
        name=name,
    )
    return call if after is None else lambda *args: call(*args, after)


def attend_kernel(
    kv_heads, group, slots, batch, begin,
    small_ref, cache_ref, after_ref, out_ref,
    keys, values, q_rows, scores, own_scores, probs, own_probs, mixed, sems,
):
    rows = out_ref.shape[0]
    context = keys.shape[1]
    width = kv_heads * HD
    heads = kv_heads * group
    steps = rows // batch
    scale = 1.0 / math.sqrt(HD)
    fresh = [slice(heads * HD + k * width, heads * HD + (k + 1) * width) for k in range(2)]
    spans = slice(heads * HD + 2 * width, heads * HD + 2 * width + context)

    def fetch(step, kind):
        buffer = (keys, values)[kind]
        return pltpu.make_async_copy(
            cache_ref.at[kind, pl.ds(begin + step * batch, batch)],
            buffer.at[pl.ds(step * batch, batch)],
            sems.at[kind, step],
        )

    for kind in range(2):
        for step in range(steps):
            fetch(step, kind).start()
    q_rows[...] = jnp.zeros_like(q_rows)
    for head in range(heads):
        q_rows[head // group, pl.ds(head, rows, stride=slots), :] = small_ref[
            begin : begin + rows, head * HD : (head + 1) * HD
        ].astype(F32)
    place = lax.broadcasted_iota(jnp.int32, (slots, context), 1).astype(F32)

    def score(step):
        fetch(step, 0).wait()
        for k in range(batch):
            row = step * batch + k
            whole = slice(begin + row, begin + row + 1)
            mine = jnp.concatenate(
                [q_rows[g, row * slots : (row + 1) * slots, :] for g in range(kv_heads)], axis=1
            )
            cached = lax.dot_general(
                mine.astype(BF16), keys[row], (((1,), (1,)), ((), ())),
                preferred_element_type=F32,
            )
            here = slice(k * slots, (k + 1) * slots)
            seen = place < small_ref[whole, spans].astype(F32)
            scores[step % 2, here, :] = jnp.where(seen, cached * scale, -jnp.inf)
            fresh_key = small_ref[whole, fresh[0]].astype(F32)
            own_scores[step % 2, here, :] = jnp.broadcast_to(
                jnp.sum(mine * fresh_key, axis=1, keepdims=True) * scale, (slots, HD)
            )

    score(0)
    for step in range(steps):
        if step + 1 < steps:
            score(step + 1)
        cached = scores[step % 2]
        own = own_scores[step % 2, :, :1]
        largest = jnp.maximum(jnp.max(cached, axis=1, keepdims=True), own)
        lifted = jnp.exp(cached - largest)
        own_lifted = jnp.exp(own - largest)
        total = jnp.sum(lifted, axis=1, keepdims=True) + own_lifted
        probs[step % 2] = (lifted / total).astype(BF16)
        own_probs[step % 2] = jnp.broadcast_to(
            (own_lifted / total).astype(BF16).astype(F32), own_probs.shape[1:]
        )
        fetch(step, 1).wait()
        for k in range(batch):
            row = step * batch + k
            whole = slice(begin + row, begin + row + 1)
            here = slice(k * slots, (k + 1) * slots)
            weighted = jnp.dot(probs[step % 2, here, :], values[row], preferred_element_type=F32)
            fresh_value = small_ref[whole, fresh[1]].astype(F32)
            total = weighted + own_probs[step % 2, here, :1] * fresh_value
            for g in range(kv_heads):
                mixed[step % 2, g, here, :] = total[:, g * HD : (g + 1) * HD]
        for head in range(heads):
            out_ref[step * batch : (step + 1) * batch, head * HD : (head + 1) * HD] = mixed[
                step % 2, head // group, pl.ds(head, batch, stride=slots), :
            ].astype(BF16)


def beside(queries, new_kv, lengths, context):
    lanes = -(-context // HD) * HD
    spans = jnp.broadcast_to(lengths.astype(BF16)[:, None], (lengths.shape[0], lanes))
    return jnp.concatenate([queries, new_kv[0], new_kv[1], spans], axis=1)


def attend(small, kv_cache, heads, begin, rows, after):
    context, width = kv_cache.shape[2:]
    kv_heads = width // HD
    slots = -(-heads // 8) * 8
    batch = 16
    shape = jax.ShapeDtypeStruct((rows, heads * HD), BF16)
    return pl.pallas_call(
        functools.partial(attend_kernel, kv_heads, heads // kv_heads, slots, batch, begin),
        out_shape=shape,
        in_specs=[VMEM, ANYWHERE, ANYWHERE],
        out_specs=VMEM,
        scratch_shapes=[
            pltpu.VMEM((rows, context, width), BF16),
            pltpu.VMEM((rows, context, width), BF16),
            pltpu.VMEM((kv_heads, rows * slots, HD), F32),
            pltpu.VMEM((2, batch * slots, context), F32),
            pltpu.VMEM((2, batch * slots, HD), F32),
            pltpu.VMEM((2, batch * slots, context), BF16),
            pltpu.VMEM((2, batch * slots, HD), F32),
            pltpu.VMEM((2, kv_heads, batch * slots, HD), F32),
            pltpu.SemaphoreType.DMA((2, rows // batch)),
        ],
        compiler_params=pltpu.CompilerParams(vmem_limit_bytes=50 * MIB),
        cost_estimate=pl.CostEstimate(flops=1024, bytes_accessed=1024, transcendentals=0),
        name="attend",
    )(small, kv_cache, after)


def pair_kernel(own_ref, other_ref, out_ref):
    out_ref[0] = own_ref[...]
    out_ref[1] = other_ref[...]


def gate_kernel(ids_ref, gates_ref, gate_ref):
    parts, rows, lanes = gate_ref.shape
    ids = ids_ref[pl.ds(pl.multiple_of(lax.axis_index("gx") * rows, rows), rows), :]
    for s in range(parts):
        gate = jnp.sum(
            jnp.where(ids == (lax.axis_index("gx") ^ s), gates_ref[...], 0.0), axis=1, keepdims=True
        )
        gate_ref[s] = jnp.broadcast_to(gate, (rows, lanes))


def project_kernel(parts, *refs):
    shards, weight_ref = refs[:parts], refs[parts]
    outs, held = refs[parts + 1 : -1], refs[-1]
    rows = shards[0].shape[0]
    turn = lax.axis_index("gx") ^ lax.axis_index("ta")
    block = jnp.concatenate([shard[...] for shard in shards], axis=0)
    pieces = jnp.dot(block, weight_ref[...], preferred_element_type=F32).astype(BF16)
    for s in range(parts):
        held[turn ^ s] = pieces[s * rows : (s + 1) * rows, :]
    for t in range(parts):
        outs[t][...] = held[t]


def add_kernel(*refs):
    terms, out = refs[:-1], refs[-1]
    total = terms[0][...].astype(F32)
    for term in terms[1:]:
        total = total + term[...].astype(F32)
    out[...] = total.astype(BF16)


def norm_kernel(parts, gain_ref, *refs):
    shards, out = refs[:parts], refs[parts]
    width = shards[0].shape[1]
    values = [shard[...].astype(F32) for shard in shards]
    center = sum(jnp.sum(part, axis=1, keepdims=True) for part in values) / out.shape[1]
    values = [part - center for part in values]
    spread = sum(jnp.sum(part * part, axis=1, keepdims=True) for part in values) / out.shape[1]
    scale = lax.rsqrt(spread + 1e-05)
    for s in range(parts):
        here = pl.ds(pl.multiple_of((lax.axis_index("gx") ^ s) * width, HD), width)
        out[:, here] = (values[s] * scale * gain_ref[:, here]).astype(BF16)


def by_distance(pair_ref, second_ref):
    return pair_ref.at[0], second_ref.at[0], pair_ref.at[1], second_ref.at[1]


def load_kernel(rows, source_hbm, out_ref, sem):
    copy = pltpu.make_async_copy(source_hbm.at[pl.ds(0, rows)], out_ref, sem)
    copy.start()
    copy.wait()


def lift_kernel(chunks, *refs):
    count = 2 * chunks
    shards, (up_ref, down_ref, down_hbm) = refs[:count], refs[count : count + 3]
    active_ref, far_ref, close_ref, rest_ref, held, passed, sem = refs[count + 3 :]
    hidden = active_ref.shape[1]
    share = far_ref.shape[2]
    half = far_ref.shape[1]
    rows = shards[0].shape[1]
    cut = down_ref.shape[0]
    copy = pltpu.make_async_copy(down_hbm.at[pl.ds(cut, hidden - cut)], rest_ref, sem)
    copy.start()
    for c in range(chunks):
        for t, shard in enumerate(by_distance(*shards[2 * c : 2 * c + 2])):
            first = pl.multiple_of(((lax.axis_index("ta") ^ t) * chunks + c) * rows, rows)
            held[pl.ds(first, rows), :] = shard[...]
    for first in range(0, hidden, 6 * HD):
        last = min(first + 6 * HD, hidden)
        raised = lax.dot_general(
            up_ref[first:last, :], held[...], (((1,), (1,)), ((), ())), preferred_element_type=F32
        )
        active_ref[:, first:last] = (raised / (1.0 + jnp.exp(-raised))).T.astype(BF16)
    copy.wait()
    mine = lax.axis_index("gx") // 2
    for k in range(2):
        passed[...] = lowered(2 * k + 1, active_ref, down_ref, rest_ref, share).astype(BF16)
        for out_ref, side in ((far_ref, 1 - mine), (close_ref, mine)):
            out_ref[k] = passed[pl.ds(pl.multiple_of(side * half, half), half), :]


def lowered(turn, active_ref, down_ref, rest_ref, share):
    cut = down_ref.shape[0]
    here = pl.ds(pl.multiple_of((lax.axis_index("ta") ^ turn) * share, HD), share)
    return jnp.dot(
        active_ref[:, :cut], down_ref[:, here], preferred_element_type=F32
    ) + jnp.dot(active_ref[:, cut:], rest_ref[:, here], preferred_element_type=F32)


def lower_kernel(turn, active_ref, down_ref, rest_ref, out_ref):
    out_ref[...] = lowered(turn, active_ref, down_ref, rest_ref, out_ref.shape[1])


def turn_kernel(distances, cross_ref, near_ref, *outs):
    rows = outs[0].shape[0]
    for distance, out_ref in zip(distances, outs):
        z = lax.axis_index("gx") ^ distance
        here = pl.ds(pl.multiple_of(z * rows, rows), rows)
        there = pl.ds(pl.multiple_of(z % 2 * rows, rows), rows)
        out_ref[...] = (cross_ref[here, :] + near_ref[1, there, :].astype(F32)).astype(BF16)


def split_kernel(distances, own_ref, near_ref, *refs):
    count = len(distances)
    rows = refs[0].shape[0]
    for distance, crossed_ref, out_ref in zip(distances, refs[:count], refs[count:]):
        z = lax.axis_index("gx") ^ distance
        here = pl.ds(pl.multiple_of(z * rows, rows), rows)
        there = pl.ds(pl.multiple_of(z % 2 * rows, rows), rows)
        total = own_ref[here, :] + near_ref[0, there, :].astype(F32)
        out_ref[...] = (total + crossed_ref[...].astype(F32)).astype(BF16)


def mix_kernel(distances, gate_ref, *refs):
    out = refs[-1]
    lanes = gate_ref.shape[2]
    for begin in range(0, out.shape[1], lanes):
        part = slice(begin, begin + lanes)
        total = sum(
            gate_ref[s] * term[:, part].astype(F32) for s, term in zip(distances, refs)
        )
        for ref in refs[len(distances) : -1]:
            total = total + ref[:, part]
        out[:, part] = total.astype(out.dtype)


def trade(array, axis, turn):
    count = lax.axis_size(axis)
    return lax.ppermute(array, axis, [(k, k ^ turn) for k in range(count)])


def every_row_body(
    queries, new_kv, kv_cache, lengths, out_proj, norm_gain, expert_ids, gate_weights, w_up, w_down
):
    gx_count = lax.axis_size("gx")
    ta_count = lax.axis_size("ta")
    chunks = 2
    block_rows = queries.shape[0]
    rows = block_rows // chunks
    width = out_proj.shape[1]
    model = norm_gain.shape[0]
    hidden_share = w_up.shape[2]
    share = model // ta_count
    all_rows = block_rows * gx_count
    shape = jax.ShapeDtypeStruct
    gain = norm_gain.reshape(1, model)
    heads = queries.shape[1] // HD
    small = beside(queries, new_kv, lengths, kv_cache.shape[2])
    attended = []
    for c in range(chunks):
        after = attended[-1] if attended else small
        attended.append(attend(small, kv_cache, heads, c * rows, rows, after))
    order = [s for s in range(gx_count - 1, 0, -1)]

    def spread(array, axis):
        parts = {0: array, **{s: trade(array, axis, s) for s in order}}
        return [parts[s] for s in range(len(parts))]

    shards = [spread(part, "gx") for part in attended]
    pieces, hidden = [], []
    for c in range(chunks):
        pieces.append(
            local_call(
                functools.partial(project_kernel, gx_count),
                [shape((rows, width), BF16)] * ta_count,
                [VMEM] * (gx_count + 1),
                [pltpu.VMEM((ta_count, rows, width), BF16)],
                name="project",
                after=pieces[-1][0] if pieces else attended[-1],
                cost=PROJECT_COST,
            )(*shards[c], out_proj)
        )
    for c in range(chunks):
        parts = [pieces[c][0]] + [trade(pieces[c][t], "ta", t) for t in range(1, ta_count)]
        hidden.append(
            local_call(
                add_kernel,
                shape((rows, width), BF16),
                [VMEM] * ta_count,
                name="add",
                after=hidden[-1] if hidden else pieces[-1][0],
            )(*parts)
        )
    shards = [spread(part, "gx") for part in hidden]
    normed, pairs = [], []
    for c in range(chunks):
        normed.append(
            local_call(
                functools.partial(norm_kernel, gx_count),
                shape((rows, model), BF16),
                [VMEM] * (gx_count + 1),
                name="norm",
                after=normed[-1] if normed else hidden[-1],
            )(gain, *shards[c])
        )
    gates = local_call(
        gate_kernel,
        shape((gx_count, block_rows, HD), F32),
        [VMEM, VMEM],
        name="gates",
        after=normed[-1],
    )(expert_ids, gate_weights)
    up = local_call(
        functools.partial(load_kernel, hidden_share),
        shape((hidden_share, model), BF16),
        [ANYWHERE],
        [pltpu.SemaphoreType.DMA],
        vmem=40,
        name="load_up",
        after=gates,
    )(jnp.swapaxes(w_up[0], 0, 1))
    for c in range(chunks):
        pairs.append(
            local_call(
                pair_kernel,
                shape((2, rows, model), BF16),
                [VMEM] * 2,
                name="pair",
                after=pairs[-1] if pairs else up,
            )(normed[c], trade(normed[c], "ta", 2))
        )
    blocks = [block for pair in pairs for block in (pair, trade(pair, "ta", 1))]
    cut = hidden_share // (4 * HD) * 2 * HD
    part = local_call(
        functools.partial(load_kernel, cut),
        shape((cut, model), BF16),
        [ANYWHERE],
        [pltpu.SemaphoreType.DMA],
        vmem=46,
        name="load_down",
        after=pairs[-1],
    )(w_down[0])
    half = all_rows // 2
    active, far, close, rest = local_call(
        functools.partial(lift_kernel, chunks),
        [
            shape((all_rows, hidden_share), BF16),
            shape((2, half, share), BF16),
            shape((2, half, share), BF16),
            shape((hidden_share - cut, model), BF16),
        ],
        [VMEM] * (2 * chunks + 2) + [ANYWHERE],
        [
            pltpu.VMEM((all_rows, model), BF16),
            pltpu.VMEM((all_rows, share), BF16),
            pltpu.SemaphoreType.DMA,
        ],
        vmem=30,
        name="lift",
    )(*blocks, up, part, w_down[0])
    near = {1: trade(far, "ta", 1), 0: trade(close, "ta", 1)}

    def lower(turn, after):
        return local_call(
            functools.partial(lower_kernel, turn),
            shape((all_rows, share), F32),
            [VMEM] * 3,
            name="lower",
            after=after,
        )(active, part, rest)

    def on_rows(kernel, distances, after, *arrays):
        return local_call(
            functools.partial(kernel, distances),
            [shape((block_rows, share), BF16)] * len(distances),
            [VMEM] * len(arrays),
            name=kernel.__name__[:-7],
            after=after,
        )(*arrays)

    cross = lower(2, None)
    groups = ((3,), (2,), (1, 0))
    turned = [cross]
    crossed = {}
    for distances in groups:
        sums = on_rows(turn_kernel, distances, turned[0], cross, near[distances[0] // 2])
        turned = sums
        crossed.update({s: trade(part, "ta", 2) for s, part in zip(distances, sums)})
    own = lower(0, turned[0])
    gathered, total, after = {}, [], None
    for distances in groups:
        terms = on_rows(
            split_kernel, distances, after, own, near[distances[0] // 2],
            *[crossed[s] for s in distances],
        )
        after = terms[0]
        for s, term in zip(distances, terms):
            gathered[s] = trade(term, "gx", s) if s else term
    for distances in groups:
        last = 0 in distances
        total = [
            local_call(
                functools.partial(mix_kernel, distances),
                shape((block_rows, share), BF16 if last else F32),
                [VMEM] * (1 + len(distances) + len(total)),
                name="mix",
                cost=1024 if last else MIX_COST,
            )(gates, *[gathered[s] for s in distances], *total)
        ]
    return total[0]


def route_tables(expert_ids, expert_count, block_rows, capacity):
    blocks = expert_ids.shape[0] // block_rows
    expert_range = jnp.arange(expert_count, dtype=jnp.int32)
    matches = (expert_ids[:, :, None] == expert_range[None, None, :]).astype(jnp.int32)
    routed = jnp.sum(matches, axis=1).reshape(blocks, block_rows, expert_count)
    position = jnp.cumsum(routed, axis=1) - routed
    slot_range = jnp.arange(capacity, dtype=jnp.int32)
    slot_hits = routed[:, :, :, None] * (
        position[:, :, :, None] == slot_range[None, None, None, :]
    ).astype(jnp.int32)
    row_range = jnp.arange(block_rows, dtype=jnp.int32)
    block_start = (jnp.arange(blocks, dtype=jnp.int32) * block_rows)[:, None, None]
    source_row = jnp.sum(slot_hits * row_range[None, :, None, None], axis=1) + block_start
    filled = jnp.sum(slot_hits, axis=1)
    source_row = jnp.transpose(source_row, (1, 0, 2)).reshape(expert_count, blocks * capacity)
    filled = jnp.transpose(filled, (1, 0, 2)).reshape(expert_count, blocks * capacity)
    pick_slot = jnp.sum(matches * position.reshape(blocks * block_rows, 1, expert_count), axis=2)
    return (source_row, filled, pick_slot)


def layer_norm(hidden, norm_gain):
    values = hidden.astype(jnp.float32)
    center = values - jnp.mean(values, axis=1, keepdims=True)
    spread = jnp.mean(center * center, axis=1, keepdims=True)
    return (center * lax.rsqrt(spread + 1e-05) * norm_gain).astype(jnp.bfloat16)


def body(
    queries, new_kv, kv_cache, lengths, out_proj, norm_gain, expert_ids, gate_weights, w_up, w_down
):
    gx_count = lax.axis_size("gx")
    ta_count = lax.axis_size("ta")
    block_rows = queries.shape[0]
    top_count = expert_ids.shape[1]
    capacity = min(block_rows, 2 * block_rows * top_count // gx_count)
    slot_count = gx_count * capacity
    model_width = norm_gain.shape[0]
    width_share = model_width // ta_count
    if gx_count == top_count and ta_count == gx_count == 4:
        return every_row_body(
            queries, new_kv, kv_cache, lengths, out_proj, norm_gain, expert_ids, gate_weights,
            w_up, w_down,
        )
    small = beside(queries, new_kv, lengths, kv_cache.shape[2])
    attended = attend(small, kv_cache, queries.shape[1] // HD, 0, block_rows, small)
    projected = jnp.dot(
        lax.all_gather(attended, "gx", axis=0, tiled=True),
        out_proj,
        preferred_element_type=jnp.float32,
    ).astype(jnp.bfloat16)
    source_row, filled, pick_slot = route_tables(expert_ids, gx_count, block_rows, capacity)
    live_slots = (filled > 0)[:, :, None]
    widened = lax.optimization_barrier(projected).astype(jnp.float32)
    hidden_share = lax.psum_scatter(
        widened.astype(jnp.bfloat16), "ta", scatter_dimension=1, tiled=True
    )
    outgoing = jnp.where(live_slots, hidden_share[source_row], jnp.zeros((), jnp.bfloat16))[
        :, :, None, :
    ]
    arrived = lax.all_to_all(outgoing, "gx", split_axis=0, concat_axis=2, tiled=True)
    gathered = lax.all_gather(arrived, "ta", axis=3, tiled=True)
    hidden = gathered.reshape(slot_count, model_width)
    normed = layer_norm(hidden, norm_gain)
    raised = jnp.dot(normed, w_up[0], preferred_element_type=jnp.float32)
    active = jax.nn.silu(raised).astype(jnp.bfloat16)
    terms = jnp.dot(active, w_down[0], preferred_element_type=jnp.float32)
    mine = lax.psum_scatter(terms, "ta", scatter_dimension=1, tiled=True)
    result = mine.astype(jnp.bfloat16).reshape(gx_count, capacity, width_share)
    returned = lax.all_to_all(result, "gx", split_axis=0, concat_axis=0, tiled=True)
    first_row = lax.axis_index("gx") * block_rows
    local_ids = lax.dynamic_slice_in_dim(expert_ids, first_row, block_rows, 0)
    local_slot = lax.dynamic_slice_in_dim(pick_slot, first_row, block_rows, 0)
    flat_rows = returned.reshape(gx_count * capacity, width_share)
    picked = flat_rows[local_ids * capacity + local_slot]
    return jnp.sum(picked.astype(jnp.float32) * gate_weights[:, :, None], axis=1).astype(
        jnp.bfloat16
    )


def solution(mesh):
    return jax.shard_map(
        body,
        mesh=mesh,
        in_specs=(
            P(("groups", "gx"), "ta"),
            P(None, ("groups", "gx"), "ta"),
            P(None, ("groups", "gx"), None, "ta"),
            P(("groups", "gx")),
            P("ta", "gx"),
            P(),
            P("groups", None),
            P(("groups", "gx"), None),
            P("gx", None, "ta"),
            P("gx", "ta", None),
        ),
        out_specs=P(("groups", "gx"), "ta"),
        check_vma=False,
    )
```

```python
import functools
import math

import jax
import jax.numpy as jnp
from jax import lax
from jax.experimental import pallas as pl
from jax.experimental.pallas import tpu as pltpu
from jax.sharding import PartitionSpec as P

HD = 128
MIB = 1 << 20
MIX_COST = 1 << 22
PROJECT_COST = 1 << 21
VMEM = pl.BlockSpec(memory_space=pltpu.VMEM)
F32 = jnp.float32
BF16 = jnp.bfloat16


ANYWHERE = pl.BlockSpec(memory_space=pl.ANY)


def local_call(kernel, out_shape, in_specs, scratch=(), vmem=8, name=None, after=None, cost=1024):
    several = isinstance(out_shape, (tuple, list))
    if after is not None:
        count, inner = len(in_specs), kernel
        in_specs = [*in_specs, ANYWHERE]
        kernel = lambda *refs: inner(*refs[:count], *refs[count + 1 :])
    call = pl.pallas_call(
        kernel,
        out_shape=out_shape,
        in_specs=in_specs,
        out_specs=[VMEM] * len(out_shape) if several else VMEM,
        scratch_shapes=list(scratch),
        compiler_params=pltpu.CompilerParams(vmem_limit_bytes=vmem * MIB),
        cost_estimate=pl.CostEstimate(flops=1024, bytes_accessed=cost, transcendentals=0),
        name=name,
    )
    return call if after is None else lambda *args: call(*args, after)


def attend_kernel(
    kv_heads, group, slots, batch, begin,
    small_ref, cache_ref, after_ref, out_ref,
    keys, values, q_rows, scores, own_scores, probs, own_probs, mixed, sems,
):
    rows = out_ref.shape[0]
    context = keys.shape[1]
    width = kv_heads * HD
    heads = kv_heads * group
    steps = rows // batch
    scale = 1.0 / math.sqrt(HD)
    fresh = [slice(heads * HD + k * width, heads * HD + (k + 1) * width) for k in range(2)]
    spans = slice(heads * HD + 2 * width, heads * HD + 2 * width + context)

    def fetch(step, kind):
        buffer = (keys, values)[kind]
        return pltpu.make_async_copy(
            cache_ref.at[kind, pl.ds(begin + step * batch, batch)],
            buffer.at[pl.ds(step * batch, batch)],
            sems.at[kind, step],
        )

    for kind in range(2):
        for step in range(steps):
            fetch(step, kind).start()
    q_rows[...] = jnp.zeros_like(q_rows)
    for head in range(heads):
        q_rows[head // group, pl.ds(head, rows, stride=slots), :] = small_ref[
            begin : begin + rows, head * HD : (head + 1) * HD
        ].astype(F32)
    place = lax.broadcasted_iota(jnp.int32, (slots, context), 1).astype(F32)

    def score(step):
        fetch(step, 0).wait()
        for k in range(batch):
            row = step * batch + k
            whole = slice(begin + row, begin + row + 1)
            mine = jnp.concatenate(
                [q_rows[g, row * slots : (row + 1) * slots, :] for g in range(kv_heads)], axis=1
            )
            cached = lax.dot_general(
                mine.astype(BF16), keys[row], (((1,), (1,)), ((), ())),
                preferred_element_type=F32,
            )
            here = slice(k * slots, (k + 1) * slots)
            seen = place < small_ref[whole, spans].astype(F32)
            scores[step % 2, here, :] = jnp.where(seen, cached * scale, -jnp.inf)
            fresh_key = small_ref[whole, fresh[0]].astype(F32)
            own_scores[step % 2, here, :] = jnp.broadcast_to(
                jnp.sum(mine * fresh_key, axis=1, keepdims=True) * scale, (slots, HD)
            )

    score(0)
    for step in range(steps):
        if step + 1 < steps:
            score(step + 1)
        cached = scores[step % 2]
        own = own_scores[step % 2, :, :1]
        largest = jnp.maximum(jnp.max(cached, axis=1, keepdims=True), own)
        lifted = jnp.exp(cached - largest)
        own_lifted = jnp.exp(own - largest)
        total = jnp.sum(lifted, axis=1, keepdims=True) + own_lifted
        probs[step % 2] = (lifted / total).astype(BF16)
        own_probs[step % 2] = jnp.broadcast_to(
            (own_lifted / total).astype(BF16).astype(F32), own_probs.shape[1:]
        )
        fetch(step, 1).wait()
        for k in range(batch):
            row = step * batch + k
            whole = slice(begin + row, begin + row + 1)
            here = slice(k * slots, (k + 1) * slots)
            weighted = jnp.dot(probs[step % 2, here, :], values[row], preferred_element_type=F32)
            fresh_value = small_ref[whole, fresh[1]].astype(F32)
            total = weighted + own_probs[step % 2, here, :1] * fresh_value
            for g in range(kv_heads):
                mixed[step % 2, g, here, :] = total[:, g * HD : (g + 1) * HD]
        for head in range(heads):
            out_ref[step * batch : (step + 1) * batch, head * HD : (head + 1) * HD] = mixed[
                step % 2, head // group, pl.ds(head, batch, stride=slots), :
            ].astype(BF16)


def beside(queries, new_kv, lengths, context):
    lanes = -(-context // HD) * HD
    spans = jnp.broadcast_to(lengths.astype(BF16)[:, None], (lengths.shape[0], lanes))
    return jnp.concatenate([queries, new_kv[0], new_kv[1], spans], axis=1)


def attend(small, kv_cache, heads, begin, rows, after):
    context, width = kv_cache.shape[2:]
    kv_heads = width // HD
    slots = -(-heads // 8) * 8
    batch = 16
    shape = jax.ShapeDtypeStruct((rows, heads * HD), BF16)
    return pl.pallas_call(
        functools.partial(attend_kernel, kv_heads, heads // kv_heads, slots, batch, begin),
        out_shape=shape,
        in_specs=[VMEM, ANYWHERE, ANYWHERE],
        out_specs=VMEM,
        scratch_shapes=[
            pltpu.VMEM((rows, context, width), BF16),
            pltpu.VMEM((rows, context, width), BF16),
            pltpu.VMEM((kv_heads, rows * slots, HD), F32),
            pltpu.VMEM((2, batch * slots, context), F32),
            pltpu.VMEM((2, batch * slots, HD), F32),
            pltpu.VMEM((2, batch * slots, context), BF16),
            pltpu.VMEM((2, batch * slots, HD), F32),
            pltpu.VMEM((2, kv_heads, batch * slots, HD), F32),
            pltpu.SemaphoreType.DMA((2, rows // batch)),
        ],
        compiler_params=pltpu.CompilerParams(vmem_limit_bytes=50 * MIB),
        cost_estimate=pl.CostEstimate(flops=1024, bytes_accessed=1024, transcendentals=0),
        name="attend",
    )(small, kv_cache, after)


def pair_kernel(own_ref, other_ref, out_ref):
    out_ref[0] = own_ref[...]
    out_ref[1] = other_ref[...]


def pass_kernel(source_ref, out_ref):
    out_ref[...] = source_ref[...]


def gate_kernel(ids_ref, gates_ref, gate_ref):
    parts, rows, lanes = gate_ref.shape
    ids = ids_ref[pl.ds(pl.multiple_of(lax.axis_index("gx") * rows, rows), rows), :]
    for s in range(parts):
        gate = jnp.sum(
            jnp.where(ids == (lax.axis_index("gx") ^ s), gates_ref[...], 0.0), axis=1, keepdims=True
        )
        gate_ref[s] = jnp.broadcast_to(gate, (rows, lanes))


def project_kernel(parts, *refs):
    shards, weight_ref = refs[:parts], refs[parts]
    outs, held = refs[parts + 1 : -1], refs[-1]
    rows = shards[0].shape[0]
    turn = lax.axis_index("gx") ^ lax.axis_index("ta")
    block = jnp.concatenate([shard[...] for shard in shards], axis=0)
    pieces = jnp.dot(block, weight_ref[...], preferred_element_type=F32).astype(BF16)
    for s in range(parts):
        held[turn ^ s] = pieces[s * rows : (s + 1) * rows, :]
    for t in range(parts):
        outs[t][...] = held[t]


def add_kernel(*refs):
    terms, out = refs[:-1], refs[-1]
    total = terms[0][...].astype(F32)
    for term in terms[1:]:
        total = total + term[...].astype(F32)
    out[...] = total.astype(BF16)


def norm_kernel(parts, gain_ref, *refs):
    shards, out = refs[:parts], refs[parts]
    width = shards[0].shape[1]
    values = [shard[...].astype(F32) for shard in shards]
    center = sum(jnp.sum(part, axis=1, keepdims=True) for part in values) / out.shape[1]
    values = [part - center for part in values]
    spread = sum(jnp.sum(part * part, axis=1, keepdims=True) for part in values) / out.shape[1]
    scale = lax.rsqrt(spread + 1e-05)
    for s in range(parts):
        here = pl.ds(pl.multiple_of((lax.axis_index("gx") ^ s) * width, HD), width)
        out[:, here] = (values[s] * scale * gain_ref[:, here]).astype(BF16)


def by_distance(pair_ref, second_ref):
    return pair_ref.at[0], second_ref.at[0], pair_ref.at[1], second_ref.at[1]


def load_kernel(rows, source_hbm, out_ref, sem):
    copy = pltpu.make_async_copy(source_hbm.at[pl.ds(0, rows)], out_ref, sem)
    copy.start()
    copy.wait()


def lift_kernel(chunks, *refs):
    count = 2 * chunks
    shards, (up_ref, down_ref, down_hbm) = refs[:count], refs[count : count + 3]
    active_ref, far_ref, close_ref, rest_ref, held, passed, sem = refs[count + 3 :]
    hidden = active_ref.shape[1]
    share = far_ref.shape[2]
    half = far_ref.shape[1]
    rows = shards[0].shape[1]
    cut = down_ref.shape[0]
    copy = pltpu.make_async_copy(down_hbm.at[pl.ds(cut, hidden - cut)], rest_ref, sem)
    copy.start()
    for c in range(chunks):
        for t, shard in enumerate(by_distance(*shards[2 * c : 2 * c + 2])):
            first = pl.multiple_of(((lax.axis_index("ta") ^ t) * chunks + c) * rows, rows)
            held[pl.ds(first, rows), :] = shard[...]
    for first in range(0, hidden, 6 * HD):
        last = min(first + 6 * HD, hidden)
        raised = lax.dot_general(
            up_ref[first:last, :], held[...], (((1,), (1,)), ((), ())), preferred_element_type=F32
        )
        active_ref[:, first:last] = (raised / (1.0 + jnp.exp(-raised))).T.astype(BF16)
    copy.wait()
    mine = lax.axis_index("gx") // 2
    for k in range(2):
        passed[...] = lowered(2 * k + 1, active_ref, down_ref, rest_ref, share).astype(BF16)
        for out_ref, side in ((far_ref, 1 - mine), (close_ref, mine)):
            out_ref[k] = passed[pl.ds(pl.multiple_of(side * half, half), half), :]


def lowered(turn, active_ref, down_ref, rest_ref, share):
    cut = down_ref.shape[0]
    here = pl.ds(pl.multiple_of((lax.axis_index("ta") ^ turn) * share, HD), share)
    return jnp.dot(
        active_ref[:, :cut], down_ref[:, here], preferred_element_type=F32
    ) + jnp.dot(active_ref[:, cut:], rest_ref[:, here], preferred_element_type=F32)


def lower_kernel(turn, active_ref, down_ref, rest_ref, out_ref):
    out_ref[...] = lowered(turn, active_ref, down_ref, rest_ref, out_ref.shape[1])


def turn_kernel(distances, cross_ref, near_ref, *outs):
    rows = outs[0].shape[0]
    for distance, out_ref in zip(distances, outs):
        z = lax.axis_index("gx") ^ distance
        here = pl.ds(pl.multiple_of(z * rows, rows), rows)
        there = pl.ds(pl.multiple_of(z % 2 * rows, rows), rows)
        out_ref[...] = (cross_ref[here, :] + near_ref[1, there, :].astype(F32)).astype(BF16)


def split_kernel(distances, own_ref, near_ref, *refs):
    count = len(distances)
    rows = refs[0].shape[0]
    for distance, crossed_ref, out_ref in zip(distances, refs[:count], refs[count:]):
        z = lax.axis_index("gx") ^ distance
        here = pl.ds(pl.multiple_of(z * rows, rows), rows)
        there = pl.ds(pl.multiple_of(z % 2 * rows, rows), rows)
        total = own_ref[here, :] + near_ref[0, there, :].astype(F32)
        out_ref[...] = (total + crossed_ref[...].astype(F32)).astype(BF16)


def mix_kernel(distances, gate_ref, *refs):
    out = refs[-1]
    lanes = gate_ref.shape[2]
    for begin in range(0, out.shape[1], lanes):
        part = slice(begin, begin + lanes)
        total = sum(
            gate_ref[s] * term[:, part].astype(F32) for s, term in zip(distances, refs)
        )
        for ref in refs[len(distances) : -1]:
            total = total + ref[:, part]
        out[:, part] = total.astype(out.dtype)


def trade(array, axis, turn):
    count = lax.axis_size(axis)
    return lax.ppermute(array, axis, [(k, k ^ turn) for k in range(count)])


def every_row_body(
    queries, new_kv, kv_cache, lengths, out_proj, norm_gain, expert_ids, gate_weights, w_up, w_down
):
    gx_count = lax.axis_size("gx")
    ta_count = lax.axis_size("ta")
    chunks = 2
    block_rows = queries.shape[0]
    rows = block_rows // chunks
    width = out_proj.shape[1]
    model = norm_gain.shape[0]
    hidden_share = w_up.shape[2]
    share = model // ta_count
    all_rows = block_rows * gx_count
    shape = jax.ShapeDtypeStruct
    gain = norm_gain.reshape(1, model)
    heads = queries.shape[1] // HD
    small = beside(queries, new_kv, lengths, kv_cache.shape[2])
    attended = []
    for c in range(chunks):
        after = attended[-1] if attended else small
        attended.append(attend(small, kv_cache, heads, c * rows, rows, after))
    order = [s for s in range(gx_count - 1, 0, -1)]

    def spread(array, axis):
        parts = {0: array, **{s: trade(array, axis, s) for s in order}}
        return [parts[s] for s in range(len(parts))]

    two = trade(attended[0], "gx", 2)
    onward = local_call(
        pass_kernel, shape(two.shape, BF16), [VMEM], name="pass", after=attended[1]
    )(two)
    shards = [
        [attended[0], trade(attended[0], "gx", 1), two, trade(onward, "gx", 1)],
        spread(attended[1], "gx"),
    ]
    pieces, hidden = [], []
    for c in range(chunks):
        pieces.append(
            local_call(
                functools.partial(project_kernel, gx_count),
                [shape((rows, width), BF16)] * ta_count,
                [VMEM] * (gx_count + 1),
                [pltpu.VMEM((ta_count, rows, width), BF16)],
                name="project",
                after=pieces[-1][0] if pieces else attended[-1],
                cost=PROJECT_COST,
            )(*shards[c], out_proj)
        )
    for c in range(chunks):
        parts = [pieces[c][0]] + [trade(pieces[c][t], "ta", t) for t in range(1, ta_count)]
        hidden.append(
            local_call(
                add_kernel,
                shape((rows, width), BF16),
                [VMEM] * ta_count,
                name="add",
                after=hidden[-1] if hidden else pieces[-1][0],
            )(*parts)
        )
    shards = [spread(part, "gx") for part in hidden]
    normed, pairs = [], []
    for c in range(chunks):
        normed.append(
            local_call(
                functools.partial(norm_kernel, gx_count),
                shape((rows, model), BF16),
                [VMEM] * (gx_count + 1),
                name="norm",
                after=normed[-1] if normed else hidden[-1],
            )(gain, *shards[c])
        )
    gates = local_call(
        gate_kernel,
        shape((gx_count, block_rows, HD), F32),
        [VMEM, VMEM],
        name="gates",
        after=normed[-1],
    )(expert_ids, gate_weights)
    up = local_call(
        functools.partial(load_kernel, hidden_share),
        shape((hidden_share, model), BF16),
        [ANYWHERE],
        [pltpu.SemaphoreType.DMA],
        vmem=40,
        name="load_up",
        after=gates,
    )(jnp.swapaxes(w_up[0], 0, 1))
    for c in range(chunks):
        pairs.append(
            local_call(
                pair_kernel,
                shape((2, rows, model), BF16),
                [VMEM] * 2,
                name="pair",
                after=pairs[-1] if pairs else up,
            )(normed[c], trade(normed[c], "ta", 2))
        )
    blocks = [block for pair in pairs for block in (pair, trade(pair, "ta", 1))]
    cut = 2 * HD
    part = local_call(
        functools.partial(load_kernel, cut),
        shape((cut, model), BF16),
        [ANYWHERE],
        [pltpu.SemaphoreType.DMA],
        vmem=48,
        name="load_down",
        after=pairs[-1],
    )(w_down[0])
    half = all_rows // 2
    active, far, close, rest = local_call(
        functools.partial(lift_kernel, chunks),
        [
            shape((all_rows, hidden_share), BF16),
            shape((2, half, share), BF16),
            shape((2, half, share), BF16),
            shape((hidden_share - cut, model), BF16),
        ],
        [VMEM] * (2 * chunks + 2) + [ANYWHERE],
        [
            pltpu.VMEM((all_rows, model), BF16),
            pltpu.VMEM((all_rows, share), BF16),
            pltpu.SemaphoreType.DMA,
        ],
        vmem=30,
        name="lift",
    )(*blocks, up, part, w_down[0])
    near = {1: trade(far, "ta", 1), 0: trade(close, "ta", 1)}

    def lower(turn, after):
        return local_call(
            functools.partial(lower_kernel, turn),
            shape((all_rows, share), F32),
            [VMEM] * 3,
            name="lower",
            after=after,
        )(active, part, rest)

    def on_rows(kernel, distances, after, *arrays):
        return local_call(
            functools.partial(kernel, distances),
            [shape((block_rows, share), BF16)] * len(distances),
            [VMEM] * len(arrays),
            name=kernel.__name__[:-7],
            after=after,
        )(*arrays)

    cross = lower(2, None)
    groups = ((3,), (2,), (1, 0))
    turned = [cross]
    crossed = {}
    for distances in groups:
        sums = on_rows(turn_kernel, distances, turned[0], cross, near[distances[0] // 2])
        turned = sums
        crossed.update({s: trade(part, "ta", 2) for s, part in zip(distances, sums)})
    own = lower(0, turned[0])
    gathered, total, after = {}, [], None
    for distances in groups:
        terms = on_rows(
            split_kernel, distances, after, own, near[distances[0] // 2],
            *[crossed[s] for s in distances],
        )
        after = terms[0]
        for s, term in zip(distances, terms):
            gathered[s] = trade(term, "gx", s) if s else term
    for distances in groups:
        last = 0 in distances
        total = [
            local_call(
                functools.partial(mix_kernel, distances),
                shape((block_rows, share), BF16 if last else F32),
                [VMEM] * (1 + len(distances) + len(total)),
                name="mix",
                cost=1024 if last else MIX_COST,
            )(gates, *[gathered[s] for s in distances], *total)
        ]
    return total[0]


def route_tables(expert_ids, expert_count, block_rows, capacity):
    blocks = expert_ids.shape[0] // block_rows
    expert_range = jnp.arange(expert_count, dtype=jnp.int32)
    matches = (expert_ids[:, :, None] == expert_range[None, None, :]).astype(jnp.int32)
    routed = jnp.sum(matches, axis=1).reshape(blocks, block_rows, expert_count)
    position = jnp.cumsum(routed, axis=1) - routed
    slot_range = jnp.arange(capacity, dtype=jnp.int32)
    slot_hits = routed[:, :, :, None] * (
        position[:, :, :, None] == slot_range[None, None, None, :]
    ).astype(jnp.int32)
    row_range = jnp.arange(block_rows, dtype=jnp.int32)
    block_start = (jnp.arange(blocks, dtype=jnp.int32) * block_rows)[:, None, None]
    source_row = jnp.sum(slot_hits * row_range[None, :, None, None], axis=1) + block_start
    filled = jnp.sum(slot_hits, axis=1)
    source_row = jnp.transpose(source_row, (1, 0, 2)).reshape(expert_count, blocks * capacity)
    filled = jnp.transpose(filled, (1, 0, 2)).reshape(expert_count, blocks * capacity)
    pick_slot = jnp.sum(matches * position.reshape(blocks * block_rows, 1, expert_count), axis=2)
    return (source_row, filled, pick_slot)


def layer_norm(hidden, norm_gain):
    values = hidden.astype(jnp.float32)
    center = values - jnp.mean(values, axis=1, keepdims=True)
    spread = jnp.mean(center * center, axis=1, keepdims=True)
    return (center * lax.rsqrt(spread + 1e-05) * norm_gain).astype(jnp.bfloat16)


def body(
    queries, new_kv, kv_cache, lengths, out_proj, norm_gain, expert_ids, gate_weights, w_up, w_down
):
    gx_count = lax.axis_size("gx")
    ta_count = lax.axis_size("ta")
    block_rows = queries.shape[0]
    top_count = expert_ids.shape[1]
    capacity = min(block_rows, 2 * block_rows * top_count // gx_count)
    slot_count = gx_count * capacity
    model_width = norm_gain.shape[0]
    width_share = model_width // ta_count
    if gx_count == top_count and ta_count == gx_count == 4:
        return every_row_body(
            queries, new_kv, kv_cache, lengths, out_proj, norm_gain, expert_ids, gate_weights,
            w_up, w_down,
        )
    small = beside(queries, new_kv, lengths, kv_cache.shape[2])
    attended = attend(small, kv_cache, queries.shape[1] // HD, 0, block_rows, small)
    projected = jnp.dot(
        lax.all_gather(attended, "gx", axis=0, tiled=True),
        out_proj,
        preferred_element_type=jnp.float32,
    ).astype(jnp.bfloat16)
    source_row, filled, pick_slot = route_tables(expert_ids, gx_count, block_rows, capacity)
    live_slots = (filled > 0)[:, :, None]
    widened = lax.optimization_barrier(projected).astype(jnp.float32)
    hidden_share = lax.psum_scatter(
        widened.astype(jnp.bfloat16), "ta", scatter_dimension=1, tiled=True
    )
    outgoing = jnp.where(live_slots, hidden_share[source_row], jnp.zeros((), jnp.bfloat16))[
        :, :, None, :
    ]
    arrived = lax.all_to_all(outgoing, "gx", split_axis=0, concat_axis=2, tiled=True)
    gathered = lax.all_gather(arrived, "ta", axis=3, tiled=True)
    hidden = gathered.reshape(slot_count, model_width)
    normed = layer_norm(hidden, norm_gain)
    raised = jnp.dot(normed, w_up[0], preferred_element_type=jnp.float32)
    active = jax.nn.silu(raised).astype(jnp.bfloat16)
    terms = jnp.dot(active, w_down[0], preferred_element_type=jnp.float32)
    mine = lax.psum_scatter(terms, "ta", scatter_dimension=1, tiled=True)
    result = mine.astype(jnp.bfloat16).reshape(gx_count, capacity, width_share)
    returned = lax.all_to_all(result, "gx", split_axis=0, concat_axis=0, tiled=True)
    first_row = lax.axis_index("gx") * block_rows
    local_ids = lax.dynamic_slice_in_dim(expert_ids, first_row, block_rows, 0)
    local_slot = lax.dynamic_slice_in_dim(pick_slot, first_row, block_rows, 0)
    flat_rows = returned.reshape(gx_count * capacity, width_share)
    picked = flat_rows[local_ids * capacity + local_slot]
    return jnp.sum(picked.astype(jnp.float32) * gate_weights[:, :, None], axis=1).astype(
        jnp.bfloat16
    )


def solution(mesh):
    return jax.shard_map(
        body,
        mesh=mesh,
        in_specs=(
            P(("groups", "gx"), "ta"),
            P(None, ("groups", "gx"), "ta"),
            P(None, ("groups", "gx"), None, "ta"),
            P(("groups", "gx")),
            P("ta", "gx"),
            P(),
            P("groups", None),
            P(("groups", "gx"), None),
            P("gx", None, "ta"),
            P("gx", "ta", None),
        ),
        out_specs=P(("groups", "gx"), "ta"),
        check_vma=False,
    )
```

```python
import functools
import math

import jax
import jax.numpy as jnp
from jax import lax
from jax.experimental import pallas as pl
from jax.experimental.pallas import tpu as pltpu
from jax.sharding import PartitionSpec as P

HD = 128
MIB = 1 << 20
MIX_COST = 1 << 22
PROJECT_COST = 1 << 21
VMEM = pl.BlockSpec(memory_space=pltpu.VMEM)
F32 = jnp.float32
BF16 = jnp.bfloat16


ANYWHERE = pl.BlockSpec(memory_space=pl.ANY)


def local_call(kernel, out_shape, in_specs, scratch=(), vmem=8, name=None, after=None, cost=1024):
    several = isinstance(out_shape, (tuple, list))
    if after is not None:
        count, inner = len(in_specs), kernel
        in_specs = [*in_specs, ANYWHERE]
        kernel = lambda *refs: inner(*refs[:count], *refs[count + 1 :])
    call = pl.pallas_call(
        kernel,
        out_shape=out_shape,
        in_specs=in_specs,
        out_specs=[VMEM] * len(out_shape) if several else VMEM,
        scratch_shapes=list(scratch),
        compiler_params=pltpu.CompilerParams(vmem_limit_bytes=vmem * MIB),
        cost_estimate=pl.CostEstimate(flops=1024, bytes_accessed=cost, transcendentals=0),
        name=name,
    )
    return call if after is None else lambda *args: call(*args, after)


def attend_kernel(
    kv_heads, group, slots, batch, begin,
    small_ref, cache_ref, after_ref, out_ref,
    keys, values, q_rows, scores, own_scores, probs, own_probs, mixed, sems,
):
    rows = out_ref.shape[0]
    context = keys.shape[1]
    width = kv_heads * HD
    heads = kv_heads * group
    steps = rows // batch
    scale = 1.0 / math.sqrt(HD)
    fresh = [slice(heads * HD + k * width, heads * HD + (k + 1) * width) for k in range(2)]
    spans = slice(heads * HD + 2 * width, heads * HD + 2 * width + context)

    def fetch(step, kind):
        buffer = (keys, values)[kind]
        return pltpu.make_async_copy(
            cache_ref.at[kind, pl.ds(begin + step * batch, batch)],
            buffer.at[pl.ds(step * batch, batch)],
            sems.at[kind, step],
        )

    for kind in range(2):
        for step in range(steps):
            fetch(step, kind).start()
    q_rows[...] = jnp.zeros_like(q_rows)
    for head in range(heads):
        q_rows[head // group, pl.ds(head, rows, stride=slots), :] = small_ref[
            begin : begin + rows, head * HD : (head + 1) * HD
        ].astype(F32)
    place = lax.broadcasted_iota(jnp.int32, (slots, context), 1).astype(F32)

    def score(step):
        fetch(step, 0).wait()
        for k in range(batch):
            row = step * batch + k
            whole = slice(begin + row, begin + row + 1)
            mine = jnp.concatenate(
                [q_rows[g, row * slots : (row + 1) * slots, :] for g in range(kv_heads)], axis=1
            )
            cached = lax.dot_general(
                mine.astype(BF16), keys[row], (((1,), (1,)), ((), ())),
                preferred_element_type=F32,
            )
            here = slice(k * slots, (k + 1) * slots)
            seen = place < small_ref[whole, spans].astype(F32)
            scores[step % 2, here, :] = jnp.where(seen, cached * scale, -jnp.inf)
            fresh_key = small_ref[whole, fresh[0]].astype(F32)
            own_scores[step % 2, here, :] = jnp.broadcast_to(
                jnp.sum(mine * fresh_key, axis=1, keepdims=True) * scale, (slots, HD)
            )

    score(0)
    for step in range(steps):
        if step + 1 < steps:
            score(step + 1)
        cached = scores[step % 2]
        own = own_scores[step % 2, :, :1]
        largest = jnp.maximum(jnp.max(cached, axis=1, keepdims=True), own)
        lifted = jnp.exp(cached - largest)
        own_lifted = jnp.exp(own - largest)
        total = jnp.sum(lifted, axis=1, keepdims=True) + own_lifted
        probs[step % 2] = (lifted / total).astype(BF16)
        own_probs[step % 2] = jnp.broadcast_to(
            (own_lifted / total).astype(BF16).astype(F32), own_probs.shape[1:]
        )
        fetch(step, 1).wait()
        for k in range(batch):
            row = step * batch + k
            whole = slice(begin + row, begin + row + 1)
            here = slice(k * slots, (k + 1) * slots)
            weighted = jnp.dot(probs[step % 2, here, :], values[row], preferred_element_type=F32)
            fresh_value = small_ref[whole, fresh[1]].astype(F32)
            total = weighted + own_probs[step % 2, here, :1] * fresh_value
            for g in range(kv_heads):
                mixed[step % 2, g, here, :] = total[:, g * HD : (g + 1) * HD]
        for head in range(heads):
            out_ref[step * batch : (step + 1) * batch, head * HD : (head + 1) * HD] = mixed[
                step % 2, head // group, pl.ds(head, batch, stride=slots), :
            ].astype(BF16)


def beside(queries, new_kv, lengths, context):
    lanes = -(-context // HD) * HD
    spans = jnp.broadcast_to(lengths.astype(BF16)[:, None], (lengths.shape[0], lanes))
    return jnp.concatenate([queries, new_kv[0], new_kv[1], spans], axis=1)


def attend(small, kv_cache, heads, begin, rows, after):
    context, width = kv_cache.shape[2:]
    kv_heads = width // HD
    slots = -(-heads // 8) * 8
    batch = 16
    shape = jax.ShapeDtypeStruct((rows, heads * HD), BF16)
    return pl.pallas_call(
        functools.partial(attend_kernel, kv_heads, heads // kv_heads, slots, batch, begin),
        out_shape=shape,
        in_specs=[VMEM, ANYWHERE, ANYWHERE],
        out_specs=VMEM,
        scratch_shapes=[
            pltpu.VMEM((rows, context, width), BF16),
            pltpu.VMEM((rows, context, width), BF16),
            pltpu.VMEM((kv_heads, rows * slots, HD), F32),
            pltpu.VMEM((2, batch * slots, context), F32),
            pltpu.VMEM((2, batch * slots, HD), F32),
            pltpu.VMEM((2, batch * slots, context), BF16),
            pltpu.VMEM((2, batch * slots, HD), F32),
            pltpu.VMEM((2, kv_heads, batch * slots, HD), F32),
            pltpu.SemaphoreType.DMA((2, rows // batch)),
        ],
        compiler_params=pltpu.CompilerParams(vmem_limit_bytes=50 * MIB),
        cost_estimate=pl.CostEstimate(flops=1024, bytes_accessed=1024, transcendentals=0),
        name="attend",
    )(small, kv_cache, after)


def pair_kernel(own_ref, other_ref, out_ref):
    out_ref[0] = own_ref[...]
    out_ref[1] = other_ref[...]


def gate_kernel(ids_ref, gates_ref, gate_ref):
    parts, rows, lanes = gate_ref.shape
    ids = ids_ref[pl.ds(pl.multiple_of(lax.axis_index("gx") * rows, rows), rows), :]
    for s in range(parts):
        gate = jnp.sum(
            jnp.where(ids == (lax.axis_index("gx") ^ s), gates_ref[...], 0.0), axis=1, keepdims=True
        )
        gate_ref[s] = jnp.broadcast_to(gate, (rows, lanes))


def project_kernel(parts, *refs):
    shards, weight_ref = refs[:parts], refs[parts]
    outs, held = refs[parts + 1 : -1], refs[-1]
    rows = shards[0].shape[0]
    turn = lax.axis_index("gx") ^ lax.axis_index("ta")
    block = jnp.concatenate([shard[...] for shard in shards], axis=0)
    pieces = jnp.dot(block, weight_ref[...], preferred_element_type=F32).astype(BF16)
    for s in range(parts):
        held[turn ^ s] = pieces[s * rows : (s + 1) * rows, :]
    for t in range(parts):
        outs[t][...] = held[t]


def add_kernel(*refs):
    terms, out = refs[:-1], refs[-1]
    total = terms[0][...].astype(F32)
    for term in terms[1:]:
        total = total + term[...].astype(F32)
    out[...] = total.astype(BF16)


def norm_kernel(parts, gain_ref, *refs):
    shards, out = refs[:parts], refs[parts]
    width = shards[0].shape[1]
    values = [shard[...].astype(F32) for shard in shards]
    center = sum(jnp.sum(part, axis=1, keepdims=True) for part in values) / out.shape[1]
    values = [part - center for part in values]
    spread = sum(jnp.sum(part * part, axis=1, keepdims=True) for part in values) / out.shape[1]
    scale = lax.rsqrt(spread + 1e-05)
    for s in range(parts):
        here = pl.ds(pl.multiple_of((lax.axis_index("gx") ^ s) * width, HD), width)
        out[:, here] = (values[s] * scale * gain_ref[:, here]).astype(BF16)


def by_distance(pair_ref, second_ref):
    return pair_ref.at[0], second_ref.at[0], pair_ref.at[1], second_ref.at[1]


def load_kernel(rows, source_hbm, out_ref, sem):
    copy = pltpu.make_async_copy(source_hbm.at[pl.ds(0, rows)], out_ref, sem)
    copy.start()
    copy.wait()


def lift_kernel(chunks, *refs):
    count = 2 * chunks
    shards, (up_ref, down_ref, down_hbm) = refs[:count], refs[count : count + 3]
    active_ref, far_ref, close_ref, rest_ref, held, passed, sem = refs[count + 3 :]
    hidden = active_ref.shape[1]
    share = far_ref.shape[2]
    half = far_ref.shape[1]
    rows = shards[0].shape[1]
    cut = down_ref.shape[0]
    copy = pltpu.make_async_copy(down_hbm.at[pl.ds(cut, hidden - cut)], rest_ref, sem)
    copy.start()
    for c in range(chunks):
        for t, shard in enumerate(by_distance(*shards[2 * c : 2 * c + 2])):
            first = pl.multiple_of(((lax.axis_index("ta") ^ t) * chunks + c) * rows, rows)
            held[pl.ds(first, rows), :] = shard[...]
    raised = lax.dot_general(
        up_ref[...], held[...], (((1,), (1,)), ((), ())), preferred_element_type=F32
    )
    active_ref[...] = (raised / (1.0 + jnp.exp(-raised))).T.astype(BF16)
    copy.wait()
    mine = lax.axis_index("gx") // 2
    for k in range(2):
        passed[...] = lowered(2 * k + 1, active_ref, down_ref, rest_ref, share).astype(BF16)
        for out_ref, side in ((far_ref, 1 - mine), (close_ref, mine)):
            out_ref[k] = passed[pl.ds(pl.multiple_of(side * half, half), half), :]


def lowered(turn, active_ref, down_ref, rest_ref, share):
    cut = down_ref.shape[0]
    here = pl.ds(pl.multiple_of((lax.axis_index("ta") ^ turn) * share, HD), share)
    return jnp.dot(
        active_ref[:, :cut], down_ref[:, here], preferred_element_type=F32
    ) + jnp.dot(active_ref[:, cut:], rest_ref[:, here], preferred_element_type=F32)


def lower_kernel(turn, active_ref, down_ref, rest_ref, out_ref):
    out_ref[...] = lowered(turn, active_ref, down_ref, rest_ref, out_ref.shape[1])


def turn_kernel(distances, cross_ref, near_ref, *outs):
    rows = outs[0].shape[0]
    for distance, out_ref in zip(distances, outs):
        z = lax.axis_index("gx") ^ distance
        here = pl.ds(pl.multiple_of(z * rows, rows), rows)
        there = pl.ds(pl.multiple_of(z % 2 * rows, rows), rows)
        out_ref[...] = (cross_ref[here, :] + near_ref[1, there, :].astype(F32)).astype(BF16)


def split_kernel(distances, own_ref, near_ref, *refs):
    count = len(distances)
    rows = refs[0].shape[0]
    for distance, crossed_ref, out_ref in zip(distances, refs[:count], refs[count:]):
        z = lax.axis_index("gx") ^ distance
        here = pl.ds(pl.multiple_of(z * rows, rows), rows)
        there = pl.ds(pl.multiple_of(z % 2 * rows, rows), rows)
        total = own_ref[here, :] + near_ref[0, there, :].astype(F32)
        out_ref[...] = (total + crossed_ref[...].astype(F32)).astype(BF16)


def mix_kernel(distances, gate_ref, *refs):
    out = refs[-1]
    lanes = gate_ref.shape[2]
    for begin in range(0, out.shape[1], lanes):
        part = slice(begin, begin + lanes)
        total = sum(
            gate_ref[s] * term[:, part].astype(F32) for s, term in zip(distances, refs)
        )
        for ref in refs[len(distances) : -1]:
            total = total + ref[:, part]
        out[:, part] = total.astype(out.dtype)


def trade(array, axis, turn):
    count = lax.axis_size(axis)
    return lax.ppermute(array, axis, [(k, k ^ turn) for k in range(count)])


def every_row_body(
    queries, new_kv, kv_cache, lengths, out_proj, norm_gain, expert_ids, gate_weights, w_up, w_down
):
    gx_count = lax.axis_size("gx")
    ta_count = lax.axis_size("ta")
    chunks = 2
    block_rows = queries.shape[0]
    rows = block_rows // chunks
    width = out_proj.shape[1]
    model = norm_gain.shape[0]
    hidden_share = w_up.shape[2]
    share = model // ta_count
    all_rows = block_rows * gx_count
    shape = jax.ShapeDtypeStruct
    gain = norm_gain.reshape(1, model)
    heads = queries.shape[1] // HD
    small = beside(queries, new_kv, lengths, kv_cache.shape[2])
    attended = []
    for c in range(chunks):
        after = attended[-1] if attended else small
        attended.append(attend(small, kv_cache, heads, c * rows, rows, after))
    order = [s for s in range(gx_count - 1, 0, -1)]

    def spread(array, axis):
        parts = {0: array, **{s: trade(array, axis, s) for s in order}}
        return [parts[s] for s in range(len(parts))]

    shards = [spread(part, "gx") for part in attended]
    pieces, hidden = [], []
    for c in range(chunks):
        pieces.append(
            local_call(
                functools.partial(project_kernel, gx_count),
                [shape((rows, width), BF16)] * ta_count,
                [VMEM] * (gx_count + 1),
                [pltpu.VMEM((ta_count, rows, width), BF16)],
                name="project",
                after=pieces[-1][0] if pieces else attended[-1],
                cost=PROJECT_COST,
            )(*shards[c], out_proj)
        )
    for c in range(chunks):
        parts = [pieces[c][0]] + [trade(pieces[c][t], "ta", t) for t in range(1, ta_count)]
        hidden.append(
            local_call(
                add_kernel,
                shape((rows, width), BF16),
                [VMEM] * ta_count,
                name="add",
                after=hidden[-1] if hidden else pieces[-1][0],
            )(*parts)
        )
    shards = [spread(part, "gx") for part in hidden]
    normed, pairs = [], []
    for c in range(chunks):
        normed.append(
            local_call(
                functools.partial(norm_kernel, gx_count),
                shape((rows, model), BF16),
                [VMEM] * (gx_count + 1),
                name="norm",
                after=normed[-1] if normed else hidden[-1],
            )(gain, *shards[c])
        )
    gates = local_call(
        gate_kernel,
        shape((gx_count, block_rows, HD), F32),
        [VMEM, VMEM],
        name="gates",
        after=normed[-1],
    )(expert_ids, gate_weights)
    up = local_call(
        functools.partial(load_kernel, hidden_share),
        shape((hidden_share, model), BF16),
        [ANYWHERE],
        [pltpu.SemaphoreType.DMA],
        vmem=40,
        name="load_up",
        after=gates,
    )(jnp.swapaxes(w_up[0], 0, 1))
    for c in range(chunks):
        pairs.append(
            local_call(
                pair_kernel,
                shape((2, rows, model), BF16),
                [VMEM] * 2,
                name="pair",
                after=pairs[-1] if pairs else up,
            )(normed[c], trade(normed[c], "ta", 2))
        )
    blocks = [block for pair in pairs for block in (pair, trade(pair, "ta", 1))]
    cut = hidden_share // (4 * HD) * 2 * HD
    part = local_call(
        functools.partial(load_kernel, cut),
        shape((cut, model), BF16),
        [ANYWHERE],
        [pltpu.SemaphoreType.DMA],
        vmem=46,
        name="load_down",
        after=pairs[-1],
    )(w_down[0])
    half = all_rows // 2
    active, far, close, rest = local_call(
        functools.partial(lift_kernel, chunks),
        [
            shape((all_rows, hidden_share), BF16),
            shape((2, half, share), BF16),
            shape((2, half, share), BF16),
            shape((hidden_share - cut, model), BF16),
        ],
        [VMEM] * (2 * chunks + 2) + [ANYWHERE],
        [
            pltpu.VMEM((all_rows, model), BF16),
            pltpu.VMEM((all_rows, share), BF16),
            pltpu.SemaphoreType.DMA,
        ],
        vmem=30,
        name="lift",
    )(*blocks, up, part, w_down[0])
    near = {1: trade(far, "ta", 1), 0: trade(close, "ta", 1)}

    def lower(turn, after):
        return local_call(
            functools.partial(lower_kernel, turn),
            shape((all_rows, share), F32),
            [VMEM] * 3,
            name="lower",
            after=after,
        )(active, part, rest)

    def on_rows(kernel, distances, after, *arrays):
        return local_call(
            functools.partial(kernel, distances),
            [shape((block_rows, share), BF16)] * len(distances),
            [VMEM] * len(arrays),
            name=kernel.__name__[:-7],
            after=after,
        )(*arrays)

    cross = lower(2, None)
    groups = ((3,), (2,), (1, 0))
    turned = [cross]
    crossed = {}
    for distances in groups:
        sums = on_rows(turn_kernel, distances, turned[0], cross, near[distances[0] // 2])
        turned = sums
        crossed.update({s: trade(part, "ta", 2) for s, part in zip(distances, sums)})
    own = lower(0, turned[0])
    gathered, total, after = {}, [], None
    for distances in groups:
        terms = on_rows(
            split_kernel, distances, after, own, near[distances[0] // 2],
            *[crossed[s] for s in distances],
        )
        after = terms[0]
        for s, term in zip(distances, terms):
            gathered[s] = trade(term, "gx", s) if s else term
    for distances in groups:
        last = 0 in distances
        total = [
            local_call(
                functools.partial(mix_kernel, distances),
                shape((block_rows, share), BF16 if last else F32),
                [VMEM] * (1 + len(distances) + len(total)),
                name="mix",
                cost=1024 if last else MIX_COST,
            )(gates, *[gathered[s] for s in distances], *total)
        ]
    return total[0]


def route_tables(expert_ids, expert_count, block_rows, capacity):
    blocks = expert_ids.shape[0] // block_rows
    expert_range = jnp.arange(expert_count, dtype=jnp.int32)
    matches = (expert_ids[:, :, None] == expert_range[None, None, :]).astype(jnp.int32)
    routed = jnp.sum(matches, axis=1).reshape(blocks, block_rows, expert_count)
    position = jnp.cumsum(routed, axis=1) - routed
    slot_range = jnp.arange(capacity, dtype=jnp.int32)
    slot_hits = routed[:, :, :, None] * (
        position[:, :, :, None] == slot_range[None, None, None, :]
    ).astype(jnp.int32)
    row_range = jnp.arange(block_rows, dtype=jnp.int32)
    block_start = (jnp.arange(blocks, dtype=jnp.int32) * block_rows)[:, None, None]
    source_row = jnp.sum(slot_hits * row_range[None, :, None, None], axis=1) + block_start
    filled = jnp.sum(slot_hits, axis=1)
    source_row = jnp.transpose(source_row, (1, 0, 2)).reshape(expert_count, blocks * capacity)
    filled = jnp.transpose(filled, (1, 0, 2)).reshape(expert_count, blocks * capacity)
    pick_slot = jnp.sum(matches * position.reshape(blocks * block_rows, 1, expert_count), axis=2)
    return (source_row, filled, pick_slot)


def layer_norm(hidden, norm_gain):
    values = hidden.astype(jnp.float32)
    center = values - jnp.mean(values, axis=1, keepdims=True)
    spread = jnp.mean(center * center, axis=1, keepdims=True)
    return (center * lax.rsqrt(spread + 1e-05) * norm_gain).astype(jnp.bfloat16)


def body(
    queries, new_kv, kv_cache, lengths, out_proj, norm_gain, expert_ids, gate_weights, w_up, w_down
):
    gx_count = lax.axis_size("gx")
    ta_count = lax.axis_size("ta")
    block_rows = queries.shape[0]
    top_count = expert_ids.shape[1]
    capacity = min(block_rows, 2 * block_rows * top_count // gx_count)
    slot_count = gx_count * capacity
    model_width = norm_gain.shape[0]
    width_share = model_width // ta_count
    if gx_count == top_count and ta_count == gx_count == 4:
        return every_row_body(
            queries, new_kv, kv_cache, lengths, out_proj, norm_gain, expert_ids, gate_weights,
            w_up, w_down,
        )
    small = beside(queries, new_kv, lengths, kv_cache.shape[2])
    attended = attend(small, kv_cache, queries.shape[1] // HD, 0, block_rows, small)
    projected = jnp.dot(
        lax.all_gather(attended, "gx", axis=0, tiled=True),
        out_proj,
        preferred_element_type=jnp.float32,
    ).astype(jnp.bfloat16)
    source_row, filled, pick_slot = route_tables(expert_ids, gx_count, block_rows, capacity)
    live_slots = (filled > 0)[:, :, None]
    widened = lax.optimization_barrier(projected).astype(jnp.float32)
    hidden_share = lax.psum_scatter(
        widened.astype(jnp.bfloat16), "ta", scatter_dimension=1, tiled=True
    )
    outgoing = jnp.where(live_slots, hidden_share[source_row], jnp.zeros((), jnp.bfloat16))[
        :, :, None, :
    ]
    arrived = lax.all_to_all(outgoing, "gx", split_axis=0, concat_axis=2, tiled=True)
    gathered = lax.all_gather(arrived, "ta", axis=3, tiled=True)
    hidden = gathered.reshape(slot_count, model_width)
    normed = layer_norm(hidden, norm_gain)
    raised = jnp.dot(normed, w_up[0], preferred_element_type=jnp.float32)
    active = jax.nn.silu(raised).astype(jnp.bfloat16)
    terms = jnp.dot(active, w_down[0], preferred_element_type=jnp.float32)
    mine = lax.psum_scatter(terms, "ta", scatter_dimension=1, tiled=True)
    result = mine.astype(jnp.bfloat16).reshape(gx_count, capacity, width_share)
    returned = lax.all_to_all(result, "gx", split_axis=0, concat_axis=0, tiled=True)
    first_row = lax.axis_index("gx") * block_rows
    local_ids = lax.dynamic_slice_in_dim(expert_ids, first_row, block_rows, 0)
    local_slot = lax.dynamic_slice_in_dim(pick_slot, first_row, block_rows, 0)
    flat_rows = returned.reshape(gx_count * capacity, width_share)
    picked = flat_rows[local_ids * capacity + local_slot]
    return jnp.sum(picked.astype(jnp.float32) * gate_weights[:, :, None], axis=1).astype(
        jnp.bfloat16
    )


def solution(mesh):
    return jax.shard_map(
        body,
        mesh=mesh,
        in_specs=(
            P(("groups", "gx"), "ta"),
            P(None, ("groups", "gx"), "ta"),
            P(None, ("groups", "gx"), None, "ta"),
            P(("groups", "gx")),
            P("ta", "gx"),
            P(),
            P("groups", None),
            P(("groups", "gx"), None),
            P("gx", None, "ta"),
            P("gx", "ta", None),
        ),
        out_specs=P(("groups", "gx"), "ta"),
        check_vma=False,
    )
```
